32 devices in a mesh: seq: 8 (over z, x), tp: 4 (over y, core).
Axes of the slice: x: 2, y: 2, z: 4, core: 2. Of those that a mesh axis runs over, the one named last changes fastest.
Arguments:
- queries: bfloat16 [2048, 4096], P('seq', 'tp'), may hold values from -6 to 6
- vocab_rows: bfloat16 [16384, 1024], P('seq', 'tp'), may hold values from -36 to 36
- neighbour_ids: int32 [32, 2, 128], P('seq'), may hold values from 0 to 16383, as said below
- w_in: bfloat16 [1024, 4096], P(None, 'tp'), may hold values from -0.1875 to 0.1875
- w_out: bfloat16 [4096, 1024], P('tp'), may hold values from -0.09375 to 0.09375
- w_key: bfloat16 [1024, 4096], P(None, 'tp'), may hold values from -0.1875 to 0.1875
- w_value: bfloat16 [1024, 4096], P(None, 'tp'), may hold values from -0.1875 to 0.1875
Outputs:
- cross_out: bfloat16 [2048, 4096], P('seq', 'tp')
The draws below stay inside these ranges and needn't reach their ends.
Inputs may be any that keep to these rules, and one draw needn't show every extreme that they name: `neighbour_ids`: the owner of id i is i // 2048. Among the neighbour ids of the groups of one index of seq, at most 256 have one owner; some owner has exactly 256 among those of every index.
All inputs are finite; a program needn't handle non-finite values.
Results may differ from the reference program's by a relative error of at most 0.0095.
Values may be sent and summed in bfloat16 or wider, within the bound.
No kernel may reach another device: no remote copies, remote signals or barrier semaphores. Data moves between devices by JAX's collectives and lax.ppermute only.
A program may use at most 64 MiB of HBM per device.

```python
import math
import jax
import jax.numpy as jnp
from jax import lax

D_ENC = 1024
ENC_FF = 4096
HEADS = 32
HEAD_WIDTH = 128
VOC_DEV = 2048
GROUP = 64
NBRS = 2
NLEN = 128
TOK_DEV = 256
TOKENS = 2048
SEQLEN = 2048
VOCAB = 16384
CAP = 256


def draw_vocab_rows(key, part):
    first, second, third = jax.random.split(key, 3)
    col_scale = jnp.exp(jax.random.uniform(third, (1, D_ENC), jnp.float32, math.log(0.3), math.log(3.0)))
    base = jnp.clip(jax.random.normal(first, (VOCAB, D_ENC), jnp.float32), -4.0, 4.0)
    row_scale = jnp.exp(jax.random.uniform(second, (VOCAB, 1), jnp.float32, math.log(0.3), math.log(3.0)))
    return (base * row_scale * col_scale).astype(jnp.bfloat16)


def draw_neighbour_ids(key, part):
    owners = VOCAB // VOC_DEV
    rows = TOK_DEV // GROUP * NBRS * NLEN
    spread = max(rows - CAP, 1)
    hot_key, block_key = jax.random.split(key)
    hot = jax.random.randint(hot_key, (), 0, owners)

    def one_block(bkey):
        first, second, third = jax.random.split(bkey, 3)
        others = (hot + 1 + jax.random.permutation(first, owners - 1)) % owners
        slots = jnp.arange(rows, dtype=jnp.int32)
        pick = jnp.clip((slots - CAP) * (owners - 1) // spread, 0, owners - 2)
        owner = jnp.where(slots < CAP, hot, others[pick])
        owner = jax.random.permutation(second, owner)
        return owner * VOC_DEV + jax.random.randint(third, (rows,), 0, VOC_DEV)
    ids = jax.vmap(one_block)(jax.random.split(block_key, owners))
    return ids.reshape(TOKENS // GROUP, NBRS, NLEN).astype(jnp.int32)


def level_of(key, extent, cuts, low, high):
    loudness, own = 1.0, jax.random.fold_in(key, 6)
    for axis_at, blocks in cuts:
        draws = jnp.exp(jax.random.uniform(jax.random.fold_in(own, axis_at), (blocks,), jnp.float32, low / len(cuts), high / len(cuts)))
        loudness = loudness * jnp.repeat(draws, extent[axis_at] // blocks).reshape([-1 if axis == axis_at else 1 for axis in range(len(extent))])
    return loudness


def scatter_about(stream_key, shape, deviation, most, cuts=(), kind=jnp.bfloat16):
    values = jax.random.normal(stream_key, shape, jnp.float32) * deviation
    if len(cuts) > 0:
        values = level_of(stream_key, shape, cuts, -0.22, 0.18) * values
    return jnp.clip(values, min=-most, max=most).astype(kind)


def setup_inputs(seed: int = 0) -> dict:
    key_of = jax.random.split(jax.random.key(seed), 8)
    queries = scatter_about(key_of[0], (TOKENS, HEADS * HEAD_WIDTH), 1.0, 6.0, ((0, 8), (1, 4)))
    vocab_rows = draw_vocab_rows(jax.random.fold_in(key_of[7], 71), 0)
    neighbour_ids = draw_neighbour_ids(jax.random.fold_in(key_of[7], 71), 0)
    w_in = scatter_about(key_of[3], (D_ENC, ENC_FF), D_ENC ** -0.5, 0.1875, ((1, 4),))
    w_out = scatter_about(key_of[4], (ENC_FF, D_ENC), ENC_FF ** -0.5, 0.09375, ((0, 4),))
    w_key = scatter_about(key_of[5], (D_ENC, HEADS * HEAD_WIDTH), D_ENC ** -0.5, 0.1875, ((1, 4),))
    w_value = scatter_about(key_of[6], (D_ENC, HEADS * HEAD_WIDTH), D_ENC ** -0.5, 0.1875, ((1, 4),))
    return dict(queries=queries, vocab_rows=vocab_rows, neighbour_ids=neighbour_ids, w_in=w_in, w_out=w_out, w_key=w_key, w_value=w_value)


def encode(emb, w_in, w_out):
    values = emb.astype(jnp.float32)
    normed = (values * lax.rsqrt(lax.optimization_barrier(jnp.mean(values * values, axis=-1, keepdims=True)) + 1e-06)).astype(emb.dtype)
    inner = jax.nn.gelu(jnp.dot(normed, w_in, preferred_element_type=jnp.float32), approximate=True).astype(emb.dtype)
    return (values + jnp.dot(inner, w_out, preferred_element_type=jnp.float32)).astype(emb.dtype)

def attend(q_rows, keys, values):
    count = q_rows.shape[0]
    width = q_rows.shape[1]
    heads = width // HEAD_WIDTH
    kcount = keys.shape[0]
    decoder_query = q_rows.astype(jnp.float32).reshape(count, heads, HEAD_WIDTH)
    neighbour_key_heads = keys.astype(jnp.float32).reshape(kcount, heads, HEAD_WIDTH)
    neighbour_value_heads = values.astype(jnp.float32).reshape(kcount, heads, HEAD_WIDTH)
    attention_logits = jnp.einsum('xjy,bjy->jxb', decoder_query, neighbour_key_heads) * HEAD_WIDTH ** (-0.5)
    expo = jnp.exp(attention_logits)
    attention_probs = (expo / lax.optimization_barrier(jnp.sum(expo, axis=-1, keepdims=True))).astype(q_rows.dtype)
    attended_values = jnp.einsum('lwo,olu->wlu', attention_probs.astype(jnp.float32), neighbour_value_heads)
    return attended_values.reshape(count, width).astype(q_rows.dtype)

def reference(queries, vocab_rows, neighbour_ids, w_in, w_out, w_key, w_value):
    groups = neighbour_ids.shape[0]
    width = queries.shape[1]
    padded = jnp.concatenate([queries, jnp.zeros((GROUP, width), queries.dtype)], axis=0)

    def per_group(item):
        group_ids, index = item
        emb = jnp.take(vocab_rows, group_ids.reshape(-1), axis=0)
        encoded = encode(emb, w_in, w_out)
        keys = jnp.dot(encoded, w_key, preferred_element_type=jnp.float32).astype(queries.dtype)
        values = jnp.dot(encoded, w_value, preferred_element_type=jnp.float32).astype(queries.dtype)
        start = (index * GROUP + GROUP - 1).astype(jnp.int32)
        q_rows = lax.dynamic_slice_in_dim(padded, start, GROUP, 0)
        return attend(q_rows, keys, values)
    windows = lax.map(per_group, (neighbour_ids, jnp.arange(groups, dtype=jnp.int32)))
    flat = windows.reshape(groups * GROUP, width)
    shifted = jnp.concatenate([jnp.zeros((GROUP - 1, width), flat.dtype), flat[:groups * GROUP - GROUP + 1]], axis=0)
    position = jnp.arange(groups * GROUP, dtype=jnp.int32) % SEQLEN
    return jnp.where((position >= GROUP - 1)[:, None], shifted, jnp.zeros_like(shifted))
```

```python
import functools

import jax
import jax.numpy as jnp
from jax import lax
from jax.experimental import pallas as pl
from jax.experimental.pallas import tpu as pltpu
from jax.sharding import PartitionSpec as P

HEAD_WIDTH = 128
GROUP = 64
LANES = 128
VMEM_LIMIT = 24 * 1024 * 1024
F32 = jnp.float32
BF16 = jnp.bfloat16


def call(body, outs, flops, nbytes, name, unused=None):
    specs = {}
    if unused is not None:
        vmem = pl.BlockSpec(memory_space=pltpu.VMEM)
        specs = dict(in_specs=[vmem] * (unused - 1) + [pl.BlockSpec(memory_space=pl.ANY)])
    return pl.pallas_call(
        body,
        out_shape=outs,
        **specs,
        compiler_params=pltpu.CompilerParams(vmem_limit_bytes=VMEM_LIMIT),
        cost_estimate=pl.CostEstimate(flops=flops, bytes_accessed=nbytes, transcendentals=0),
        name=name,
    )


def exchange(x, bit):
    size = lax.axis_size("tp")
    return lax.ppermute(x, "tp", [(i, i ^ bit) for i in range(size)])


def shifted(x, by):
    length = lax.axis_size("seq")
    pairs = [(i, i + by) for i in range(length) if 0 <= i + by < length]
    return lax.ppermute(x, "seq", pairs)


def columns_of(row):
    return jnp.broadcast_to(row, (LANES, row.shape[1])).T


def one_hot(column, width):
    lane = lax.broadcasted_iota(jnp.int32, column.shape, 1)
    return jnp.concatenate(
        [jnp.where(column == lane + at, 1.0, 0.0).astype(BF16) for at in range(0, width, LANES)],
        axis=1,
    )


def route_body(voc, cap, ids_ref, wanted_ref, slot_ref):
    ids = ids_ref[...]
    count = ids.shape[1]
    owners = wanted_ref.shape[0]
    owner = lax.div(ids, jnp.int32(voc))
    local = ids - owner * voc
    hit = owner == lax.broadcasted_iota(jnp.int32, (owners, count), 0)
    hot = jnp.where(hit, 1.0, 0.0)
    upper = jnp.where(
        lax.broadcasted_iota(jnp.int32, (LANES, LANES), 0)
        <= lax.broadcasted_iota(jnp.int32, (LANES, LANES), 1),
        1.0,
        0.0,
    ).astype(BF16)
    carry = jnp.zeros((owners, 1), F32)
    ranks = []
    for at in range(0, count, LANES):
        part = hot[:, at : at + LANES]
        running = jnp.dot(part.astype(BF16), upper, preferred_element_type=F32) + carry
        ranks.append(jnp.sum(part * running, axis=0, keepdims=True))
        carry = running[:, LANES - 1 :]
    rank = jnp.concatenate(ranks, axis=1).astype(jnp.int32) - 1
    high = jnp.where(hit, lax.div(local, jnp.int32(256)), 0)
    low = jnp.where(hit, lax.rem(local, jnp.int32(256)), 0)
    digits = jnp.concatenate([high, low], axis=0).astype(F32).astype(BF16)
    place = jnp.where(
        rank == lax.broadcasted_iota(jnp.int32, (cap, count), 0), 1.0, 0.0
    ).astype(BF16)
    found = lax.dot_general(
        digits, place, (((1,), (1,)), ((), ())), preferred_element_type=F32
    ).astype(jnp.int32)
    wanted_ref[...] = found[:owners] * 256 + found[owners:]
    slot_ref[...] = columns_of(owner * cap + rank)


def fetch_body(req_ref, vocab_ref, out_ref):
    step = 256
    table = vocab_ref[...]
    for at in range(0, req_ref.shape[1], step):
        picked = one_hot(columns_of(req_ref[:, at : at + step]), table.shape[0])
        out_ref[at : at + step, :] = jnp.dot(
            picked, table, preferred_element_type=F32
        ).astype(BF16)


def order_body(slot_ref, rows_ref, *out_refs):
    rows = rows_ref[...]
    for at, out_ref in enumerate(out_refs):
        count = out_ref.shape[0]
        picked = one_hot(slot_ref[at * count : (at + 1) * count, :], rows.shape[0])
        out_ref[...] = jnp.dot(picked, rows, preferred_element_type=F32).astype(BF16)


def block_rows(ref, index, width):
    return ref[pl.ds(pl.multiple_of(index * width, width), width), :]


def block_cols(ref, index, width):
    return ref[:, pl.ds(pl.multiple_of(index * width, width), width)]


def feed_body(e0_ref, e2_ref, e1_ref, e3_ref, w_in_ref, w_out_ref, _, keep_ref, send_ref):
    me = lax.axis_index("tp")
    width = e0_ref.shape[1]
    index = [me, me ^ 2, me ^ 1, me ^ 3]
    parts = [ref[...].astype(F32) for ref in (e0_ref, e2_ref, e1_ref, e3_ref)]
    square = sum(jnp.sum(part * part, axis=1, keepdims=True) for part in parts)
    scale = lax.rsqrt(square / (4 * width) + 1e-06)
    hidden = sum(
        jnp.dot(
            (part * scale).astype(BF16), block_rows(w_in_ref, at, width), preferred_element_type=F32
        )
        for part, at in zip(parts, index)
    )
    inner = jax.nn.gelu(hidden, approximate=True).astype(BF16)
    for slot in range(2):
        cols = slice(slot * width, (slot + 1) * width)
        keep_ref[:, cols] = jnp.dot(
            inner, block_cols(w_out_ref, index[slot], width), preferred_element_type=F32
        )
        send_ref[:, cols] = jnp.dot(
            inner, block_cols(w_out_ref, index[2 + slot], width), preferred_element_type=F32
        ).astype(BF16)


def add_body(keep_ref, recv_ref, _, chip_ref, send_ref):
    chip = keep_ref[...] + recv_ref[...].astype(F32)
    chip_ref[...] = chip
    send_ref[...] = chip.astype(BF16)


def finish_body(e0_ref, e2_ref, chip_ref, far_ref, _, mine_ref):
    width = e0_ref.shape[1]
    near, past = slice(0, width), slice(width, 2 * width)
    mine_ref[:, near] = (
        e0_ref[...].astype(F32) + (chip_ref[:, near] + far_ref[:, past].astype(F32))
    ).astype(BF16)
    mine_ref[:, past] = (
        e2_ref[...].astype(F32) + (chip_ref[:, past] + far_ref[:, near].astype(F32))
    ).astype(BF16)


def attended(mine_ref, other_ref, w_key_ref, w_value_ref, q_ref):
    me = lax.axis_index("tp")
    width = mine_ref.shape[1] // 2
    parts = [
        (mine_ref[:, :width], me),
        (mine_ref[:, width:], me ^ 2),
        (other_ref[:, :width], me ^ 1),
        (other_ref[:, width:], me ^ 3),
    ]

    def project(w_ref):
        return sum(
            jnp.dot(part, block_rows(w_ref, at, width), preferred_element_type=F32)
            for part, at in parts
        ).astype(BF16)

    heads = [slice(at, at + HEAD_WIDTH) for at in range(0, q_ref.shape[1], HEAD_WIDTH)]
    keys = project(w_key_ref)
    weights = []
    for cols in heads:
        logits = lax.dot_general(
            q_ref[:, cols], keys[:, cols], (((1,), (1,)), ((), ())), preferred_element_type=F32
        ) * HEAD_WIDTH ** (-0.5)
        expo = jnp.exp(logits)
        weights.append((expo * (1.0 / jnp.sum(expo, axis=1, keepdims=True))).astype(BF16))
    values = project(w_value_ref)
    return [
        jnp.dot(weight, values[:, cols], preferred_element_type=F32)
        for weight, cols in zip(weights, heads)
    ]


def attend_body(mine_ref, other_ref, w_key_ref, w_value_ref, q_ref, _, out_ref):
    for at, part in enumerate(attended(mine_ref, other_ref, w_key_ref, w_value_ref, q_ref)):
        out_ref[:, at * HEAD_WIDTH : (at + 1) * HEAD_WIDTH] = part.astype(BF16)


def attend_last_body(
    mine_ref, other_ref, w_key_ref, w_value_ref, q_ref, behind_ref, *refs
):
    before, last_ref, out_ref = refs[:-2], refs[-2], refs[-1]
    parts = attended(mine_ref, other_ref, w_key_ref, w_value_ref, q_ref)
    for at, part in enumerate(parts):
        cols = slice(at * HEAD_WIDTH, (at + 1) * HEAD_WIDTH)
        part = part.astype(BF16).astype(F32)
        stack = [behind_ref[:, cols].astype(F32)]
        stack += [ref[:, cols].astype(F32) for ref in before]
        stack += [part, last_ref[:, cols].astype(F32)]
        tall = jnp.concatenate(stack, axis=0)
        moved = pltpu.roll(tall, tall.shape[0] - 1, 0)
        out_ref[:, cols] = moved[: out_ref.shape[0]].astype(BF16)


def per_device(queries, vocab_rows, neighbour_ids, w_in, w_out, w_key, w_value):
    seq_size = lax.axis_size("seq")
    groups, nbrs, nlen = neighbour_ids.shape
    per_group = nbrs * nlen
    rows = groups * per_group
    voc, width = vocab_rows.shape
    tok, head_cols = queries.shape
    cap = max(2, 2 * rows // seq_size)
    slots = seq_size * cap
    sds = jax.ShapeDtypeStruct

    next_q = shifted(queries[:GROUP], -1)

    wanted, slot = call(
        functools.partial(route_body, voc, cap),
        (sds((seq_size, cap), jnp.int32), sds((rows, LANES), jnp.int32)),
        2 * rows * cap * 16,
        rows * 600,
        "route",
    )(neighbour_ids.reshape(1, rows))
    request = lax.all_to_all(wanted, "seq", split_axis=0, concat_axis=0, tiled=True)
    found = call(
        fetch_body, sds((slots, width), BF16), 2 * slots * voc * width, 3 * slots * width * 2, "fetch"
    )(request.reshape(1, slots), vocab_rows)
    answered = lax.all_to_all(
        found.reshape(seq_size, cap, width), "seq", split_axis=0, concat_axis=0, tiled=True
    ).reshape(slots, width)
    own = call(
        order_body,
        tuple(sds((per_group, width), BF16) for _ in range(groups)),
        2 * slots * rows * width,
        3 * slots * width * 2,
        "order",
    )(slot, answered)

    local_q = jnp.concatenate([queries[GROUP - 1 :], next_q[: GROUP - 1]], axis=0)
    order = [groups - 1] + list(range(groups - 1))
    half = sds((per_group, 2 * width), BF16)
    whole = sds((per_group, 2 * width), F32)
    window = {}
    emb, fed, summed, far = {}, {}, {}, {}
    behind = None
    token = slot

    def embed(g):
        e0 = own[g]
        e2 = exchange(e0, 2)
        emb[g] = (e0, e2, exchange(e0, 1), exchange(e2, 1))

    def feed(g):
        nonlocal token
        keep, send = call(
            feed_body,
            (whole, half),
            16 * per_group * width * w_in.shape[1],
            4 * w_in.shape[0] * w_in.shape[1],
            "feed",
            unused=7,
        )(*emb[g], w_in, w_out, token)
        fed[g] = keep, exchange(send, 1)
        token = send

    def add(g):
        nonlocal token
        chip, send = call(
            add_body, (whole, half), per_group * width, per_group * width * 16, "add", unused=3
        )(*fed[g], token)
        summed[g] = chip
        far[g] = exchange(send, 2)
        token = send

    def finish(g):
        nonlocal token, behind
        mine = call(
            finish_body, half, per_group * width, per_group * width * 16, "finish", unused=5
        )(*emb[g][:2], summed[g], far[g], token)
        other = exchange(mine, 1)
        token = mine
        args = (mine, other, w_key, w_value, local_q[g * GROUP : (g + 1) * GROUP])
        cost = 16 * per_group * width * head_cols, 4 * w_key.shape[0] * w_key.shape[1]
        if g == order[-1]:
            before = [window[at] for at in range(groups - 2)]
            return call(attend_last_body, sds((tok, head_cols), BF16), *cost, "attend_last")(
                *args, behind, *before, window[groups - 1]
            )
        window[g] = call(
            attend_body, sds((GROUP, head_cols), BF16), *cost, "attend", unused=6
        )(*args, token)
        token = window[g]
        if g == groups - 1:
            behind = shifted(window[g], 1)

    for at, g in enumerate(order):
        embed(g)
    for at, g in enumerate(order):
        feed(g)
        if at >= 1:
            add(order[at - 1])
    add(order[-1])
    out = None
    for g in order:
        out = finish(g)
    return out


def solution(mesh):
    return jax.shard_map(
        per_device,
        mesh=mesh,
        in_specs=(
            P("seq", "tp"),
            P("seq", "tp"),
            P("seq", None, None),
            P(None, "tp"),
            P("tp", None),
            P(None, "tp"),
            P(None, "tp"),
        ),
        out_specs=P("seq", "tp"),
        check_vma=False,
    )
```

```python
import functools

import jax
import jax.numpy as jnp
from jax import lax
from jax.experimental import pallas as pl
from jax.experimental.pallas import tpu as pltpu
from jax.sharding import PartitionSpec as P

HEAD_WIDTH = 128
GROUP = 64
LANES = 128
VMEM_LIMIT = 24 * 1024 * 1024
F32 = jnp.float32
BF16 = jnp.bfloat16


def call(body, outs, name, used=None, after=()):
    vmem = pl.BlockSpec(memory_space=pltpu.VMEM)
    unread = pl.BlockSpec(memory_space=pl.ANY)

    def without_after(*refs):
        body(*refs[: len(used)], *refs[len(used) + len(after) :])

    return pl.pallas_call(
        without_after,
        out_shape=outs,
        in_specs=[vmem] * len(used) + [unread] * len(after),
        compiler_params=pltpu.CompilerParams(vmem_limit_bytes=VMEM_LIMIT),
        cost_estimate=pl.CostEstimate(flops=1024, bytes_accessed=1024, transcendentals=0),
        name=name,
    )(*used, *after)


def exchange(x, bit):
    size = lax.axis_size("tp")
    return lax.ppermute(x, "tp", [(i, i ^ bit) for i in range(size)])


def shifted(x, by):
    length = lax.axis_size("seq")
    pairs = [(i, i + by) for i in range(length) if 0 <= i + by < length]
    return lax.ppermute(x, "seq", pairs)


def columns_of(row):
    return jnp.broadcast_to(row, (LANES, row.shape[1])).T


def one_hot(column, width):
    lane = lax.broadcasted_iota(jnp.int32, column.shape, 1)
    return jnp.concatenate(
        [jnp.where(column == lane + at, 1.0, 0.0).astype(BF16) for at in range(0, width, LANES)],
        axis=1,
    )


def route_body(voc, cap, ids_ref, wanted_ref, slot_ref):
    ids = ids_ref[...]
    count = ids.shape[1]
    owners = wanted_ref.shape[0]
    owner = lax.div(ids, jnp.int32(voc))
    local = ids - owner * voc
    hit = owner == lax.broadcasted_iota(jnp.int32, (owners, count), 0)
    hot = jnp.where(hit, 1.0, 0.0)
    upper = jnp.where(
        lax.broadcasted_iota(jnp.int32, (LANES, LANES), 0)
        <= lax.broadcasted_iota(jnp.int32, (LANES, LANES), 1),
        1.0,
        0.0,
    ).astype(BF16)
    carry = jnp.zeros((owners, 1), F32)
    ranks = []
    for at in range(0, count, LANES):
        part = hot[:, at : at + LANES]
        running = jnp.dot(part.astype(BF16), upper, preferred_element_type=F32) + carry
        ranks.append(jnp.sum(part * running, axis=0, keepdims=True))
        carry = running[:, LANES - 1 :]
    rank = jnp.concatenate(ranks, axis=1).astype(jnp.int32) - 1
    high = jnp.where(hit, lax.div(local, jnp.int32(256)), 0)
    low = jnp.where(hit, lax.rem(local, jnp.int32(256)), 0)
    digits = jnp.concatenate([high, low], axis=0).astype(F32).astype(BF16)
    place = jnp.where(
        rank == lax.broadcasted_iota(jnp.int32, (cap, count), 0), 1.0, 0.0
    ).astype(BF16)
    found = lax.dot_general(
        digits, place, (((1,), (1,)), ((), ())), preferred_element_type=F32
    ).astype(jnp.int32)
    wanted_ref[...] = found[:owners] * 256 + found[owners:]
    slot_ref[...] = columns_of(owner * cap + rank)


def fetch_body(req_ref, vocab_ref, out_ref):
    step = 256
    table = vocab_ref[...]
    for at in range(0, req_ref.shape[1], step):
        picked = one_hot(columns_of(req_ref[:, at : at + step]), table.shape[0])
        out_ref[at : at + step, :] = jnp.dot(
            picked, table, preferred_element_type=F32
        ).astype(BF16)


def order_body(plan, slot_ref, rows_ref, *out_refs):
    rows = rows_ref[...]
    for groups, out_ref in zip(plan, out_refs):
        count = out_ref.shape[0] // len(groups)
        for at, g in enumerate(groups):
            picked = one_hot(slot_ref[g * count : (g + 1) * count, :], rows.shape[0])
            out_ref[at * count : (at + 1) * count, :] = jnp.dot(
                picked, rows, preferred_element_type=F32
            ).astype(BF16)


def block_rows(ref, index, width):
    return ref[pl.ds(pl.multiple_of(index * width, width), width), :]


def block_cols(ref, index, width):
    return ref[:, pl.ds(pl.multiple_of(index * width, width), width)]


def feed_body(first, e0_ref, e2_ref, e1_ref, e3_ref, w_in_ref, w_out_ref, keep_ref, send_ref):
    me = lax.axis_index("tp")
    width = e0_ref.shape[1]
    index = [me, me ^ 2, me ^ 1, me ^ 3]
    here = slice(first, first + keep_ref.shape[0])
    parts = [ref[here, :].astype(F32) for ref in (e0_ref, e2_ref, e1_ref, e3_ref)]
    square = sum(jnp.sum(part * part, axis=1, keepdims=True) for part in parts)
    scale = lax.rsqrt(square / (4 * width) + 1e-06)
    hidden = sum(
        jnp.dot(
            (part * scale).astype(BF16), block_rows(w_in_ref, at, width), preferred_element_type=F32
        )
        for part, at in zip(parts, index)
    )
    inner = jax.nn.gelu(hidden, approximate=True).astype(BF16)
    for slot in range(2):
        cols = slice(slot * width, (slot + 1) * width)
        keep_ref[:, cols] = jnp.dot(
            inner, block_cols(w_out_ref, index[slot], width), preferred_element_type=F32
        )
        send_ref[:, cols] = jnp.dot(
            inner, block_cols(w_out_ref, index[2 + slot], width), preferred_element_type=F32
        ).astype(BF16)


def add_body(keep_ref, recv_ref, chip_ref, send_ref):
    chip = keep_ref[...] + recv_ref[...].astype(F32)
    chip_ref[...] = chip
    send_ref[...] = chip.astype(BF16)


def finish_body(first, e0_ref, e2_ref, chip_ref, far_ref, mine_ref):
    width = e0_ref.shape[1]
    near, past = slice(0, width), slice(width, 2 * width)
    here = slice(first, first + mine_ref.shape[0])
    mine_ref[:, near] = (
        e0_ref[here, :].astype(F32) + (chip_ref[:, near] + far_ref[:, past].astype(F32))
    ).astype(BF16)
    mine_ref[:, past] = (
        e2_ref[here, :].astype(F32) + (chip_ref[:, past] + far_ref[:, near].astype(F32))
    ).astype(BF16)


def attended(mine_ref, other_ref, w_key_ref, w_value_ref, q_ref):
    me = lax.axis_index("tp")
    width = mine_ref.shape[1] // 2
    parts = [
        (mine_ref[:, :width], me),
        (mine_ref[:, width:], me ^ 2),
        (other_ref[:, :width], me ^ 1),
        (other_ref[:, width:], me ^ 3),
    ]

    def project(w_ref):
        return sum(
            jnp.dot(part, block_rows(w_ref, at, width), preferred_element_type=F32)
            for part, at in parts
        ).astype(BF16)

    heads = [slice(at, at + HEAD_WIDTH) for at in range(0, q_ref.shape[1], HEAD_WIDTH)]
    keys = project(w_key_ref)
    weights = []
    for cols in heads:
        logits = lax.dot_general(
            q_ref[:, cols], keys[:, cols], (((1,), (1,)), ((), ())), preferred_element_type=F32
        ) * HEAD_WIDTH ** (-0.5)
        expo = jnp.exp(logits)
        weights.append((expo * (1.0 / jnp.sum(expo, axis=1, keepdims=True))).astype(BF16))
    values = project(w_value_ref)
    return [
        jnp.dot(weight, values[:, cols], preferred_element_type=F32)
        for weight, cols in zip(weights, heads)
    ]


def attend_body(mine_ref, other_ref, w_key_ref, w_value_ref, q_ref, out_ref):
    for at, part in enumerate(attended(mine_ref, other_ref, w_key_ref, w_value_ref, q_ref)):
        out_ref[:, at * HEAD_WIDTH : (at + 1) * HEAD_WIDTH] = part.astype(BF16)


def attend_last_body(
    mine_ref, other_ref, w_key_ref, w_value_ref, q_ref, behind_ref, *refs
):
    before, last_ref, out_ref = refs[:-2], refs[-2], refs[-1]
    parts = attended(mine_ref, other_ref, w_key_ref, w_value_ref, q_ref)
    for at, part in enumerate(parts):
        cols = slice(at * HEAD_WIDTH, (at + 1) * HEAD_WIDTH)
        part = part.astype(BF16).astype(F32)
        stack = [behind_ref[:, cols].astype(F32)]
        stack += [ref[:, cols].astype(F32) for ref in before]
        stack += [part, last_ref[:, cols].astype(F32)]
        tall = jnp.concatenate(stack, axis=0)
        moved = pltpu.roll(tall, tall.shape[0] - 1, 0)
        out_ref[:, cols] = moved[: out_ref.shape[0]].astype(BF16)


def per_device(queries, vocab_rows, neighbour_ids, w_in, w_out, w_key, w_value):
    seq_size = lax.axis_size("seq")
    groups, nbrs, nlen = neighbour_ids.shape
    per_group = nbrs * nlen
    rows = groups * per_group
    voc, width = vocab_rows.shape
    tok, head_cols = queries.shape
    cap = max(2, 2 * rows // seq_size)
    slots = seq_size * cap
    sds = jax.ShapeDtypeStruct

    next_q = shifted(queries[:GROUP], -1)

    wanted, slot = call(
        functools.partial(route_body, voc, cap),
        (sds((seq_size, cap), jnp.int32), sds((rows, LANES), jnp.int32)),
        "route",
        (neighbour_ids.reshape(1, rows),),
    )
    request = lax.all_to_all(wanted, "seq", split_axis=0, concat_axis=0, tiled=True)
    found = call(
        fetch_body,
        sds((slots, width), BF16),
        "fetch",
        (request.reshape(1, slots), vocab_rows),
        (next_q,),
    )
    answered = lax.all_to_all(
        found.reshape(seq_size, cap, width), "seq", split_axis=0, concat_axis=0, tiled=True
    ).reshape(slots, width)
    order = [groups - 1] + list(range(groups - 1))
    plan = [order[at : at + 2] for at in range(0, groups, 2)]
    own = call(
        functools.partial(order_body, plan),
        tuple(sds((len(part) * per_group, width), BF16) for part in plan),
        "order",
        (slot, answered),
    )

    local_q = jnp.concatenate([queries[GROUP - 1 :], next_q[: GROUP - 1]], axis=0)
    half = sds((per_group, 2 * width), BF16)
    whole = sds((per_group, 2 * width), F32)
    emb, first, window = {}, {}, {}
    fed, summed, far, encoded = {}, {}, {}, {}
    behind = None
    token = slot

    for part, e0 in zip(plan, own):
        e2 = exchange(e0, 2)
        pieces = e0, e2, exchange(e0, 1), exchange(e2, 1)
        for at, g in enumerate(part):
            emb[g], first[g] = pieces, at * per_group

    def feed(g):
        nonlocal token
        keep, token = call(
            functools.partial(feed_body, first[g]),
            (whole, half),
            "feed",
            (*emb[g], w_in, w_out),
            (token,),
        )
        fed[g] = keep, exchange(token, 1)

    def add(g):
        nonlocal token
        summed[g], token = call(add_body, (whole, half), "add", fed[g], (token,))
        far[g] = exchange(token, 2)

    def finish(g):
        nonlocal token
        token = call(
            functools.partial(finish_body, first[g]),
            half,
            "finish",
            (*emb[g][:2], summed[g], far[g]),
            (token, behind) if g == order[-1] else (token,),
        )
        encoded[g] = token, exchange(token, 1)

    def attend(g):
        nonlocal token, behind
        args = (*encoded[g], w_key, w_value, local_q[g * GROUP : (g + 1) * GROUP])
        if g == order[-1]:
            before = [window[at] for at in order[1:-1]]
            return call(
                attend_last_body,
                sds((tok, head_cols), BF16),
                "attend_last",
                (*args, behind, *before, window[groups - 1]),
            )
        window[g] = token = call(
            attend_body, sds((GROUP, head_cols), BF16), "attend", args, (token,)
        )
        if g == groups - 1:
            behind = shifted(token, 1)
        return None

    out = None
    for stage in range(groups + 4):
        for step, lag in ((finish, 3), (attend, 4), (feed, 0), (add, 1)):
            if 0 <= stage - lag < groups:
                out = step(order[stage - lag])
    return out


def solution(mesh):
    return jax.shard_map(
        per_device,
        mesh=mesh,
        in_specs=(
            P("seq", "tp"),
            P("seq", "tp"),
            P("seq", None, None),
            P(None, "tp"),
            P("tp", None),
            P(None, "tp"),
            P(None, "tp"),
        ),
        out_specs=P("seq", "tp"),
        check_vma=False,
    )
```

```python
import functools

import jax
import jax.numpy as jnp
from jax import lax
from jax.experimental import pallas as pl
from jax.experimental.pallas import tpu as pltpu
from jax.sharding import PartitionSpec as P

HEAD_WIDTH = 128
GROUP = 64
LANES = 128
VMEM_LIMIT = 24 * 1024 * 1024
F32 = jnp.float32
BF16 = jnp.bfloat16


def call(body, outs, name, used=None, after=()):
    vmem = pl.BlockSpec(memory_space=pltpu.VMEM)
    unread = pl.BlockSpec(memory_space=pl.ANY)

    def without_after(*refs):
        body(*refs[: len(used)], *refs[len(used) + len(after) :])

    return pl.pallas_call(
        without_after,
        out_shape=outs,
        in_specs=[vmem] * len(used) + [unread] * len(after),
        compiler_params=pltpu.CompilerParams(vmem_limit_bytes=VMEM_LIMIT),
        cost_estimate=pl.CostEstimate(flops=1024, bytes_accessed=1024, transcendentals=0),
        name=name,
    )(*used, *after)


def exchange(x, bit):
    size = lax.axis_size("tp")
    return lax.ppermute(x, "tp", [(i, i ^ bit) for i in range(size)])


def shifted(x, by):
    length = lax.axis_size("seq")
    pairs = [(i, i + by) for i in range(length) if 0 <= i + by < length]
    return lax.ppermute(x, "seq", pairs)


def columns_of(row):
    return jnp.broadcast_to(row, (LANES, row.shape[1])).T


def one_hot(column, width):
    lane = lax.broadcasted_iota(jnp.int32, column.shape, 1)
    return jnp.concatenate(
        [jnp.where(column == lane + at, 1.0, 0.0).astype(BF16) for at in range(0, width, LANES)],
        axis=1,
    )


def route_body(voc, cap, mirrored, ids_ref, wanted_ref, slot_ref):
    ids = ids_ref[...]
    count = ids.shape[1]
    owners = wanted_ref.shape[0]
    owner = lax.div(ids, jnp.int32(voc))
    local = ids - owner * voc
    hit = owner == lax.broadcasted_iota(jnp.int32, (owners, count), 0)
    hot = jnp.where(hit, 1.0, 0.0)
    upper = jnp.where(
        lax.broadcasted_iota(jnp.int32, (LANES, LANES), 0)
        <= lax.broadcasted_iota(jnp.int32, (LANES, LANES), 1),
        1.0,
        0.0,
    ).astype(BF16)
    carry = jnp.zeros((owners, 1), F32)
    ranks = []
    for at in range(0, count, LANES):
        part = hot[:, at : at + LANES]
        running = jnp.dot(part.astype(BF16), upper, preferred_element_type=F32) + carry
        ranks.append(jnp.sum(part * running, axis=0, keepdims=True))
        carry = running[:, LANES - 1 :]
    rank = jnp.concatenate(ranks, axis=1).astype(jnp.int32) - 1
    high = jnp.where(hit, lax.div(local, jnp.int32(256)), 0)
    low = jnp.where(hit, lax.rem(local, jnp.int32(256)), 0)
    digits = jnp.concatenate([high, low], axis=0).astype(F32).astype(BF16)
    place = jnp.where(
        rank == lax.broadcasted_iota(jnp.int32, (cap, count), 0), 1.0, 0.0
    ).astype(BF16)
    found = lax.dot_general(
        digits, place, (((1,), (1,)), ((), ())), preferred_element_type=F32
    ).astype(jnp.int32)
    wanted_ref[...] = found[:owners] * 256 + found[owners:]
    if mirrored:
        owner = owner ^ lax.axis_index("seq")
    slot_ref[...] = columns_of(owner * cap + rank)


def fetch_body(req_ref, vocab_ref, out_ref):
    step = 256
    table = vocab_ref[...]
    for at in range(0, req_ref.shape[1], step):
        picked = one_hot(columns_of(req_ref[:, at : at + step]), table.shape[0])
        out_ref[at : at + step, :] = jnp.dot(
            picked, table, preferred_element_type=F32
        ).astype(BF16)


def fetch_for_body(partners, req_ref, vocab_ref, *out_refs):
    me = lax.axis_index("seq")
    table = vocab_ref[...]
    for at, k in enumerate(partners):
        picked = one_hot(columns_of(req_ref[me ^ k]), table.shape[0])
        rows = jnp.dot(picked, table, preferred_element_type=F32).astype(BF16)
        for half in range(2):
            out_refs[2 * at + half][...] = rows[:, half * LANES : (half + 1) * LANES]


def order_body(slot_ref, *refs):
    rows_refs, out_ref = refs[:-1], refs[-1]
    step = 256
    for at in range(0, out_ref.shape[0], step):
        total, base = None, 0
        for rows_ref in rows_refs:
            count = rows_ref.shape[0]
            picked = one_hot(slot_ref[at : at + step, :] - base, count)
            part = jnp.dot(picked, rows_ref[...], preferred_element_type=F32)
            total, base = part if total is None else total + part, base + count
        out_ref[at : at + step, :] = total.astype(BF16)


def block_rows(ref, index, width):
    return ref[pl.ds(pl.multiple_of(index * width, width), width), :]


def block_cols(ref, index, width):
    return ref[:, pl.ds(pl.multiple_of(index * width, width), width)]


def piece(refs, here):
    return jnp.concatenate([ref[here, :] for ref in refs], axis=1)


def feed_body(first, *refs):
    emb_refs, (w_in_ref, w_out_ref, keep_ref, send_ref) = refs[:-4], refs[-4:]
    me = lax.axis_index("tp")
    index = [me, me ^ 2, me ^ 1, me ^ 3]
    here = slice(first, first + keep_ref.shape[0])
    parts = [piece(emb_refs[2 * at : 2 * at + 2], here).astype(F32) for at in range(4)]
    width = parts[0].shape[1]
    square = sum(jnp.sum(part * part, axis=1, keepdims=True) for part in parts)
    scale = lax.rsqrt(square / (4 * width) + 1e-06)
    hidden = sum(
        jnp.dot(
            (part * scale).astype(BF16), block_rows(w_in_ref, at, width), preferred_element_type=F32
        )
        for part, at in zip(parts, index)
    )
    inner = jax.nn.gelu(hidden, approximate=True).astype(BF16)
    for slot in range(2):
        cols = slice(slot * width, (slot + 1) * width)
        keep_ref[:, cols] = jnp.dot(
            inner, block_cols(w_out_ref, index[slot], width), preferred_element_type=F32
        )
        send_ref[:, cols] = jnp.dot(
            inner, block_cols(w_out_ref, index[2 + slot], width), preferred_element_type=F32
        ).astype(BF16)


def add_body(keep_ref, recv_ref, chip_ref, send_ref):
    chip = keep_ref[...] + recv_ref[...].astype(F32)
    chip_ref[...] = chip
    send_ref[...] = chip.astype(BF16)


def finish_body(first, *refs):
    emb_refs, (chip_ref, far_ref, mine_ref) = refs[:-3], refs[-3:]
    width = mine_ref.shape[1] // 2
    near, past = slice(0, width), slice(width, 2 * width)
    here = slice(first, first + mine_ref.shape[0])
    mine_ref[:, near] = (
        piece(emb_refs[:2], here).astype(F32) + (chip_ref[:, near] + far_ref[:, past].astype(F32))
    ).astype(BF16)
    mine_ref[:, past] = (
        piece(emb_refs[2:], here).astype(F32) + (chip_ref[:, past] + far_ref[:, near].astype(F32))
    ).astype(BF16)


def attended(mine_ref, other_ref, w_key_ref, w_value_ref, q_ref):
    me = lax.axis_index("tp")
    width = mine_ref.shape[1] // 2
    parts = [
        (mine_ref[:, :width], me),
        (mine_ref[:, width:], me ^ 2),
        (other_ref[:, :width], me ^ 1),
        (other_ref[:, width:], me ^ 3),
    ]

    def project(w_ref):
        return sum(
            jnp.dot(part, block_rows(w_ref, at, width), preferred_element_type=F32)
            for part, at in parts
        ).astype(BF16)

    heads = [slice(at, at + HEAD_WIDTH) for at in range(0, q_ref.shape[1], HEAD_WIDTH)]
    keys = project(w_key_ref)
    weights = []
    for cols in heads:
        logits = lax.dot_general(
            q_ref[:, cols], keys[:, cols], (((1,), (1,)), ((), ())), preferred_element_type=F32
        ) * HEAD_WIDTH ** (-0.5)
        expo = jnp.exp(logits)
        weights.append((expo * (1.0 / jnp.sum(expo, axis=1, keepdims=True))).astype(BF16))
    values = project(w_value_ref)
    return [
        jnp.dot(weight, values[:, cols], preferred_element_type=F32)
        for weight, cols in zip(weights, heads)
    ]


def attend_body(mine_ref, other_ref, w_key_ref, w_value_ref, q_ref, out_ref):
    for at, part in enumerate(attended(mine_ref, other_ref, w_key_ref, w_value_ref, q_ref)):
        out_ref[:, at * HEAD_WIDTH : (at + 1) * HEAD_WIDTH] = part.astype(BF16)


def attend_last_body(
    mine_ref, other_ref, w_key_ref, w_value_ref, q_ref, behind_ref, *refs
):
    before, last_ref, out_ref = refs[:-2], refs[-2], refs[-1]
    parts = attended(mine_ref, other_ref, w_key_ref, w_value_ref, q_ref)
    for at, part in enumerate(parts):
        cols = slice(at * HEAD_WIDTH, (at + 1) * HEAD_WIDTH)
        part = part.astype(BF16).astype(F32)
        stack = [behind_ref[:, cols].astype(F32)]
        stack += [ref[:, cols].astype(F32) for ref in before]
        stack += [part, last_ref[:, cols].astype(F32)]
        tall = jnp.concatenate(stack, axis=0)
        moved = pltpu.roll(tall, tall.shape[0] - 1, 0)
        out_ref[:, cols] = moved[: out_ref.shape[0]].astype(BF16)


def per_device(queries, vocab_rows, neighbour_ids, w_in, w_out, w_key, w_value):
    seq_size = lax.axis_size("seq")
    groups, nbrs, nlen = neighbour_ids.shape
    per_group = nbrs * nlen
    rows = groups * per_group
    voc, width = vocab_rows.shape
    tok, head_cols = queries.shape
    cap = max(2, 2 * rows // seq_size)
    slots = seq_size * cap
    sds = jax.ShapeDtypeStruct

    next_q = shifted(queries[:GROUP], -1)

    mirrored = seq_size <= 8 and seq_size & (seq_size - 1) == 0
    wanted, slot = call(
        functools.partial(route_body, voc, cap, mirrored),
        (sds((seq_size, cap), jnp.int32), sds((rows, LANES), jnp.int32)),
        "route",
        (neighbour_ids.reshape(1, rows),),
    )
    request = lax.all_to_all(wanted, "seq", split_axis=0, concat_axis=0, tiled=True)
    if mirrored:
        request = request.reshape(seq_size, 1, cap)
        part = sds((cap, LANES), BF16)
        found = {}
        token = None
        for partners in (range(seq_size // 2, seq_size), range(seq_size // 2)):
            got = call(
                functools.partial(fetch_for_body, partners),
                (part,) * (2 * len(partners)),
                "fetch",
                (request, vocab_rows),
                () if token is None else (token,),
            )
            token = got[0]
            for at, k in enumerate(partners):
                found[k] = got[2 * at : 2 * at + 2]
        answered = [
            [found[k][half] if k == 0 else lax.ppermute(
                found[k][half], "seq", [(i, i ^ k) for i in range(seq_size)]
            ) for k in range(seq_size)]
            for half in range(2)
        ]
    else:
        found = call(
            fetch_body,
            sds((slots, width), BF16),
            "fetch",
            (request.reshape(1, slots), vocab_rows),
        )
        answered = lax.all_to_all(
            found.reshape(seq_size, cap, width), "seq", split_axis=0, concat_axis=0, tiled=True
        ).reshape(slots, width)
        answered = [[answered[:, :LANES]], [answered[:, LANES:]]]
    order = [groups - 1] + list(range(groups - 1))
    emb = [[], [], [], []]
    token = slot
    for half in range(2):
        e0 = call(
            order_body, sds((rows, LANES), BF16), "order", (slot, *answered[half]), (token,)
        )
        e2 = exchange(e0, 2)
        for at, part in enumerate((e0, e2, exchange(e0, 1), exchange(e2, 1))):
            emb[at].append(part)
        token = e2
    emb = [part for pair in emb for part in pair]

    local_q = jnp.concatenate([queries[GROUP - 1 :], next_q[: GROUP - 1]], axis=0)
    half = sds((per_group, 2 * width), BF16)
    whole = sds((per_group, 2 * width), F32)
    window, fed, summed, far, encoded = {}, {}, {}, {}, {}
    behind = None

    def feed(g):
        nonlocal token
        keep, token = call(
            functools.partial(feed_body, g * per_group),
            (whole, half),
            "feed",
            (*emb, w_in, w_out),
            (token,),
        )
        fed[g] = keep, exchange(token, 1)

    def add(g):
        nonlocal token
        summed[g], token = call(add_body, (whole, half), "add", fed[g], (token,))
        far[g] = exchange(token, 2)

    def finish(g):
        nonlocal token
        token = call(
            functools.partial(finish_body, g * per_group),
            half,
            "finish",
            (*emb[:4], summed[g], far[g]),
            (token, behind) if g == order[-1] else (token,),
        )
        encoded[g] = token, exchange(token, 1)

    def attend(g):
        nonlocal token, behind
        args = (*encoded[g], w_key, w_value, local_q[g * GROUP : (g + 1) * GROUP])
        if g == order[-1]:
            before = [window[at] for at in order[1:-1]]
            return call(
                attend_last_body,
                sds((tok, head_cols), BF16),
                "attend_last",
                (*args, behind, *before, window[groups - 1]),
            )
        window[g] = token = call(
            attend_body, sds((GROUP, head_cols), BF16), "attend", args, (token,)
        )
        if g == groups - 1:
            behind = shifted(token, 1)
        return None

    out = None
    for stage in range(groups + 4):
        for step, lag in ((finish, 3), (attend, 4), (feed, 0), (add, 1)):
            if 0 <= stage - lag < groups:
                out = step(order[stage - lag])
    return out


def solution(mesh):
    return jax.shard_map(
        per_device,
        mesh=mesh,
        in_specs=(
            P("seq", "tp"),
            P("seq", "tp"),
            P("seq", None, None),
            P(None, "tp"),
            P("tp", None),
            P(None, "tp"),
            P(None, "tp"),
        ),
        out_specs=P("seq", "tp"),
        check_vma=False,
    )
```

```python
import functools

import jax
import jax.numpy as jnp
from jax import lax
from jax.experimental import pallas as pl
from jax.experimental.pallas import tpu as pltpu
from jax.sharding import PartitionSpec as P

HEAD_WIDTH = 128
GROUP = 64
LANES = 128
VMEM_LIMIT = 24 * 1024 * 1024
F32 = jnp.float32
BF16 = jnp.bfloat16


def call(body, outs, name, used, after=(), flops=1024, **extra):
    vmem = pl.BlockSpec(memory_space=pltpu.VMEM)
    unread = pl.BlockSpec(memory_space=pl.ANY)
    in_specs = extra.pop("in_specs", [vmem] * len(used))

    def without_after(*refs):
        body(*refs[: len(used)], *refs[len(used) + len(after) :])

    return pl.pallas_call(
        without_after,
        out_shape=outs,
        in_specs=in_specs + [unread] * len(after),
        compiler_params=pltpu.CompilerParams(vmem_limit_bytes=VMEM_LIMIT),
        cost_estimate=pl.CostEstimate(flops=flops, bytes_accessed=1024, transcendentals=0),
        name=name,
        **extra,
    )(*used, *after)


def exchange(x, bit):
    size = lax.axis_size("tp")
    return lax.ppermute(x, "tp", [(i, i ^ bit) for i in range(size)])


def shifted(x, by):
    length = lax.axis_size("seq")
    pairs = [(i, i + by) for i in range(length) if 0 <= i + by < length]
    return lax.ppermute(x, "seq", pairs)


def columns_of(row):
    return jnp.broadcast_to(row, (LANES, row.shape[1])).T


def one_hot(column, width):
    lane = lax.broadcasted_iota(jnp.int32, column.shape, 1)
    return jnp.concatenate(
        [jnp.where(column == lane + at, 1.0, 0.0).astype(BF16) for at in range(0, width, LANES)],
        axis=1,
    )


def route_body(voc, cap, ids_ref, wanted_ref, slot_ref):
    ids = ids_ref[...]
    count = ids.shape[1]
    owners = wanted_ref.shape[0]
    owner = lax.div(ids, jnp.int32(voc))
    local = ids - owner * voc
    hit = owner == lax.broadcasted_iota(jnp.int32, (owners, count), 0)
    hot = jnp.where(hit, 1.0, 0.0)
    upper = jnp.where(
        lax.broadcasted_iota(jnp.int32, (LANES, LANES), 0)
        <= lax.broadcasted_iota(jnp.int32, (LANES, LANES), 1),
        1.0,
        0.0,
    ).astype(BF16)
    carry = jnp.zeros((owners, 1), F32)
    ranks = []
    for at in range(0, count, LANES):
        part = hot[:, at : at + LANES]
        running = jnp.dot(part.astype(BF16), upper, preferred_element_type=F32) + carry
        ranks.append(jnp.sum(part * running, axis=0, keepdims=True))
        carry = running[:, LANES - 1 :]
    rank = jnp.concatenate(ranks, axis=1).astype(jnp.int32) - 1
    high = jnp.where(hit, lax.div(local, jnp.int32(256)), 0)
    low = jnp.where(hit, lax.rem(local, jnp.int32(256)), 0)
    digits = jnp.concatenate([high, low], axis=0).astype(F32).astype(BF16)
    place = jnp.where(
        rank == lax.broadcasted_iota(jnp.int32, (cap, count), 0), 1.0, 0.0
    ).astype(BF16)
    found = lax.dot_general(
        digits, place, (((1,), (1,)), ((), ())), preferred_element_type=F32
    ).astype(jnp.int32)
    wanted_ref[...] = found[:owners] * 256 + found[owners:]
    slot_ref[...] = columns_of(owner * cap + rank)


def fetch_body(req_ref, vocab_ref, out_ref):
    step = 256
    table = vocab_ref[...]
    for at in range(0, req_ref.shape[1], step):
        picked = one_hot(columns_of(req_ref[:, at : at + step]), table.shape[0])
        out_ref[at : at + step, :] = jnp.dot(
            picked, table, preferred_element_type=F32
        ).astype(BF16)


def mark_body(out_ref):
    out_ref[...] = jnp.zeros_like(out_ref)


def head_body(queries_ref, out_ref):
    out_ref[...] = queries_ref[: out_ref.shape[0], :]


def order_body(groups, slot_ref, rows_ref, out_ref):
    rows = rows_ref[...]
    count = out_ref.shape[0] // len(groups)
    for at, g in enumerate(groups):
        picked = one_hot(slot_ref[g * count : (g + 1) * count, :], rows.shape[0])
        out_ref[at * count : (at + 1) * count, :] = jnp.dot(
            picked, rows, preferred_element_type=F32
        ).astype(BF16)


def block_rows(ref, index, width):
    return ref[pl.ds(pl.multiple_of(index * width, width), width), :]


def block_cols(ref, index, width):
    return ref[:, pl.ds(pl.multiple_of(index * width, width), width)]


def feed_body(first, e0_ref, e2_ref, e1_ref, e3_ref, w_in_ref, w_out_ref, keep_ref, send_ref):
    me = lax.axis_index("tp")
    width = e0_ref.shape[1]
    index = [me, me ^ 2, me ^ 1, me ^ 3]
    here = slice(first, first + keep_ref.shape[0])
    parts = [ref[here, :].astype(F32) for ref in (e0_ref, e2_ref, e1_ref, e3_ref)]
    square = sum(jnp.sum(part * part, axis=1, keepdims=True) for part in parts)
    scale = lax.rsqrt(square / (4 * width) + 1e-06)
    hidden = sum(
        jnp.dot(
            (part * scale).astype(BF16), block_rows(w_in_ref, at, width), preferred_element_type=F32
        )
        for part, at in zip(parts, index)
    )
    inner = jax.nn.gelu(hidden, approximate=True).astype(BF16)
    for slot in range(2):
        cols = slice(slot * width, (slot + 1) * width)
        keep_ref[:, cols] = jnp.dot(
            inner, block_cols(w_out_ref, index[slot], width), preferred_element_type=F32
        )
        send_ref[:, cols] = jnp.dot(
            inner, block_cols(w_out_ref, index[2 + slot], width), preferred_element_type=F32
        ).astype(BF16)


def add_body(keep_ref, recv_ref, chip_ref, send_ref):
    chip = keep_ref[...] + recv_ref[...].astype(F32)
    chip_ref[...] = chip
    send_ref[...] = chip.astype(BF16)


def finish_body(first, e0_ref, e2_ref, chip_ref, far_ref, mine_ref):
    width = e0_ref.shape[1]
    near, past = slice(0, width), slice(width, 2 * width)
    here = slice(first, first + mine_ref.shape[0])
    mine_ref[:, near] = (
        e0_ref[here, :].astype(F32) + (chip_ref[:, near] + far_ref[:, past].astype(F32))
    ).astype(BF16)
    mine_ref[:, past] = (
        e2_ref[here, :].astype(F32) + (chip_ref[:, past] + far_ref[:, near].astype(F32))
    ).astype(BF16)


def attended(mine_ref, other_ref, w_key_ref, w_value_ref, q_ref):
    me = lax.axis_index("tp")
    width = mine_ref.shape[1] // 2
    parts = [
        (mine_ref[:, :width], me),
        (mine_ref[:, width:], me ^ 2),
        (other_ref[:, :width], me ^ 1),
        (other_ref[:, width:], me ^ 3),
    ]

    def project(w_ref):
        return sum(
            jnp.dot(part, block_rows(w_ref, at, width), preferred_element_type=F32)
            for part, at in parts
        ).astype(BF16)

    heads = [slice(at, at + HEAD_WIDTH) for at in range(0, q_ref.shape[1], HEAD_WIDTH)]
    keys = project(w_key_ref)
    weights = []
    for cols in heads:
        logits = lax.dot_general(
            q_ref[:, cols], keys[:, cols], (((1,), (1,)), ((), ())), preferred_element_type=F32
        ) * HEAD_WIDTH ** (-0.5)
        expo = jnp.exp(logits)
        weights.append((expo * (1.0 / jnp.sum(expo, axis=1, keepdims=True))).astype(BF16))
    values = project(w_value_ref)
    return [
        jnp.dot(weight, values[:, cols], preferred_element_type=F32)
        for weight, cols in zip(weights, heads)
    ]


def attend_body(mine_ref, other_ref, w_key_ref, w_value_ref, q_ref, out_ref):
    for at, part in enumerate(attended(mine_ref, other_ref, w_key_ref, w_value_ref, q_ref)):
        out_ref[:, at * HEAD_WIDTH : (at + 1) * HEAD_WIDTH] = part.astype(BF16)


def one_up(refs, cols, rows):
    tall = jnp.concatenate([ref[:, cols].astype(F32) for ref in refs], axis=0)
    return pltpu.roll(tall, tall.shape[0] - 1, 0)[:rows].astype(BF16)


def attend_before_body(
    mine_ref, other_ref, w_key_ref, w_value_ref, q_ref, *refs
):
    earlier, (window_ref, out_hbm, rows_ref, sem) = refs[:-4], refs[-4:]
    for at, part in enumerate(attended(mine_ref, other_ref, w_key_ref, w_value_ref, q_ref)):
        cols = slice(at * HEAD_WIDTH, (at + 1) * HEAD_WIDTH)
        window_ref[:, cols] = part.astype(BF16)
        rows_ref[:, cols] = one_up((*earlier, window_ref), cols, rows_ref.shape[0])
    copy = pltpu.make_async_copy(rows_ref, out_hbm.at[pl.ds(0, rows_ref.shape[0]), :], sem)
    copy.start()
    copy.wait()


def attend_last_body(
    mine_ref, other_ref, w_key_ref, w_value_ref, q_ref, before_ref, after_ref, _, out_hbm, window_ref, rows_ref, sem
):
    count = rows_ref.shape[0]
    edge = (count - window_ref.shape[0])
    for at, part in enumerate(attended(mine_ref, other_ref, w_key_ref, w_value_ref, q_ref)):
        cols = slice(at * HEAD_WIDTH, (at + 1) * HEAD_WIDTH)
        window_ref[:, cols] = part.astype(BF16)
        pieces = (before_ref.at[pl.ds(GROUP - edge, edge), :], window_ref, after_ref.at[pl.ds(0, edge), :])
        rows_ref[:, cols] = one_up(pieces, cols, count)
    copy = pltpu.make_async_copy(
        rows_ref, out_hbm.at[pl.ds(out_hbm.shape[0] - count, count), :], sem
    )
    copy.start()
    copy.wait()


def per_device(queries, vocab_rows, neighbour_ids, w_in, w_out, w_key, w_value):
    seq_size = lax.axis_size("seq")
    groups, nbrs, nlen = neighbour_ids.shape
    per_group = nbrs * nlen
    rows = groups * per_group
    voc, width = vocab_rows.shape
    tok, head_cols = queries.shape
    cap = max(2, 2 * rows // seq_size)
    slots = seq_size * cap
    sds = jax.ShapeDtypeStruct

    wanted, slot = call(
        functools.partial(route_body, voc, cap),
        (sds((seq_size, cap), jnp.int32), sds((rows, LANES), jnp.int32)),
        "route",
        (neighbour_ids.reshape(1, rows),),
        flops=8 * 10**9,
    )
    request = lax.all_to_all(wanted, "seq", split_axis=0, concat_axis=0, tiled=True)
    found = call(
        fetch_body,
        sds((slots, width), BF16),
        "fetch",
        (request.reshape(1, slots), vocab_rows),
    )
    answered = lax.all_to_all(
        found.reshape(seq_size, cap, width), "seq", split_axis=0, concat_axis=0, tiled=True
    ).reshape(slots, width)
    order = [groups - 1] + list(range(groups - 1))
    plan = [order[:1], order[1:2], order[2:]]
    emb, first, window = {}, {}, {}
    token = slot
    ahead = []
    for part in plan:
        e0 = token = call(
            functools.partial(order_body, part),
            sds((len(part) * per_group, width), BF16),
            "order",
            (slot, answered),
            (token,),
        )
        e2 = exchange(e0, 2)
        pieces = e0, e2, exchange(e0, 1), exchange(e2, 1)
        ahead.append(e2)
        for at, g in enumerate(part):
            emb[g], first[g] = pieces, at * per_group

    head = call(head_body, sds((GROUP, head_cols), BF16), "head", (queries,), (token,))
    next_q = shifted(head, -1)
    local_q = jnp.concatenate([queries[GROUP - 1 :], next_q[: GROUP - 1]], axis=0)
    half = sds((per_group, 2 * width), BF16)
    whole = sds((per_group, 2 * width), F32)
    fed, summed, far, encoded = {}, {}, {}, {}
    behind = out = None

    def feed(g):
        nonlocal token
        keep, token = call(
            functools.partial(feed_body, first[g]),
            (whole, half),
            "feed",
            (*emb[g], w_in, w_out),
            (token,),
        )
        fed[g] = keep, exchange(token, 1)

    def pause(g):
        nonlocal token
        if g == order[0]:
            token = call(mark_body, sds((8, LANES), F32), "mark", (), (token, ahead[-1]))

    def add(g):
        nonlocal token
        summed[g], token = call(add_body, (whole, half), "add", fed[g], (token,))
        far[g] = exchange(token, 2)

    def finish(g):
        nonlocal token
        token = call(
            functools.partial(finish_body, first[g]),
            half,
            "finish",
            (*emb[g][:2], summed[g], far[g]),
            (token, *{order[0]: (next_q,), order[-1]: (behind,)}.get(g, ())),
        )
        encoded[g] = token, exchange(token, 1)

    def attend(g):
        nonlocal token, behind, out
        args = (*encoded[g], w_key, w_value, local_q[g * GROUP : (g + 1) * GROUP])
        piece = sds((GROUP, head_cols), BF16)
        edge = 16
        last_rows = GROUP + edge
        vmem, hbm = pl.BlockSpec(memory_space=pltpu.VMEM), pl.BlockSpec(memory_space=pl.ANY)

        def scratch(count):
            return [pltpu.VMEM((count, head_cols), BF16), pltpu.SemaphoreType.DMA]

        if g == order[-1]:
            out = call(
                attend_last_body,
                sds((tok, head_cols), BF16),
                "attend_last",
                (*args, window[order[-2]], window[order[0]], out),
                in_specs=[vmem] * (len(args) + 2) + [hbm],
                out_specs=hbm,
                scratch_shapes=[pltpu.VMEM((GROUP, head_cols), BF16), *scratch(last_rows)],
                input_output_aliases={len(args) + 2: 0},
            )
        elif g == order[-2]:
            window[g], out = call(
                attend_before_body,
                (piece, sds((tok, head_cols), BF16)),
                "attend_before",
                (*args, behind, *[window[at] for at in order[1:-2]]),
                (token,),
                out_specs=(vmem, hbm),
                scratch_shapes=scratch(tok - last_rows),
            )
            token = window[g]
        else:
            window[g] = token = call(attend_body, piece, "attend", args, (token,))
            if g == order[0]:
                behind = shifted(token, 1)

    for stage in range(groups + 4):
        for step, lag in ((finish, 3), (attend, 4), (feed, 0), (pause, 1), (add, 1)):
            if 0 <= stage - lag < groups:
                step(order[stage - lag])
    return out


def solution(mesh):
    return jax.shard_map(
        per_device,
        mesh=mesh,
        in_specs=(
            P("seq", "tp"),
            P("seq", "tp"),
            P("seq", None, None),
            P(None, "tp"),
            P("tp", None),
            P(None, "tp"),
            P(None, "tp"),
        ),
        out_specs=P("seq", "tp"),
        check_vma=False,
    )
```

```python
import functools

import jax
import jax.numpy as jnp
from jax import lax
from jax.experimental import pallas as pl
from jax.experimental.pallas import tpu as pltpu
from jax.sharding import PartitionSpec as P

HEAD_WIDTH = 128
GROUP = 64
LANES = 128
VMEM_LIMIT = 24 * 1024 * 1024
F32 = jnp.float32
BF16 = jnp.bfloat16


def call(body, outs, name, used, after=(), flops=1024, **extra):
    vmem = pl.BlockSpec(memory_space=pltpu.VMEM)
    unread = pl.BlockSpec(memory_space=pl.ANY)
    in_specs = extra.pop("in_specs", [vmem] * len(used))

    def without_after(*refs):
        body(*refs[: len(used)], *refs[len(used) + len(after) :])

    return pl.pallas_call(
        without_after,
        out_shape=outs,
        in_specs=in_specs + [unread] * len(after),
        compiler_params=pltpu.CompilerParams(vmem_limit_bytes=VMEM_LIMIT),
        cost_estimate=pl.CostEstimate(flops=flops, bytes_accessed=1024, transcendentals=0),
        name=name,
        **extra,
    )(*used, *after)


def exchange(x, bit):
    size = lax.axis_size("tp")
    return lax.ppermute(x, "tp", [(i, i ^ bit) for i in range(size)])


def shifted(x, by):
    length = lax.axis_size("seq")
    pairs = [(i, i + by) for i in range(length) if 0 <= i + by < length]
    return lax.ppermute(x, "seq", pairs)


def columns_of(row):
    return jnp.broadcast_to(row, (LANES, row.shape[1])).T


def one_hot(column, width):
    lane = lax.broadcasted_iota(jnp.int32, column.shape, 1)
    return jnp.concatenate(
        [jnp.where(column == lane + at, 1.0, 0.0).astype(BF16) for at in range(0, width, LANES)],
        axis=1,
    )


def route_body(voc, cap, ids_ref, wanted_ref, slot_ref):
    ids = ids_ref[...]
    count = ids.shape[1]
    owners = wanted_ref.shape[0]
    owner = lax.div(ids, jnp.int32(voc))
    local = ids - owner * voc
    hit = owner == lax.broadcasted_iota(jnp.int32, (owners, count), 0)
    hot = jnp.where(hit, 1.0, 0.0)
    upper = jnp.where(
        lax.broadcasted_iota(jnp.int32, (LANES, LANES), 0)
        <= lax.broadcasted_iota(jnp.int32, (LANES, LANES), 1),
        1.0,
        0.0,
    ).astype(BF16)
    carry = jnp.zeros((owners, 1), F32)
    ranks = []
    for at in range(0, count, LANES):
        part = hot[:, at : at + LANES]
        running = jnp.dot(part.astype(BF16), upper, preferred_element_type=F32) + carry
        ranks.append(jnp.sum(part * running, axis=0, keepdims=True))
        carry = running[:, LANES - 1 :]
    rank = jnp.concatenate(ranks, axis=1).astype(jnp.int32) - 1
    high = jnp.where(hit, lax.div(local, jnp.int32(256)), 0)
    low = jnp.where(hit, lax.rem(local, jnp.int32(256)), 0)
    digits = jnp.concatenate([high, low], axis=0).astype(F32).astype(BF16)
    place = jnp.where(
        rank == lax.broadcasted_iota(jnp.int32, (cap, count), 0), 1.0, 0.0
    ).astype(BF16)
    found = lax.dot_general(
        digits, place, (((1,), (1,)), ((), ())), preferred_element_type=F32
    ).astype(jnp.int32)
    wanted_ref[...] = found[:owners] * 256 + found[owners:]
    slot_ref[...] = columns_of(owner * cap + rank)


def fetch_body(req_ref, vocab_ref, out_ref):
    step = 256
    table = vocab_ref[...]
    for at in range(0, req_ref.shape[1], step):
        picked = one_hot(columns_of(req_ref[:, at : at + step]), table.shape[0])
        out_ref[at : at + step, :] = jnp.dot(
            picked, table, preferred_element_type=F32
        ).astype(BF16)


def pair_body(left_ref, right_ref, out_ref):
    width = left_ref.shape[1]
    out_ref[:, :width] = left_ref[...]
    out_ref[:, width:] = right_ref[...]


def head_body(queries_ref, out_ref):
    out_ref[...] = queries_ref[: out_ref.shape[0], :]


def order_body(groups, slot_ref, rows_ref, out_ref):
    rows = rows_ref[...]
    count = out_ref.shape[0] // len(groups)
    for at, g in enumerate(groups):
        picked = one_hot(slot_ref[g * count : (g + 1) * count, :], rows.shape[0])
        out_ref[at * count : (at + 1) * count, :] = jnp.dot(
            picked, rows, preferred_element_type=F32
        ).astype(BF16)


def block_rows(ref, index, width):
    return ref[pl.ds(pl.multiple_of(index * width, width), width), :]


def block_cols(ref, index, width):
    return ref[:, pl.ds(pl.multiple_of(index * width, width), width)]


def feed_body(first, e0_ref, e2_ref, other_ref, w_in_ref, w_out_ref, keep_ref, send_ref):
    me = lax.axis_index("tp")
    width = e0_ref.shape[1]
    index = [me, me ^ 2, me ^ 1, me ^ 3]
    here = slice(first, first + keep_ref.shape[0])
    parts = [e0_ref[here, :], e2_ref[here, :], other_ref[here, :width], other_ref[here, width:]]
    parts = [part.astype(F32) for part in parts]
    square = sum(jnp.sum(part * part, axis=1, keepdims=True) for part in parts)
    scale = lax.rsqrt(square / (4 * width) + 1e-06)
    hidden = sum(
        jnp.dot(
            (part * scale).astype(BF16), block_rows(w_in_ref, at, width), preferred_element_type=F32
        )
        for part, at in zip(parts, index)
    )
    inner = jax.nn.gelu(hidden, approximate=True).astype(BF16)
    for slot in range(2):
        cols = slice(slot * width, (slot + 1) * width)
        keep_ref[:, cols] = jnp.dot(
            inner, block_cols(w_out_ref, index[slot], width), preferred_element_type=F32
        )
        send_ref[:, cols] = jnp.dot(
            inner, block_cols(w_out_ref, index[2 + slot], width), preferred_element_type=F32
        ).astype(BF16)


def add_body(keep_ref, recv_ref, chip_ref, send_ref):
    chip = keep_ref[...] + recv_ref[...].astype(F32)
    chip_ref[...] = chip
    send_ref[...] = chip.astype(BF16)


def finish_body(first, e0_ref, e2_ref, chip_ref, far_ref, mine_ref):
    width = e0_ref.shape[1]
    near, past = slice(0, width), slice(width, 2 * width)
    here = slice(first, first + mine_ref.shape[0])
    mine_ref[:, near] = (
        e0_ref[here, :].astype(F32) + (chip_ref[:, near] + far_ref[:, past].astype(F32))
    ).astype(BF16)
    mine_ref[:, past] = (
        e2_ref[here, :].astype(F32) + (chip_ref[:, past] + far_ref[:, near].astype(F32))
    ).astype(BF16)


def attended(mine_ref, other_ref, w_key_ref, w_value_ref, q_ref):
    me = lax.axis_index("tp")
    width = mine_ref.shape[1] // 2
    parts = [
        (mine_ref[:, :width], me),
        (mine_ref[:, width:], me ^ 2),
        (other_ref[:, :width], me ^ 1),
        (other_ref[:, width:], me ^ 3),
    ]

    def project(w_ref):
        return sum(
            jnp.dot(part, block_rows(w_ref, at, width), preferred_element_type=F32)
            for part, at in parts
        ).astype(BF16)

    heads = [slice(at, at + HEAD_WIDTH) for at in range(0, q_ref.shape[1], HEAD_WIDTH)]
    keys = project(w_key_ref)
    weights = []
    for cols in heads:
        logits = lax.dot_general(
            q_ref[:, cols], keys[:, cols], (((1,), (1,)), ((), ())), preferred_element_type=F32
        ) * HEAD_WIDTH ** (-0.5)
        expo = jnp.exp(logits)
        weights.append((expo * (1.0 / jnp.sum(expo, axis=1, keepdims=True))).astype(BF16))
    values = project(w_value_ref)
    return [
        jnp.dot(weight, values[:, cols], preferred_element_type=F32)
        for weight, cols in zip(weights, heads)
    ]


def attend_body(mine_ref, other_ref, w_key_ref, w_value_ref, q_ref, out_ref):
    for at, part in enumerate(attended(mine_ref, other_ref, w_key_ref, w_value_ref, q_ref)):
        out_ref[:, at * HEAD_WIDTH : (at + 1) * HEAD_WIDTH] = part.astype(BF16)


def one_up(refs, cols, rows):
    tall = jnp.concatenate([ref[:, cols].astype(F32) for ref in refs], axis=0)
    return pltpu.roll(tall, tall.shape[0] - 1, 0)[:rows].astype(BF16)


def attend_before_body(
    mine_ref, other_ref, w_key_ref, w_value_ref, q_ref, *refs
):
    earlier, (window_ref, out_hbm, rows_ref, sem) = refs[:-4], refs[-4:]
    for at, part in enumerate(attended(mine_ref, other_ref, w_key_ref, w_value_ref, q_ref)):
        cols = slice(at * HEAD_WIDTH, (at + 1) * HEAD_WIDTH)
        window_ref[:, cols] = part.astype(BF16)
        rows_ref[:, cols] = one_up((*earlier, window_ref), cols, rows_ref.shape[0])
    copy = pltpu.make_async_copy(rows_ref, out_hbm.at[pl.ds(0, rows_ref.shape[0]), :], sem)
    copy.start()
    copy.wait()


def attend_last_body(
    mine_ref, other_ref, w_key_ref, w_value_ref, q_ref, before_ref, after_ref, _, out_hbm, window_ref, rows_ref, sem
):
    count = rows_ref.shape[0]
    edge = (count - window_ref.shape[0])
    for at, part in enumerate(attended(mine_ref, other_ref, w_key_ref, w_value_ref, q_ref)):
        cols = slice(at * HEAD_WIDTH, (at + 1) * HEAD_WIDTH)
        window_ref[:, cols] = part.astype(BF16)
        pieces = (before_ref.at[pl.ds(GROUP - edge, edge), :], window_ref, after_ref.at[pl.ds(0, edge), :])
        rows_ref[:, cols] = one_up(pieces, cols, count)
    copy = pltpu.make_async_copy(
        rows_ref, out_hbm.at[pl.ds(out_hbm.shape[0] - count, count), :], sem
    )
    copy.start()
    copy.wait()


def per_device(queries, vocab_rows, neighbour_ids, w_in, w_out, w_key, w_value):
    seq_size = lax.axis_size("seq")
    groups, nbrs, nlen = neighbour_ids.shape
    per_group = nbrs * nlen
    rows = groups * per_group
    voc, width = vocab_rows.shape
    tok, head_cols = queries.shape
    cap = max(2, 2 * rows // seq_size)
    slots = seq_size * cap
    sds = jax.ShapeDtypeStruct

    wanted, slot = call(
        functools.partial(route_body, voc, cap),
        (sds((seq_size, cap), jnp.int32), sds((rows, LANES), jnp.int32)),
        "route",
        (neighbour_ids.reshape(1, rows),),
        flops=8 * 10**9,
    )
    request = lax.all_to_all(wanted, "seq", split_axis=0, concat_axis=0, tiled=True)
    found = call(
        fetch_body,
        sds((slots, width), BF16),
        "fetch",
        (request.reshape(1, slots), vocab_rows),
    )
    answered = lax.all_to_all(
        found.reshape(seq_size, cap, width), "seq", split_axis=0, concat_axis=0, tiled=True
    ).reshape(slots, width)
    order = [groups - 1] + list(range(groups - 1))
    plan = [order[:1], order[1:]]
    first, window = {}, {}
    token = slot
    pieces = []
    for part in plan:
        e0 = token = call(
            functools.partial(order_body, part),
            sds((len(part) * per_group, width), BF16),
            "order",
            (slot, answered),
            (token,),
        )
        pieces.append([e0, exchange(e0, 2), None])
        for at, g in enumerate(part):
            first[g] = at * per_group

    def across(piece, after=()):
        count = piece[0].shape[0]
        both = call(pair_body, sds((count, 2 * width), BF16), "pair", piece[:2], after)
        piece[2] = exchange(both, 1)

    across(pieces[0])
    head = call(head_body, sds((GROUP, head_cols), BF16), "head", (queries,), (token,))
    next_q = shifted(head, -1)
    local_q = jnp.concatenate([queries[GROUP - 1 :], next_q[: GROUP - 1]], axis=0)
    half = sds((per_group, 2 * width), BF16)
    whole = sds((per_group, 2 * width), F32)
    fed, summed, far, encoded = {}, {}, {}, {}
    behind = out = None

    def emb(g):
        return pieces[0 if g in plan[0] else 1]

    def rest(_):
        across(pieces[1], (token,))

    def feed(g):
        nonlocal token
        keep, token = call(
            functools.partial(feed_body, first[g]),
            (whole, half),
            "feed",
            (*emb(g), w_in, w_out),
            (token, pieces[1][1]),
        )
        fed[g] = keep, exchange(token, 1)

    def add(g):
        nonlocal token
        summed[g], token = call(add_body, (whole, half), "add", fed[g], (token,))
        far[g] = exchange(token, 2)

    def finish(g):
        nonlocal token
        token = call(
            functools.partial(finish_body, first[g]),
            half,
            "finish",
            (*emb(g)[:2], summed[g], far[g]),
            (token, *{order[0]: (next_q,), order[-1]: (behind,)}.get(g, ())),
        )
        encoded[g] = token, exchange(token, 1)

    def attend(g):
        nonlocal token, behind, out
        args = (*encoded[g], w_key, w_value, local_q[g * GROUP : (g + 1) * GROUP])
        piece = sds((GROUP, head_cols), BF16)
        edge = 16
        last_rows = GROUP + edge
        vmem, hbm = pl.BlockSpec(memory_space=pltpu.VMEM), pl.BlockSpec(memory_space=pl.ANY)

        def scratch(count):
            return [pltpu.VMEM((count, head_cols), BF16), pltpu.SemaphoreType.DMA]

        if g == order[-1]:
            out = call(
                attend_last_body,
                sds((tok, head_cols), BF16),
                "attend_last",
                (*args, window[order[-2]], window[order[0]], out),
                in_specs=[vmem] * (len(args) + 2) + [hbm],
                out_specs=hbm,
                scratch_shapes=[pltpu.VMEM((GROUP, head_cols), BF16), *scratch(last_rows)],
                input_output_aliases={len(args) + 2: 0},
            )
        elif g == order[-2]:
            window[g], out = call(
                attend_before_body,
                (piece, sds((tok, head_cols), BF16)),
                "attend_before",
                (*args, behind, *[window[at] for at in order[1:-2]]),
                (token,),
                out_specs=(vmem, hbm),
                scratch_shapes=scratch(tok - last_rows),
            )
            token = window[g]
        else:
            window[g] = token = call(attend_body, piece, "attend", args, (token,))
            if g == order[0]:
                behind = shifted(token, 1)

    a, b, c, d = order
    for step, g in (
        (feed, a), (rest, b), (add, a), (feed, b), (feed, c),
        (finish, a), (add, b), (add, c), (feed, d),
        (finish, b), (add, d), (attend, a),
        (finish, c), (attend, b),
        (finish, d), (attend, c), (attend, d),
    ):
        step(g)
    return out


def solution(mesh):
    return jax.shard_map(
        per_device,
        mesh=mesh,
        in_specs=(
            P("seq", "tp"),
            P("seq", "tp"),
            P("seq", None, None),
            P(None, "tp"),
            P("tp", None),
            P(None, "tp"),
            P(None, "tp"),
        ),
        out_specs=P("seq", "tp"),
        check_vma=False,
    )
```

```python
import functools

import jax
import jax.numpy as jnp
from jax import lax
from jax.experimental import pallas as pl
from jax.experimental.pallas import tpu as pltpu
from jax.sharding import PartitionSpec as P

HEAD_WIDTH = 128
GROUP = 64
LANES = 128
VMEM_LIMIT = 24 * 1024 * 1024
F32 = jnp.float32
BF16 = jnp.bfloat16


def call(body, outs, name, used, after=(), flops=1024, **extra):
    vmem = pl.BlockSpec(memory_space=pltpu.VMEM)
    unread = pl.BlockSpec(memory_space=pl.ANY)
    in_specs = extra.pop("in_specs", [vmem] * len(used))

    def without_after(*refs):
        body(*refs[: len(used)], *refs[len(used) + len(after) :])

    return pl.pallas_call(
        without_after,
        out_shape=outs,
        in_specs=in_specs + [unread] * len(after),
        compiler_params=pltpu.CompilerParams(vmem_limit_bytes=VMEM_LIMIT),
        cost_estimate=pl.CostEstimate(flops=flops, bytes_accessed=1024, transcendentals=0),
        name=name,
        **extra,
    )(*used, *after)


def exchange(x, bit):
    size = lax.axis_size("tp")
    return lax.ppermute(x, "tp", [(i, i ^ bit) for i in range(size)])


def shifted(x, by):
    length = lax.axis_size("seq")
    pairs = [(i, i + by) for i in range(length) if 0 <= i + by < length]
    return lax.ppermute(x, "seq", pairs)


def columns_of(row):
    return jnp.broadcast_to(row, (LANES, row.shape[1])).T


def one_hot(column, width):
    lane = lax.broadcasted_iota(jnp.int32, column.shape, 1)
    return jnp.concatenate(
        [jnp.where(column == lane + at, 1.0, 0.0).astype(BF16) for at in range(0, width, LANES)],
        axis=1,
    )


def route_body(voc, cap, ids_ref, wanted_ref, slot_ref):
    ids = ids_ref[...]
    count = ids.shape[1]
    owners = wanted_ref.shape[0]
    owner = lax.div(ids, jnp.int32(voc))
    local = ids - owner * voc
    hit = owner == lax.broadcasted_iota(jnp.int32, (owners, count), 0)
    hot = jnp.where(hit, 1.0, 0.0)
    upper = jnp.where(
        lax.broadcasted_iota(jnp.int32, (LANES, LANES), 0)
        <= lax.broadcasted_iota(jnp.int32, (LANES, LANES), 1),
        1.0,
        0.0,
    ).astype(BF16)
    carry = jnp.zeros((owners, 1), F32)
    ranks = []
    for at in range(0, count, LANES):
        part = hot[:, at : at + LANES]
        running = jnp.dot(part.astype(BF16), upper, preferred_element_type=F32) + carry
        ranks.append(jnp.sum(part * running, axis=0, keepdims=True))
        carry = running[:, LANES - 1 :]
    rank = jnp.concatenate(ranks, axis=1).astype(jnp.int32) - 1
    high = jnp.where(hit, lax.div(local, jnp.int32(256)), 0)
    low = jnp.where(hit, lax.rem(local, jnp.int32(256)), 0)
    digits = jnp.concatenate([high, low], axis=0).astype(F32).astype(BF16)
    place = jnp.where(
        rank == lax.broadcasted_iota(jnp.int32, (cap, count), 0), 1.0, 0.0
    ).astype(BF16)
    found = lax.dot_general(
        digits, place, (((1,), (1,)), ((), ())), preferred_element_type=F32
    ).astype(jnp.int32)
    wanted_ref[...] = found[:owners] * 256 + found[owners:]
    slot_ref[...] = columns_of(owner * cap + rank)


def fetch_body(req_ref, vocab_ref, queries_hbm, out_ref, head_ref, sem):
    copy = pltpu.make_async_copy(queries_hbm.at[pl.ds(0, head_ref.shape[0]), :], head_ref, sem)
    copy.start()
    step = 256
    table = vocab_ref[...]
    for at in range(0, req_ref.shape[1], step):
        picked = one_hot(columns_of(req_ref[:, at : at + step]), table.shape[0])
        out_ref[at : at + step, :] = jnp.dot(
            picked, table, preferred_element_type=F32
        ).astype(BF16)
    copy.wait()


def relay(x, after):
    unread = pl.BlockSpec(memory_space=pl.ANY)
    return pl.pallas_call(
        lambda *refs: None,
        out_shape=jax.ShapeDtypeStruct(x.shape, x.dtype),
        in_specs=[unread] * 2,
        out_specs=unread,
        input_output_aliases={0: 0},
        cost_estimate=pl.CostEstimate(flops=1024, bytes_accessed=1024, transcendentals=0),
        name="relay",
    )(x, after)


def pair_body(left_ref, right_ref, out_ref):
    width = left_ref.shape[1]
    out_ref[:, :width] = left_ref[...]
    out_ref[:, width:] = right_ref[...]


def order_body(groups, slot_ref, rows_ref, out_ref):
    rows = rows_ref[...]
    count = out_ref.shape[0] // len(groups)
    for at, g in enumerate(groups):
        picked = one_hot(slot_ref[g * count : (g + 1) * count, :], rows.shape[0])
        out_ref[at * count : (at + 1) * count, :] = jnp.dot(
            picked, rows, preferred_element_type=F32
        ).astype(BF16)


def block_rows(ref, index, width):
    return ref[pl.ds(pl.multiple_of(index * width, width), width), :]


def block_cols(ref, index, width):
    return ref[:, pl.ds(pl.multiple_of(index * width, width), width)]


def feed_body(first, e0_ref, e2_ref, other_ref, w_in_ref, w_out_ref, keep_ref, send_ref):
    me = lax.axis_index("tp")
    width = e0_ref.shape[1]
    index = [me, me ^ 2, me ^ 1, me ^ 3]
    here = slice(first, first + keep_ref.shape[0])
    parts = [e0_ref[here, :], e2_ref[here, :], other_ref[here, :width], other_ref[here, width:]]
    parts = [part.astype(F32) for part in parts]
    square = sum(jnp.sum(part * part, axis=1, keepdims=True) for part in parts)
    scale = lax.rsqrt(square / (4 * width) + 1e-06)
    hidden = sum(
        jnp.dot(
            (part * scale).astype(BF16), block_rows(w_in_ref, at, width), preferred_element_type=F32
        )
        for part, at in zip(parts, index)
    )
    inner = jax.nn.gelu(hidden, approximate=True).astype(BF16)
    for slot in range(2):
        cols = slice(slot * width, (slot + 1) * width)
        keep_ref[:, cols] = jnp.dot(
            inner, block_cols(w_out_ref, index[slot], width), preferred_element_type=F32
        )
        send_ref[:, cols] = jnp.dot(
            inner, block_cols(w_out_ref, index[2 + slot], width), preferred_element_type=F32
        ).astype(BF16)


def add_body(keep_ref, recv_ref, chip_ref, send_ref):
    chip = keep_ref[...] + recv_ref[...].astype(F32)
    chip_ref[...] = chip
    send_ref[...] = chip.astype(BF16)


def finish_body(first, e0_ref, e2_ref, chip_ref, far_ref, mine_ref):
    width = e0_ref.shape[1]
    near, past = slice(0, width), slice(width, 2 * width)
    here = slice(first, first + mine_ref.shape[0])
    mine_ref[:, near] = (
        e0_ref[here, :].astype(F32) + (chip_ref[:, near] + far_ref[:, past].astype(F32))
    ).astype(BF16)
    mine_ref[:, past] = (
        e2_ref[here, :].astype(F32) + (chip_ref[:, past] + far_ref[:, near].astype(F32))
    ).astype(BF16)


def attended(mine_ref, other_ref, w_key_ref, w_value_ref, q_ref):
    me = lax.axis_index("tp")
    width = mine_ref.shape[1] // 2
    parts = [
        (mine_ref[:, :width], me),
        (mine_ref[:, width:], me ^ 2),
        (other_ref[:, :width], me ^ 1),
        (other_ref[:, width:], me ^ 3),
    ]

    def project(w_ref):
        return sum(
            jnp.dot(part, block_rows(w_ref, at, width), preferred_element_type=F32)
            for part, at in parts
        ).astype(BF16)

    heads = [slice(at, at + HEAD_WIDTH) for at in range(0, q_ref.shape[1], HEAD_WIDTH)]
    keys = project(w_key_ref)
    weights = []
    for cols in heads:
        logits = lax.dot_general(
            q_ref[:, cols], keys[:, cols], (((1,), (1,)), ((), ())), preferred_element_type=F32
        ) * HEAD_WIDTH ** (-0.5)
        expo = jnp.exp(logits)
        weights.append((expo * (1.0 / jnp.sum(expo, axis=1, keepdims=True))).astype(BF16))
    values = project(w_value_ref)
    return [
        jnp.dot(weight, values[:, cols], preferred_element_type=F32)
        for weight, cols in zip(weights, heads)
    ]


def attend_body(mine_ref, other_ref, w_key_ref, w_value_ref, q_ref, out_ref):
    for at, part in enumerate(attended(mine_ref, other_ref, w_key_ref, w_value_ref, q_ref)):
        out_ref[:, at * HEAD_WIDTH : (at + 1) * HEAD_WIDTH] = part.astype(BF16)


def attend_last_body(
    mine_ref, other_ref, w_key_ref, w_value_ref, q_ref, behind_ref, *refs
):
    before, last_ref, out_ref = refs[:-2], refs[-2], refs[-1]
    parts = attended(mine_ref, other_ref, w_key_ref, w_value_ref, q_ref)
    for at, part in enumerate(parts):
        cols = slice(at * HEAD_WIDTH, (at + 1) * HEAD_WIDTH)
        part = part.astype(BF16).astype(F32)
        stack = [behind_ref[:, cols].astype(F32)]
        stack += [ref[:, cols].astype(F32) for ref in before]
        stack += [part, last_ref[:, cols].astype(F32)]
        tall = jnp.concatenate(stack, axis=0)
        moved = pltpu.roll(tall, tall.shape[0] - 1, 0)
        out_ref[:, cols] = moved[: out_ref.shape[0]].astype(BF16)


def per_device(queries, vocab_rows, neighbour_ids, w_in, w_out, w_key, w_value):
    seq_size = lax.axis_size("seq")
    groups, nbrs, nlen = neighbour_ids.shape
    per_group = nbrs * nlen
    rows = groups * per_group
    voc, width = vocab_rows.shape
    tok, head_cols = queries.shape
    cap = max(2, 2 * rows // seq_size)
    slots = seq_size * cap
    sds = jax.ShapeDtypeStruct

    wanted, slot = call(
        functools.partial(route_body, voc, cap),
        (sds((seq_size, cap), jnp.int32), sds((rows, LANES), jnp.int32)),
        "route",
        (neighbour_ids.reshape(1, rows),),
        flops=8 * 10**9,
    )
    request = lax.all_to_all(wanted, "seq", split_axis=0, concat_axis=0, tiled=True)
    vmem = pl.BlockSpec(memory_space=pltpu.VMEM)
    found, head = call(
        fetch_body,
        (sds((slots, width), BF16), sds((GROUP, head_cols), BF16)),
        "fetch",
        (request.reshape(1, slots), vocab_rows, queries),
        in_specs=[vmem, vmem, pl.BlockSpec(memory_space=pl.ANY)],
        scratch_shapes=[pltpu.SemaphoreType.DMA],
    )
    next_q = shifted(head, -1)
    answered = lax.all_to_all(
        found.reshape(seq_size, cap, width), "seq", split_axis=0, concat_axis=0, tiled=True
    ).reshape(slots, width)
    order = [groups - 1] + list(range(groups - 1))
    plan = [order[:1], order[1:]]
    first, window = {}, {}
    token = next_q
    pieces = []
    for part in plan:
        e0 = token = call(
            functools.partial(order_body, part),
            sds((len(part) * per_group, width), BF16),
            "order",
            (slot, answered),
            (token,),
        )
        pieces.append([e0, exchange(e0, 2), None])
        for at, g in enumerate(part):
            first[g] = at * per_group

    def across(piece, after=()):
        count = piece[0].shape[0]
        both = call(pair_body, sds((count, 2 * width), BF16), "pair", piece[:2], after)
        piece[2] = exchange(both, 1)

    across(pieces[0])
    local_q = jnp.concatenate([queries[GROUP - 1 :], next_q[: GROUP - 1]], axis=0)
    half = sds((per_group, 2 * width), BF16)
    whole = sds((per_group, 2 * width), F32)
    fed, summed, far, encoded = {}, {}, {}, {}
    behind = out = None

    def emb(g):
        return pieces[0 if g in plan[0] else 1]

    def rest(_):
        across(pieces[1], (token,))

    def feed(g):
        nonlocal token
        keep, token = call(
            functools.partial(feed_body, first[g]),
            (whole, half),
            "feed",
            (*emb(g), w_in, w_out),
            (token, pieces[1][1]),
        )
        fed[g] = keep, exchange(token, 1)

    def add(g):
        nonlocal token
        summed[g], token = call(add_body, (whole, half), "add", fed[g], (token,))
        far[g] = exchange(token, 2)

    def finish(g):
        nonlocal token
        token = call(
            functools.partial(finish_body, first[g]),
            half,
            "finish",
            (*emb(g)[:2], summed[g], far[g]),
            (token, behind) if g == order[-1] else (token,),
        )
        encoded[g] = token, None if g == order[0] else exchange(token, 1)

    def hand(g):
        mine = relay(encoded[g][0], token)
        encoded[g] = mine, exchange(mine, 1)

    def attend(g):
        nonlocal token, behind, out
        args = (*encoded[g], w_key, w_value, local_q[g * GROUP : (g + 1) * GROUP])
        if g == order[-1]:
            before = [window[at] for at in order[1:-1]]
            out = call(
                attend_last_body,
                sds((tok, head_cols), BF16),
                "attend_last",
                (*args, behind, *before, window[order[0]]),
            )
            return
        window[g] = token = call(
            attend_body, sds((GROUP, head_cols), BF16), "attend", args, (token,)
        )
        if g == order[0]:
            behind = shifted(token, 1)

    a, b, c, d = order
    for step, g in (
        (feed, a), (rest, b), (add, a), (feed, b), (feed, c),
        (finish, a), (add, b), (hand, a), (add, c), (feed, d), (attend, a),
        (finish, b), (add, d),
        (finish, c), (attend, b),
        (finish, d), (attend, c), (attend, d),
    ):
        step(g)
    return out


def solution(mesh):
    return jax.shard_map(
        per_device,
        mesh=mesh,
        in_specs=(
            P("seq", "tp"),
            P("seq", "tp"),
            P("seq", None, None),
            P(None, "tp"),
            P("tp", None),
            P(None, "tp"),
            P(None, "tp"),
        ),
        out_specs=P("seq", "tp"),
        check_vma=False,
    )
```

```python
import functools

import jax
import jax.numpy as jnp
from jax import lax
from jax.experimental import pallas as pl
from jax.experimental.pallas import tpu as pltpu
from jax.sharding import PartitionSpec as P

HEAD_WIDTH = 128
GROUP = 64
LANES = 128
VMEM_LIMIT = 24 * 1024 * 1024
F32 = jnp.float32
BF16 = jnp.bfloat16


def call(body, outs, name, used, after=(), flops=1024, **extra):
    vmem = pl.BlockSpec(memory_space=pltpu.VMEM)
    unread = pl.BlockSpec(memory_space=pl.ANY)
    in_specs = extra.pop("in_specs", [vmem] * len(used))

    def without_after(*refs):
        body(*refs[: len(used)], *refs[len(used) + len(after) :])

    return pl.pallas_call(
        without_after,
        out_shape=outs,
        in_specs=in_specs + [unread] * len(after),
        compiler_params=pltpu.CompilerParams(vmem_limit_bytes=VMEM_LIMIT),
        cost_estimate=pl.CostEstimate(flops=flops, bytes_accessed=1024, transcendentals=0),
        name=name,
        **extra,
    )(*used, *after)


def exchange(x, bit):
    size = lax.axis_size("tp")
    return lax.ppermute(x, "tp", [(i, i ^ bit) for i in range(size)])


def shifted(x, by):
    length = lax.axis_size("seq")
    pairs = [(i, i + by) for i in range(length) if 0 <= i + by < length]
    return lax.ppermute(x, "seq", pairs)


def columns_of(row):
    return jnp.broadcast_to(row, (LANES, row.shape[1])).T


def one_hot(column, width):
    lane = lax.broadcasted_iota(jnp.int32, column.shape, 1)
    return jnp.concatenate(
        [jnp.where(column == lane + at, 1.0, 0.0).astype(BF16) for at in range(0, width, LANES)],
        axis=1,
    )


def route_body(voc, cap, ids_ref, wanted_ref, slot_ref):
    ids = ids_ref[...]
    count = ids.shape[1]
    owners = wanted_ref.shape[0]
    owner = lax.div(ids, jnp.int32(voc))
    local = ids - owner * voc
    hit = owner == lax.broadcasted_iota(jnp.int32, (owners, count), 0)
    hot = jnp.where(hit, 1.0, 0.0)
    upper = jnp.where(
        lax.broadcasted_iota(jnp.int32, (LANES, LANES), 0)
        <= lax.broadcasted_iota(jnp.int32, (LANES, LANES), 1),
        1.0,
        0.0,
    ).astype(BF16)
    carry = jnp.zeros((owners, 1), F32)
    ranks = []
    for at in range(0, count, LANES):
        part = hot[:, at : at + LANES]
        running = jnp.dot(part.astype(BF16), upper, preferred_element_type=F32) + carry
        ranks.append(jnp.sum(part * running, axis=0, keepdims=True))
        carry = running[:, LANES - 1 :]
    rank = jnp.concatenate(ranks, axis=1).astype(jnp.int32) - 1
    high = jnp.where(hit, lax.div(local, jnp.int32(256)), 0)
    low = jnp.where(hit, lax.rem(local, jnp.int32(256)), 0)
    digits = jnp.concatenate([high, low], axis=0).astype(F32).astype(BF16)
    place = jnp.where(
        rank == lax.broadcasted_iota(jnp.int32, (cap, count), 0), 1.0, 0.0
    ).astype(BF16)
    found = lax.dot_general(
        digits, place, (((1,), (1,)), ((), ())), preferred_element_type=F32
    ).astype(jnp.int32)
    wanted_ref[...] = found[:owners] * 256 + found[owners:]
    slot_ref[...] = columns_of(owner * cap + rank)


def fetch_body(req_ref, vocab_ref, out_ref):
    step = 256
    table = vocab_ref[...]
    for at in range(0, req_ref.shape[1], step):
        picked = one_hot(columns_of(req_ref[:, at : at + step]), table.shape[0])
        out_ref[at : at + step, :] = jnp.dot(
            picked, table, preferred_element_type=F32
        ).astype(BF16)


def pair_body(left_ref, right_ref, out_ref):
    width = left_ref.shape[1]
    out_ref[:, :width] = left_ref[...]
    out_ref[:, width:] = right_ref[...]


def head_body(queries_ref, out_ref):
    out_ref[...] = queries_ref[: out_ref.shape[0], :]


def order_body(groups, slot_ref, rows_ref, out_ref):
    rows = rows_ref[...]
    count = out_ref.shape[0] // len(groups)
    for at, g in enumerate(groups):
        picked = one_hot(slot_ref[g * count : (g + 1) * count, :], rows.shape[0])
        out_ref[at * count : (at + 1) * count, :] = jnp.dot(
            picked, rows, preferred_element_type=F32
        ).astype(BF16)


def block_rows(ref, index, width):
    return ref[pl.ds(pl.multiple_of(index * width, width), width), :]


def block_cols(ref, index, width):
    return ref[:, pl.ds(pl.multiple_of(index * width, width), width)]


def feed_body(first, e0_ref, e2_ref, other_ref, w_in_ref, w_out_ref, keep_ref, send_ref):
    me = lax.axis_index("tp")
    width = e0_ref.shape[1]
    index = [me, me ^ 2, me ^ 1, me ^ 3]
    here = slice(first, first + keep_ref.shape[0])
    parts = [e0_ref[here, :], e2_ref[here, :], other_ref[here, :width], other_ref[here, width:]]
    parts = [part.astype(F32) for part in parts]
    square = sum(jnp.sum(part * part, axis=1, keepdims=True) for part in parts)
    scale = lax.rsqrt(square / (4 * width) + 1e-06)
    hidden = sum(
        jnp.dot(
            (part * scale).astype(BF16), block_rows(w_in_ref, at, width), preferred_element_type=F32
        )
        for part, at in zip(parts, index)
    )
    inner = jax.nn.gelu(hidden, approximate=True).astype(BF16)
    for slot in range(2):
        cols = slice(slot * width, (slot + 1) * width)
        keep_ref[:, cols] = jnp.dot(
            inner, block_cols(w_out_ref, index[slot], width), preferred_element_type=F32
        )
        send_ref[:, cols] = jnp.dot(
            inner, block_cols(w_out_ref, index[2 + slot], width), preferred_element_type=F32
        ).astype(BF16)


def add_body(keep_ref, recv_ref, chip_ref, send_ref):
    chip = keep_ref[...] + recv_ref[...].astype(F32)
    chip_ref[...] = chip
    send_ref[...] = chip.astype(BF16)


def finish_body(first, e0_ref, e2_ref, chip_ref, far_ref, mine_ref):
    width = e0_ref.shape[1]
    near, past = slice(0, width), slice(width, 2 * width)
    here = slice(first, first + mine_ref.shape[0])
    mine_ref[:, near] = (
        e0_ref[here, :].astype(F32) + (chip_ref[:, near] + far_ref[:, past].astype(F32))
    ).astype(BF16)
    mine_ref[:, past] = (
        e2_ref[here, :].astype(F32) + (chip_ref[:, past] + far_ref[:, near].astype(F32))
    ).astype(BF16)


def attended(mine_ref, other_ref, w_key_ref, w_value_ref, q_ref):
    me = lax.axis_index("tp")
    width = mine_ref.shape[1] // 2
    parts = [
        (mine_ref[:, :width], me),
        (mine_ref[:, width:], me ^ 2),
        (other_ref[:, :width], me ^ 1),
        (other_ref[:, width:], me ^ 3),
    ]

    def project(w_ref):
        return sum(
            jnp.dot(part, block_rows(w_ref, at, width), preferred_element_type=F32)
            for part, at in parts
        ).astype(BF16)

    heads = [slice(at, at + HEAD_WIDTH) for at in range(0, q_ref.shape[1], HEAD_WIDTH)]
    keys = project(w_key_ref)
    weights = []
    for cols in heads:
        logits = lax.dot_general(
            q_ref[:, cols], keys[:, cols], (((1,), (1,)), ((), ())), preferred_element_type=F32
        ) * HEAD_WIDTH ** (-0.5)
        expo = jnp.exp(logits)
        weights.append((expo * (1.0 / jnp.sum(expo, axis=1, keepdims=True))).astype(BF16))
    values = project(w_value_ref)
    return [
        jnp.dot(weight, values[:, cols], preferred_element_type=F32)
        for weight, cols in zip(weights, heads)
    ]


def attend_body(mine_ref, other_ref, w_key_ref, w_value_ref, q_ref, out_ref):
    for at, part in enumerate(attended(mine_ref, other_ref, w_key_ref, w_value_ref, q_ref)):
        out_ref[:, at * HEAD_WIDTH : (at + 1) * HEAD_WIDTH] = part.astype(BF16)


def attend_last_body(
    mine_ref, other_ref, w_key_ref, w_value_ref, q_ref, behind_ref, *refs
):
    before, last_ref, out_ref = refs[:-2], refs[-2], refs[-1]
    parts = attended(mine_ref, other_ref, w_key_ref, w_value_ref, q_ref)
    for at, part in enumerate(parts):
        cols = slice(at * HEAD_WIDTH, (at + 1) * HEAD_WIDTH)
        part = part.astype(BF16).astype(F32)
        stack = [behind_ref[:, cols].astype(F32)]
        stack += [ref[:, cols].astype(F32) for ref in before]
        stack += [part, last_ref[:, cols].astype(F32)]
        tall = jnp.concatenate(stack, axis=0)
        moved = pltpu.roll(tall, tall.shape[0] - 1, 0)
        out_ref[:, cols] = moved[: out_ref.shape[0]].astype(BF16)


def per_device(queries, vocab_rows, neighbour_ids, w_in, w_out, w_key, w_value):
    seq_size = lax.axis_size("seq")
    groups, nbrs, nlen = neighbour_ids.shape
    per_group = nbrs * nlen
    rows = groups * per_group
    voc, width = vocab_rows.shape
    tok, head_cols = queries.shape
    cap = max(2, 2 * rows // seq_size)
    slots = seq_size * cap
    sds = jax.ShapeDtypeStruct

    wanted, slot = call(
        functools.partial(route_body, voc, cap),
        (sds((seq_size, cap), jnp.int32), sds((rows, LANES), jnp.int32)),
        "route",
        (neighbour_ids.reshape(1, rows),),
        flops=8 * 10**9,
    )
    request = lax.all_to_all(wanted, "seq", split_axis=0, concat_axis=0, tiled=True)
    found = call(
        fetch_body,
        sds((slots, width), BF16),
        "fetch",
        (request.reshape(1, slots), vocab_rows),
    )
    answered = lax.all_to_all(
        found.reshape(seq_size, cap, width), "seq", split_axis=0, concat_axis=0, tiled=True
    ).reshape(slots, width)
    order = [groups - 1] + list(range(groups - 1))
    plan = [order[:1], order[1:]]
    first, window = {}, {}
    token = slot
    pieces = []
    for part in plan:
        e0 = token = call(
            functools.partial(order_body, part),
            sds((len(part) * per_group, width), BF16),
            "order",
            (slot, answered),
            (token,),
        )
        pieces.append([e0, exchange(e0, 2), None])
        for at, g in enumerate(part):
            first[g] = at * per_group

    def across(piece, after=()):
        count = piece[0].shape[0]
        both = call(pair_body, sds((count, 2 * width), BF16), "pair", piece[:2], after)
        piece[2] = exchange(both, 1)

    across(pieces[0])
    head = call(head_body, sds((GROUP, head_cols), BF16), "head", (queries,), (token,))
    next_q = shifted(head, -1)
    local_q = jnp.concatenate([queries[GROUP - 1 :], next_q[: GROUP - 1]], axis=0)
    half = sds((per_group, 2 * width), BF16)
    whole = sds((per_group, 2 * width), F32)
    fed, summed, far, encoded = {}, {}, {}, {}
    behind = out = None

    def emb(g):
        return pieces[0 if g in plan[0] else 1]

    def rest(_):
        across(pieces[1], (token,))

    def feed(g):
        nonlocal token
        keep, token = call(
            functools.partial(feed_body, first[g]),
            (whole, half),
            "feed",
            (*emb(g), w_in, w_out),
            (token, pieces[1][1], next_q),
        )
        fed[g] = keep, exchange(token, 1)

    def add(g):
        nonlocal token
        summed[g], token = call(add_body, (whole, half), "add", fed[g], (token,))
        far[g] = exchange(token, 2)

    def finish(g):
        nonlocal token
        token = call(
            functools.partial(finish_body, first[g]),
            half,
            "finish",
            (*emb(g)[:2], summed[g], far[g]),
            (token, behind) if g == order[-1] else (token,),
        )
        encoded[g] = token, exchange(token, 1)

    def attend(g):
        nonlocal token, behind, out
        args = (*encoded[g], w_key, w_value, local_q[g * GROUP : (g + 1) * GROUP])
        if g == order[-1]:
            before = [window[at] for at in order[1:-1]]
            out = call(
                attend_last_body,
                sds((tok, head_cols), BF16),
                "attend_last",
                (*args, behind, *before, window[order[0]]),
            )
            return
        window[g] = token = call(
            attend_body, sds((GROUP, head_cols), BF16), "attend", args, (token,)
        )
        if g == order[0]:
            behind = shifted(token, 1)

    a, b, c, d = order
    for step, g in (
        (feed, a), (rest, b), (feed, b), (add, a), (feed, c), (add, b),
        (finish, a), (feed, d), (add, c),
        (finish, b), (attend, a), (add, d),
        (finish, c), (attend, b),
        (finish, d), (attend, c), (attend, d),
    ):
        step(g)
    return out


def solution(mesh):
    return jax.shard_map(
        per_device,
        mesh=mesh,
        in_specs=(
            P("seq", "tp"),
            P("seq", "tp"),
            P("seq", None, None),
            P(None, "tp"),
            P("tp", None),
            P(None, "tp"),
            P(None, "tp"),
        ),
        out_specs=P("seq", "tp"),
        check_vma=False,
    )
```

```python
import functools

import jax
import jax.numpy as jnp
from jax import lax
from jax.experimental import pallas as pl
from jax.experimental.pallas import tpu as pltpu
from jax.sharding import PartitionSpec as P

HEAD_WIDTH = 128
GROUP = 64
LANES = 128
VMEM_LIMIT = 24 * 1024 * 1024
F32 = jnp.float32
BF16 = jnp.bfloat16


def call(body, outs, name, used, after=(), flops=1024, **extra):
    vmem = pl.BlockSpec(memory_space=pltpu.VMEM)
    unread = pl.BlockSpec(memory_space=pl.ANY)
    in_specs = extra.pop("in_specs", [vmem] * len(used))

    def without_after(*refs):
        body(*refs[: len(used)], *refs[len(used) + len(after) :])

    return pl.pallas_call(
        without_after,
        out_shape=outs,
        in_specs=in_specs + [unread] * len(after),
        compiler_params=pltpu.CompilerParams(vmem_limit_bytes=VMEM_LIMIT),
        cost_estimate=pl.CostEstimate(flops=flops, bytes_accessed=1024, transcendentals=0),
        name=name,
        **extra,
    )(*used, *after)


def exchange(x, bit):
    size = lax.axis_size("tp")
    return lax.ppermute(x, "tp", [(i, i ^ bit) for i in range(size)])


def shifted(x, by):
    length = lax.axis_size("seq")
    pairs = [(i, i + by) for i in range(length) if 0 <= i + by < length]
    return lax.ppermute(x, "seq", pairs)


def columns_of(row):
    return jnp.broadcast_to(row, (LANES, row.shape[1])).T


def one_hot(column, width):
    lane = lax.broadcasted_iota(jnp.int32, column.shape, 1)
    return jnp.concatenate(
        [jnp.where(column == lane + at, 1.0, 0.0).astype(BF16) for at in range(0, width, LANES)],
        axis=1,
    )


def route_body(voc, cap, ids_ref, wanted_ref, slot_ref):
    ids = ids_ref[...]
    count = ids.shape[1]
    owners = wanted_ref.shape[0]
    owner = lax.div(ids, jnp.int32(voc))
    local = ids - owner * voc
    hit = owner == lax.broadcasted_iota(jnp.int32, (owners, count), 0)
    hot = jnp.where(hit, 1.0, 0.0)
    upper = jnp.where(
        lax.broadcasted_iota(jnp.int32, (LANES, LANES), 0)
        <= lax.broadcasted_iota(jnp.int32, (LANES, LANES), 1),
        1.0,
        0.0,
    ).astype(BF16)
    carry = jnp.zeros((owners, 1), F32)
    ranks = []
    for at in range(0, count, LANES):
        part = hot[:, at : at + LANES]
        running = jnp.dot(part.astype(BF16), upper, preferred_element_type=F32) + carry
        ranks.append(jnp.sum(part * running, axis=0, keepdims=True))
        carry = running[:, LANES - 1 :]
    rank = jnp.concatenate(ranks, axis=1).astype(jnp.int32) - 1
    high = jnp.where(hit, lax.div(local, jnp.int32(256)), 0)
    low = jnp.where(hit, lax.rem(local, jnp.int32(256)), 0)
    digits = jnp.concatenate([high, low], axis=0).astype(F32).astype(BF16)
    place = jnp.where(
        rank == lax.broadcasted_iota(jnp.int32, (cap, count), 0), 1.0, 0.0
    ).astype(BF16)
    found = lax.dot_general(
        digits, place, (((1,), (1,)), ((), ())), preferred_element_type=F32
    ).astype(jnp.int32)
    wanted_ref[...] = found[:owners] * 256 + found[owners:]
    slot_ref[...] = columns_of(owner * cap + rank)


def fetch_body(req_ref, vocab_ref, out_ref):
    step = 256
    table = vocab_ref[...]
    for at in range(0, req_ref.shape[1], step):
        picked = one_hot(columns_of(req_ref[:, at : at + step]), table.shape[0])
        out_ref[at : at + step, :] = jnp.dot(
            picked, table, preferred_element_type=F32
        ).astype(BF16)


def pair_body(left_ref, right_ref, out_ref):
    width = left_ref.shape[1]
    out_ref[:, :width] = left_ref[...]
    out_ref[:, width:] = right_ref[...]


def head_body(queries_ref, out_ref):
    out_ref[...] = queries_ref[: out_ref.shape[0], :]


def order_body(groups, slot_ref, rows_ref, out_ref):
    rows = rows_ref[...]
    count = out_ref.shape[0] // len(groups)
    for at, g in enumerate(groups):
        picked = one_hot(slot_ref[g * count : (g + 1) * count, :], rows.shape[0])
        out_ref[at * count : (at + 1) * count, :] = jnp.dot(
            picked, rows, preferred_element_type=F32
        ).astype(BF16)


def block_rows(ref, index, width):
    return ref[pl.ds(pl.multiple_of(index * width, width), width), :]


def block_cols(ref, index, width):
    return ref[:, pl.ds(pl.multiple_of(index * width, width), width)]


def feed_body(first, e0_ref, e2_ref, other_ref, w_in_ref, w_out_ref, keep_ref, send_ref):
    me = lax.axis_index("tp")
    width = e0_ref.shape[1]
    index = [me, me ^ 2, me ^ 1, me ^ 3]
    here = slice(first, first + keep_ref.shape[0])
    parts = [e0_ref[here, :], e2_ref[here, :], other_ref[here, :width], other_ref[here, width:]]
    parts = [part.astype(F32) for part in parts]
    square = sum(jnp.sum(part * part, axis=1, keepdims=True) for part in parts)
    scale = lax.rsqrt(square / (4 * width) + 1e-06)
    hidden = sum(
        jnp.dot(
            (part * scale).astype(BF16), block_rows(w_in_ref, at, width), preferred_element_type=F32
        )
        for part, at in zip(parts, index)
    )
    inner = jax.nn.gelu(hidden, approximate=True).astype(BF16)
    for slot in range(2):
        cols = slice(slot * width, (slot + 1) * width)
        keep_ref[:, cols] = jnp.dot(
            inner, block_cols(w_out_ref, index[slot], width), preferred_element_type=F32
        )
        send_ref[:, cols] = jnp.dot(
            inner, block_cols(w_out_ref, index[2 + slot], width), preferred_element_type=F32
        ).astype(BF16)


def add_body(keep_ref, recv_ref, chip_ref, send_ref):
    chip = keep_ref[...] + recv_ref[...].astype(F32)
    chip_ref[...] = chip
    send_ref[...] = chip.astype(BF16)


def finish_body(first, e0_ref, e2_ref, chip_ref, far_ref, mine_ref):
    width = e0_ref.shape[1]
    near, past = slice(0, width), slice(width, 2 * width)
    here = slice(first, first + mine_ref.shape[0])
    mine_ref[:, near] = (
        e0_ref[here, :].astype(F32) + (chip_ref[:, near] + far_ref[:, past].astype(F32))
    ).astype(BF16)
    mine_ref[:, past] = (
        e2_ref[here, :].astype(F32) + (chip_ref[:, past] + far_ref[:, near].astype(F32))
    ).astype(BF16)


def attended(mine_ref, other_ref, w_key_ref, w_value_ref, q_ref):
    me = lax.axis_index("tp")
    width = mine_ref.shape[1] // 2
    parts = [
        (mine_ref[:, :width], me),
        (mine_ref[:, width:], me ^ 2),
        (other_ref[:, :width], me ^ 1),
        (other_ref[:, width:], me ^ 3),
    ]

    def project(w_ref):
        return sum(
            jnp.dot(part, block_rows(w_ref, at, width), preferred_element_type=F32)
            for part, at in parts
        ).astype(BF16)

    heads = [slice(at, at + HEAD_WIDTH) for at in range(0, q_ref.shape[1], HEAD_WIDTH)]
    keys = project(w_key_ref)
    weights = []
    for cols in heads:
        logits = lax.dot_general(
            q_ref[:, cols], keys[:, cols], (((1,), (1,)), ((), ())), preferred_element_type=F32
        ) * HEAD_WIDTH ** (-0.5)
        expo = jnp.exp(logits)
        weights.append((expo * (1.0 / jnp.sum(expo, axis=1, keepdims=True))).astype(BF16))
    values = project(w_value_ref)
    return [
        jnp.dot(weight, values[:, cols], preferred_element_type=F32)
        for weight, cols in zip(weights, heads)
    ]


def attend_body(mine_ref, other_ref, w_key_ref, w_value_ref, q_ref, out_ref):
    for at, part in enumerate(attended(mine_ref, other_ref, w_key_ref, w_value_ref, q_ref)):
        out_ref[:, at * HEAD_WIDTH : (at + 1) * HEAD_WIDTH] = part.astype(BF16)


def attend_last_body(
    mine_ref, other_ref, w_key_ref, w_value_ref, q_ref, behind_ref, *refs
):
    before, last_ref, out_ref = refs[:-2], refs[-2], refs[-1]
    parts = attended(mine_ref, other_ref, w_key_ref, w_value_ref, q_ref)
    for at, part in enumerate(parts):
        cols = slice(at * HEAD_WIDTH, (at + 1) * HEAD_WIDTH)
        part = part.astype(BF16).astype(F32)
        stack = [behind_ref[:, cols].astype(F32)]
        stack += [ref[:, cols].astype(F32) for ref in before]
        stack += [part, last_ref[:, cols].astype(F32)]
        tall = jnp.concatenate(stack, axis=0)
        moved = pltpu.roll(tall, tall.shape[0] - 1, 0)
        out_ref[:, cols] = moved[: out_ref.shape[0]].astype(BF16)


def per_device(queries, vocab_rows, neighbour_ids, w_in, w_out, w_key, w_value):
    seq_size = lax.axis_size("seq")
    groups, nbrs, nlen = neighbour_ids.shape
    per_group = nbrs * nlen
    rows = groups * per_group
    voc, width = vocab_rows.shape
    tok, head_cols = queries.shape
    cap = max(2, 2 * rows // seq_size)
    slots = seq_size * cap
    sds = jax.ShapeDtypeStruct

    wanted, slot = call(
        functools.partial(route_body, voc, cap),
        (sds((seq_size, cap), jnp.int32), sds((rows, LANES), jnp.int32)),
        "route",
        (neighbour_ids.reshape(1, rows),),
        flops=8 * 10**9,
    )
    request = lax.all_to_all(wanted, "seq", split_axis=0, concat_axis=0, tiled=True)
    found = call(
        fetch_body,
        sds((slots, width), BF16),
        "fetch",
        (request.reshape(1, slots), vocab_rows),
    )
    answered = lax.all_to_all(
        found.reshape(seq_size, cap, width), "seq", split_axis=0, concat_axis=0, tiled=True
    ).reshape(slots, width)
    order = [groups - 1] + list(range(groups - 1))
    plan = [order[:1], order[1:]]
    first, window = {}, {}
    token = slot
    pieces = []
    for part in plan:
        e0 = token = call(
            functools.partial(order_body, part),
            sds((len(part) * per_group, width), BF16),
            "order",
            (slot, answered),
            (token,),
        )
        pieces.append([e0, exchange(e0, 2), None])
        for at, g in enumerate(part):
            first[g] = at * per_group

    def across(piece, after=()):
        count = piece[0].shape[0]
        both = call(pair_body, sds((count, 2 * width), BF16), "pair", piece[:2], after)
        piece[2] = exchange(both, 1)
        return both

    across(pieces[0], (token,))
    head = call(head_body, sds((GROUP, head_cols), BF16), "head", (queries,), (token,))
    next_q = shifted(head, -1)
    local_q = jnp.concatenate([queries[GROUP - 1 :], next_q[: GROUP - 1]], axis=0)
    half = sds((per_group, 2 * width), BF16)
    whole = sds((per_group, 2 * width), F32)
    fed, summed, far, encoded = {}, {}, {}, {}
    behind = out = None

    def emb(g):
        return pieces[0 if g in plan[0] else 1]

    def rest(_):
        nonlocal token
        token = across(pieces[1], (token, next_q))

    def feed(g):
        nonlocal token
        keep, token = call(
            functools.partial(feed_body, first[g]),
            (whole, half),
            "feed",
            (*emb(g), w_in, w_out),
            (token,),
        )
        fed[g] = keep, exchange(token, 1)

    def add(g):
        nonlocal token
        summed[g], token = call(add_body, (whole, half), "add", fed[g], (token,))
        far[g] = exchange(token, 2)

    def finish(g):
        nonlocal token
        token = call(
            functools.partial(finish_body, first[g]),
            half,
            "finish",
            (*emb(g)[:2], summed[g], far[g]),
            (token, behind) if g == order[-1] else (token,),
        )
        encoded[g] = token, exchange(token, 1)

    def attend(g):
        nonlocal token, behind, out
        args = (*encoded[g], w_key, w_value, local_q[g * GROUP : (g + 1) * GROUP])
        if g == order[-1]:
            before = [window[at] for at in order[1:-1]]
            out = call(
                attend_last_body,
                sds((tok, head_cols), BF16),
                "attend_last",
                (*args, behind, *before, window[order[0]]),
            )
            return
        window[g] = token = call(
            attend_body, sds((GROUP, head_cols), BF16), "attend", args, (token,)
        )
        if g == order[0]:
            behind = shifted(token, 1)

    a, b, c, d = order
    for step, g in (
        (feed, a), (add, a), (rest, b), (feed, b), (feed, c),
        (finish, a), (add, b), (add, c), (feed, d),
        (finish, b), (add, d), (attend, a),
        (finish, c), (attend, b),
        (finish, d), (attend, c), (attend, d),
    ):
        step(g)
    return out


def solution(mesh):
    return jax.shard_map(
        per_device,
        mesh=mesh,
        in_specs=(
            P("seq", "tp"),
            P("seq", "tp"),
            P("seq", None, None),
            P(None, "tp"),
            P("tp", None),
            P(None, "tp"),
            P(None, "tp"),
        ),
        out_specs=P("seq", "tp"),
        check_vma=False,
    )
```

```python
import functools

import jax
import jax.numpy as jnp
from jax import lax
from jax.experimental import pallas as pl
from jax.experimental.pallas import tpu as pltpu
from jax.sharding import PartitionSpec as P

HEAD_WIDTH = 128
GROUP = 64
LANES = 128
VMEM_LIMIT = 24 * 1024 * 1024
F32 = jnp.float32
BF16 = jnp.bfloat16


def call(body, outs, name, used, after=(), flops=1024, **extra):
    vmem = pl.BlockSpec(memory_space=pltpu.VMEM)
    unread = pl.BlockSpec(memory_space=pl.ANY)
    in_specs = extra.pop("in_specs", [vmem] * len(used))

    def without_after(*refs):
        body(*refs[: len(used)], *refs[len(used) + len(after) :])

    return pl.pallas_call(
        without_after,
        out_shape=outs,
        in_specs=in_specs + [unread] * len(after),
        compiler_params=pltpu.CompilerParams(vmem_limit_bytes=VMEM_LIMIT),
        cost_estimate=pl.CostEstimate(flops=flops, bytes_accessed=1024, transcendentals=0),
        name=name,
        **extra,
    )(*used, *after)


def exchange(x, bit):
    size = lax.axis_size("tp")
    return lax.ppermute(x, "tp", [(i, i ^ bit) for i in range(size)])


def shifted(x, by):
    length = lax.axis_size("seq")
    pairs = [(i, i + by) for i in range(length) if 0 <= i + by < length]
    return lax.ppermute(x, "seq", pairs)


def columns_of(row):
    return jnp.broadcast_to(row, (LANES, row.shape[1])).T


def one_hot(column, width):
    lane = lax.broadcasted_iota(jnp.int32, column.shape, 1)
    return jnp.concatenate(
        [jnp.where(column == lane + at, 1.0, 0.0).astype(BF16) for at in range(0, width, LANES)],
        axis=1,
    )


def route_body(voc, cap, ids_ref, wanted_ref, slot_ref):
    ids = ids_ref[...]
    count = ids.shape[1]
    owners = wanted_ref.shape[0]
    owner = lax.div(ids, jnp.int32(voc))
    local = ids - owner * voc
    hit = owner == lax.broadcasted_iota(jnp.int32, (owners, count), 0)
    hot = jnp.where(hit, 1.0, 0.0)
    upper = jnp.where(
        lax.broadcasted_iota(jnp.int32, (LANES, LANES), 0)
        <= lax.broadcasted_iota(jnp.int32, (LANES, LANES), 1),
        1.0,
        0.0,
    ).astype(BF16)
    carry = jnp.zeros((owners, 1), F32)
    ranks = []
    for at in range(0, count, LANES):
        part = hot[:, at : at + LANES]
        running = jnp.dot(part.astype(BF16), upper, preferred_element_type=F32) + carry
        ranks.append(jnp.sum(part * running, axis=0, keepdims=True))
        carry = running[:, LANES - 1 :]
    rank = jnp.concatenate(ranks, axis=1).astype(jnp.int32) - 1
    high = jnp.where(hit, lax.div(local, jnp.int32(256)), 0)
    low = jnp.where(hit, lax.rem(local, jnp.int32(256)), 0)
    digits = jnp.concatenate([high, low], axis=0).astype(F32).astype(BF16)
    place = jnp.where(
        rank == lax.broadcasted_iota(jnp.int32, (cap, count), 0), 1.0, 0.0
    ).astype(BF16)
    found = lax.dot_general(
        digits, place, (((1,), (1,)), ((), ())), preferred_element_type=F32
    ).astype(jnp.int32)
    wanted_ref[...] = found[:owners] * 256 + found[owners:]
    slot_ref[...] = columns_of(owner * cap + rank)


def fetch_body(req_ref, vocab_ref, out_ref):
    step = 256
    table = vocab_ref[...]
    for at in range(0, req_ref.shape[1], step):
        picked = one_hot(columns_of(req_ref[:, at : at + step]), table.shape[0])
        out_ref[at : at + step, :] = jnp.dot(
            picked, table, preferred_element_type=F32
        ).astype(BF16)


def mark_body(out_ref):
    out_ref[...] = jnp.zeros_like(out_ref)


def pair_body(left_ref, right_ref, out_ref):
    width = left_ref.shape[1]
    out_ref[:, :width] = left_ref[...]
    out_ref[:, width:] = right_ref[...]


def head_body(queries_ref, out_ref):
    out_ref[...] = queries_ref[: out_ref.shape[0], :]


def order_body(groups, slot_ref, rows_ref, out_ref):
    rows = rows_ref[...]
    count = out_ref.shape[0] // len(groups)
    for at, g in enumerate(groups):
        picked = one_hot(slot_ref[g * count : (g + 1) * count, :], rows.shape[0])
        out_ref[at * count : (at + 1) * count, :] = jnp.dot(
            picked, rows, preferred_element_type=F32
        ).astype(BF16)


def block_rows(ref, index, width):
    return ref[pl.ds(pl.multiple_of(index * width, width), width), :]


def block_cols(ref, index, width):
    return ref[:, pl.ds(pl.multiple_of(index * width, width), width)]


def feed_body(first, e0_ref, e2_ref, other_ref, w_in_ref, w_out_ref, keep_ref, send_ref):
    me = lax.axis_index("tp")
    width = e0_ref.shape[1]
    index = [me, me ^ 2, me ^ 1, me ^ 3]
    here = slice(first, first + keep_ref.shape[0])
    parts = [e0_ref[here, :], e2_ref[here, :], other_ref[here, :width], other_ref[here, width:]]
    parts = [part.astype(F32) for part in parts]
    square = sum(jnp.sum(part * part, axis=1, keepdims=True) for part in parts)
    scale = lax.rsqrt(square / (4 * width) + 1e-06)
    hidden = sum(
        jnp.dot(
            (part * scale).astype(BF16), block_rows(w_in_ref, at, width), preferred_element_type=F32
        )
        for part, at in zip(parts, index)
    )
    inner = jax.nn.gelu(hidden, approximate=True).astype(BF16)
    for slot in range(2):
        cols = slice(slot * width, (slot + 1) * width)
        keep_ref[:, cols] = jnp.dot(
            inner, block_cols(w_out_ref, index[slot], width), preferred_element_type=F32
        )
        send_ref[:, cols] = jnp.dot(
            inner, block_cols(w_out_ref, index[2 + slot], width), preferred_element_type=F32
        ).astype(BF16)


def add_body(keep_ref, recv_ref, chip_ref, send_ref):
    chip = keep_ref[...] + recv_ref[...].astype(F32)
    chip_ref[...] = chip
    send_ref[...] = chip.astype(BF16)


def finish_body(first, e0_ref, e2_ref, chip_ref, far_ref, mine_ref):
    width = e0_ref.shape[1]
    near, past = slice(0, width), slice(width, 2 * width)
    here = slice(first, first + mine_ref.shape[0])
    mine_ref[:, near] = (
        e0_ref[here, :].astype(F32) + (chip_ref[:, near] + far_ref[:, past].astype(F32))
    ).astype(BF16)
    mine_ref[:, past] = (
        e2_ref[here, :].astype(F32) + (chip_ref[:, past] + far_ref[:, near].astype(F32))
    ).astype(BF16)


def attended(mine_ref, other_ref, w_key_ref, w_value_ref, q_ref):
    me = lax.axis_index("tp")
    width = mine_ref.shape[1] // 2
    parts = [
        (mine_ref[:, :width], me),
        (mine_ref[:, width:], me ^ 2),
        (other_ref[:, :width], me ^ 1),
        (other_ref[:, width:], me ^ 3),
    ]

    def project(w_ref):
        return sum(
            jnp.dot(part, block_rows(w_ref, at, width), preferred_element_type=F32)
            for part, at in parts
        ).astype(BF16)

    heads = [slice(at, at + HEAD_WIDTH) for at in range(0, q_ref.shape[1], HEAD_WIDTH)]
    keys = project(w_key_ref)
    weights = []
    for cols in heads:
        logits = lax.dot_general(
            q_ref[:, cols], keys[:, cols], (((1,), (1,)), ((), ())), preferred_element_type=F32
        ) * HEAD_WIDTH ** (-0.5)
        expo = jnp.exp(logits)
        weights.append((expo * (1.0 / jnp.sum(expo, axis=1, keepdims=True))).astype(BF16))
    values = project(w_value_ref)
    return [
        jnp.dot(weight, values[:, cols], preferred_element_type=F32)
        for weight, cols in zip(weights, heads)
    ]


def attend_body(mine_ref, other_ref, w_key_ref, w_value_ref, q_ref, out_ref):
    for at, part in enumerate(attended(mine_ref, other_ref, w_key_ref, w_value_ref, q_ref)):
        out_ref[:, at * HEAD_WIDTH : (at + 1) * HEAD_WIDTH] = part.astype(BF16)


def attend_first_body(
    mine_ref, other_ref, w_key_ref, w_value_ref, queries_ref, next_ref, out_ref, q_ref
):
    edge = 16
    for at in range(0, q_ref.shape[1], HEAD_WIDTH):
        cols = slice(at, at + HEAD_WIDTH)
        tall = jnp.concatenate(
            [queries_ref[-edge:, cols].astype(F32), next_ref[:, cols].astype(F32)], axis=0
        )
        moved = pltpu.roll(tall, tall.shape[0] - edge + 1, 0)
        q_ref[:, cols] = moved[: q_ref.shape[0]].astype(BF16)
    attend_body(mine_ref, other_ref, w_key_ref, w_value_ref, q_ref, out_ref)


def attend_last_body(
    mine_ref, other_ref, w_key_ref, w_value_ref, q_ref, behind_ref, *refs
):
    before, last_ref, out_ref = refs[:-2], refs[-2], refs[-1]
    parts = attended(mine_ref, other_ref, w_key_ref, w_value_ref, q_ref)
    for at, part in enumerate(parts):
        cols = slice(at * HEAD_WIDTH, (at + 1) * HEAD_WIDTH)
        part = part.astype(BF16).astype(F32)
        stack = [behind_ref[:, cols].astype(F32)]
        stack += [ref[:, cols].astype(F32) for ref in before]
        stack += [part, last_ref[:, cols].astype(F32)]
        tall = jnp.concatenate(stack, axis=0)
        moved = pltpu.roll(tall, tall.shape[0] - 1, 0)
        out_ref[:, cols] = moved[: out_ref.shape[0]].astype(BF16)


def per_device(queries, vocab_rows, neighbour_ids, w_in, w_out, w_key, w_value):
    seq_size = lax.axis_size("seq")
    groups, nbrs, nlen = neighbour_ids.shape
    per_group = nbrs * nlen
    rows = groups * per_group
    voc, width = vocab_rows.shape
    tok, head_cols = queries.shape
    cap = max(2, 2 * rows // seq_size)
    slots = seq_size * cap
    sds = jax.ShapeDtypeStruct

    wanted, slot = call(
        functools.partial(route_body, voc, cap),
        (sds((seq_size, cap), jnp.int32), sds((rows, LANES), jnp.int32)),
        "route",
        (neighbour_ids.reshape(1, rows),),
        flops=8 * 10**9,
    )
    request = lax.all_to_all(wanted, "seq", split_axis=0, concat_axis=0, tiled=True)
    found = call(
        fetch_body,
        sds((slots, width), BF16),
        "fetch",
        (request.reshape(1, slots), vocab_rows),
    )
    answered = lax.all_to_all(
        found.reshape(seq_size, cap, width), "seq", split_axis=0, concat_axis=0, tiled=True
    ).reshape(slots, width)
    order = [groups - 1] + list(range(groups - 1))
    plan = [order[:2], order[2:]]
    first, window = {}, {}
    token = slot
    pieces = []
    for part in plan:
        e0 = token = call(
            functools.partial(order_body, part),
            sds((len(part) * per_group, width), BF16),
            "order",
            (slot, answered),
            (token,),
        )
        pieces.append([e0, exchange(e0, 2), None])
        for at, g in enumerate(part):
            first[g] = at * per_group

    def across(piece, after=()):
        count = piece[0].shape[0]
        both = call(pair_body, sds((count, 2 * width), BF16), "pair", piece[:2], after)
        piece[2] = exchange(both, 1)
        return both

    across(pieces[0], (token,))
    head = call(head_body, sds((GROUP, head_cols), BF16), "head", (queries,), (token,))
    next_q = shifted(head, -1)
    half = sds((per_group, 2 * width), BF16)
    whole = sds((per_group, 2 * width), F32)
    fed, summed, far, encoded = {}, {}, {}, {}
    behind = out = None

    def emb(g):
        return pieces[0 if g in plan[0] else 1]

    def rest(_):
        nonlocal token
        token = across(pieces[1], (token,))

    def pause(_):
        nonlocal token
        token = call(mark_body, sds((8, LANES), F32), "mark", (), (token, pieces[1][1]))

    def feed(g):
        nonlocal token
        keep, token = call(
            functools.partial(feed_body, first[g]),
            (whole, half),
            "feed",
            (*emb(g), w_in, w_out),
            (token,),
        )
        fed[g] = keep, exchange(token, 1)

    def add(g):
        nonlocal token
        summed[g], token = call(add_body, (whole, half), "add", fed[g], (token,))
        far[g] = exchange(token, 2)

    def finish(g):
        nonlocal token
        token = call(
            functools.partial(finish_body, first[g]),
            half,
            "finish",
            (*emb(g)[:2], summed[g], far[g]),
            (token, behind) if g == order[-1] else (token,),
        )
        encoded[g] = token, exchange(token, 1)

    def attend(g):
        nonlocal token, behind, out
        start = (g + 1) * GROUP - 1
        args = (*encoded[g], w_key, w_value)
        if g == order[0]:
            window[g] = token = call(
                attend_first_body,
                sds((GROUP, head_cols), BF16),
                "attend_first",
                (*args, queries, next_q),
                (token,),
                scratch_shapes=[pltpu.VMEM((GROUP, head_cols), BF16)],
            )
            behind = shifted(token, 1)
            return
        args += (queries[start : start + GROUP],)
        if g == order[-1]:
            before = [window[at] for at in order[1:-1]]
            out = call(
                attend_last_body,
                sds((tok, head_cols), BF16),
                "attend_last",
                (*args, behind, *before, window[order[0]]),
            )
            return
        window[g] = token = call(
            attend_body, sds((GROUP, head_cols), BF16), "attend", args, (token,)
        )

    a, b, c, d = order
    for step, g in (
        (feed, a), (feed, b), (pause, c), (add, a), (rest, c), (feed, c), (add, b),
        (finish, a), (feed, d), (add, c), (attend, a),
        (finish, b), (add, d),
        (finish, c), (attend, b),
        (finish, d), (attend, c), (attend, d),
    ):
        step(g)
    return out


def solution(mesh):
    return jax.shard_map(
        per_device,
        mesh=mesh,
        in_specs=(
            P("seq", "tp"),
            P("seq", "tp"),
            P("seq", None, None),
            P(None, "tp"),
            P("tp", None),
            P(None, "tp"),
            P(None, "tp"),
        ),
        out_specs=P("seq", "tp"),
        check_vma=False,
    )
```

```python
import functools

import jax
import jax.numpy as jnp
from jax import lax
from jax.experimental import pallas as pl
from jax.experimental.pallas import tpu as pltpu
from jax.sharding import PartitionSpec as P

HEAD_WIDTH = 128
GROUP = 64
LANES = 128
VMEM_LIMIT = 24 * 1024 * 1024
F32 = jnp.float32
BF16 = jnp.bfloat16


def call(body, outs, name, used, after=(), flops=1024, **extra):
    vmem = pl.BlockSpec(memory_space=pltpu.VMEM)
    unread = pl.BlockSpec(memory_space=pl.ANY)
    in_specs = extra.pop("in_specs", [vmem] * len(used))

    def without_after(*refs):
        body(*refs[: len(used)], *refs[len(used) + len(after) :])

    return pl.pallas_call(
        without_after,
        out_shape=outs,
        in_specs=in_specs + [unread] * len(after),
        compiler_params=pltpu.CompilerParams(vmem_limit_bytes=VMEM_LIMIT),
        cost_estimate=pl.CostEstimate(flops=flops, bytes_accessed=1024, transcendentals=0),
        name=name,
        **extra,
    )(*used, *after)


def exchange(x, bit):
    size = lax.axis_size("tp")
    return lax.ppermute(x, "tp", [(i, i ^ bit) for i in range(size)])


def shifted(x, by):
    length = lax.axis_size("seq")
    pairs = [(i, i + by) for i in range(length) if 0 <= i + by < length]
    return lax.ppermute(x, "seq", pairs)


def columns_of(row):
    return jnp.broadcast_to(row, (LANES, row.shape[1])).T


def one_hot(column, width):
    lane = lax.broadcasted_iota(jnp.int32, column.shape, 1)
    return jnp.concatenate(
        [jnp.where(column == lane + at, 1.0, 0.0).astype(BF16) for at in range(0, width, LANES)],
        axis=1,
    )


def route_body(voc, cap, ids_ref, wanted_ref, slot_ref):
    ids = ids_ref[...]
    count = ids.shape[1]
    owners = wanted_ref.shape[0]
    owner = lax.div(ids, jnp.int32(voc))
    local = ids - owner * voc
    hit = owner == lax.broadcasted_iota(jnp.int32, (owners, count), 0)
    hot = jnp.where(hit, 1.0, 0.0)
    upper = jnp.where(
        lax.broadcasted_iota(jnp.int32, (LANES, LANES), 0)
        <= lax.broadcasted_iota(jnp.int32, (LANES, LANES), 1),
        1.0,
        0.0,
    ).astype(BF16)
    carry = jnp.zeros((owners, 1), F32)
    ranks = []
    for at in range(0, count, LANES):
        part = hot[:, at : at + LANES]
        running = jnp.dot(part.astype(BF16), upper, preferred_element_type=F32) + carry
        ranks.append(jnp.sum(part * running, axis=0, keepdims=True))
        carry = running[:, LANES - 1 :]
    rank = jnp.concatenate(ranks, axis=1).astype(jnp.int32) - 1
    high = jnp.where(hit, lax.div(local, jnp.int32(256)), 0)
    low = jnp.where(hit, lax.rem(local, jnp.int32(256)), 0)
    digits = jnp.concatenate([high, low], axis=0).astype(F32).astype(BF16)
    place = jnp.where(
        rank == lax.broadcasted_iota(jnp.int32, (cap, count), 0), 1.0, 0.0
    ).astype(BF16)
    found = lax.dot_general(
        digits, place, (((1,), (1,)), ((), ())), preferred_element_type=F32
    ).astype(jnp.int32)
    wanted_ref[...] = found[:owners] * 256 + found[owners:]
    slot_ref[...] = columns_of(owner * cap + rank)


def fetch_body(req_ref, vocab_ref, out_ref):
    step = 256
    table = vocab_ref[...]
    for at in range(0, req_ref.shape[1], step):
        picked = one_hot(columns_of(req_ref[:, at : at + step]), table.shape[0])
        out_ref[at : at + step, :] = jnp.dot(
            picked, table, preferred_element_type=F32
        ).astype(BF16)


def mark_body(out_ref):
    out_ref[...] = jnp.zeros_like(out_ref)


def pair_body(left_ref, right_ref, out_ref):
    width = left_ref.shape[1]
    out_ref[:, :width] = left_ref[...]
    out_ref[:, width:] = right_ref[...]


def head_body(queries_ref, out_ref):
    out_ref[...] = queries_ref[: out_ref.shape[0], :]


def order_body(groups, slot_ref, rows_ref, out_ref):
    rows = rows_ref[...]
    count = out_ref.shape[0] // len(groups)
    for at, g in enumerate(groups):
        picked = one_hot(slot_ref[g * count : (g + 1) * count, :], rows.shape[0])
        out_ref[at * count : (at + 1) * count, :] = jnp.dot(
            picked, rows, preferred_element_type=F32
        ).astype(BF16)


def block_rows(ref, index, width):
    return ref[pl.ds(pl.multiple_of(index * width, width), width), :]


def block_cols(ref, index, width):
    return ref[:, pl.ds(pl.multiple_of(index * width, width), width)]


def feed_body(first, e0_ref, e2_ref, other_ref, w_in_ref, w_out_ref, keep_ref, send_ref):
    me = lax.axis_index("tp")
    width = e0_ref.shape[1]
    index = [me, me ^ 2, me ^ 1, me ^ 3]
    here = slice(first, first + keep_ref.shape[0])
    parts = [e0_ref[here, :], e2_ref[here, :], other_ref[here, :width], other_ref[here, width:]]
    parts = [part.astype(F32) for part in parts]
    square = sum(jnp.sum(part * part, axis=1, keepdims=True) for part in parts)
    scale = lax.rsqrt(square / (4 * width) + 1e-06)
    hidden = sum(
        jnp.dot(
            (part * scale).astype(BF16), block_rows(w_in_ref, at, width), preferred_element_type=F32
        )
        for part, at in zip(parts, index)
    )
    inner = jax.nn.gelu(hidden, approximate=True).astype(BF16)
    for slot in range(2):
        cols = slice(slot * width, (slot + 1) * width)
        keep_ref[:, cols] = jnp.dot(
            inner, block_cols(w_out_ref, index[slot], width), preferred_element_type=F32
        )
        send_ref[:, cols] = jnp.dot(
            inner, block_cols(w_out_ref, index[2 + slot], width), preferred_element_type=F32
        ).astype(BF16)


def add_body(keep_ref, recv_ref, chip_ref, send_ref):
    chip = keep_ref[...] + recv_ref[...].astype(F32)
    chip_ref[...] = chip
    send_ref[...] = chip.astype(BF16)


def finish_body(first, e0_ref, e2_ref, chip_ref, far_ref, mine_ref):
    width = e0_ref.shape[1]
    near, past = slice(0, width), slice(width, 2 * width)
    here = slice(first, first + mine_ref.shape[0])
    mine_ref[:, near] = (
        e0_ref[here, :].astype(F32) + (chip_ref[:, near] + far_ref[:, past].astype(F32))
    ).astype(BF16)
    mine_ref[:, past] = (
        e2_ref[here, :].astype(F32) + (chip_ref[:, past] + far_ref[:, near].astype(F32))
    ).astype(BF16)


def attended(mine_ref, other_ref, w_key_ref, w_value_ref, q_ref):
    me = lax.axis_index("tp")
    width = mine_ref.shape[1] // 2
    parts = [
        (mine_ref[:, :width], me),
        (mine_ref[:, width:], me ^ 2),
        (other_ref[:, :width], me ^ 1),
        (other_ref[:, width:], me ^ 3),
    ]

    def project(w_ref):
        return sum(
            jnp.dot(part, block_rows(w_ref, at, width), preferred_element_type=F32)
            for part, at in parts
        ).astype(BF16)

    heads = [slice(at, at + HEAD_WIDTH) for at in range(0, q_ref.shape[1], HEAD_WIDTH)]
    keys = project(w_key_ref)
    weights = []
    for cols in heads:
        logits = lax.dot_general(
            q_ref[:, cols], keys[:, cols], (((1,), (1,)), ((), ())), preferred_element_type=F32
        ) * HEAD_WIDTH ** (-0.5)
        expo = jnp.exp(logits)
        weights.append((expo * (1.0 / jnp.sum(expo, axis=1, keepdims=True))).astype(BF16))
    values = project(w_value_ref)
    return [
        jnp.dot(weight, values[:, cols], preferred_element_type=F32)
        for weight, cols in zip(weights, heads)
    ]


def attend_body(mine_ref, other_ref, w_key_ref, w_value_ref, q_ref, out_ref):
    for at, part in enumerate(attended(mine_ref, other_ref, w_key_ref, w_value_ref, q_ref)):
        out_ref[:, at * HEAD_WIDTH : (at + 1) * HEAD_WIDTH] = part.astype(BF16)


def attend_first_body(
    mine_ref, other_ref, w_key_ref, w_value_ref, queries_ref, next_ref, out_ref, q_ref
):
    edge = 16
    for at in range(0, q_ref.shape[1], HEAD_WIDTH):
        cols = slice(at, at + HEAD_WIDTH)
        tall = jnp.concatenate(
            [queries_ref[-edge:, cols].astype(F32), next_ref[:, cols].astype(F32)], axis=0
        )
        moved = pltpu.roll(tall, tall.shape[0] - edge + 1, 0)
        q_ref[:, cols] = moved[: q_ref.shape[0]].astype(BF16)
    attend_body(mine_ref, other_ref, w_key_ref, w_value_ref, q_ref, out_ref)


def attend_last_body(
    mine_ref, other_ref, w_key_ref, w_value_ref, q_ref, behind_ref, *refs
):
    before, last_ref, out_ref = refs[:-2], refs[-2], refs[-1]
    parts = attended(mine_ref, other_ref, w_key_ref, w_value_ref, q_ref)
    for at, part in enumerate(parts):
        cols = slice(at * HEAD_WIDTH, (at + 1) * HEAD_WIDTH)
        part = part.astype(BF16).astype(F32)
        stack = [behind_ref[:, cols].astype(F32)]
        stack += [ref[:, cols].astype(F32) for ref in before]
        stack += [part, last_ref[:, cols].astype(F32)]
        tall = jnp.concatenate(stack, axis=0)
        moved = pltpu.roll(tall, tall.shape[0] - 1, 0)
        out_ref[:, cols] = moved[: out_ref.shape[0]].astype(BF16)


def per_device(queries, vocab_rows, neighbour_ids, w_in, w_out, w_key, w_value):
    seq_size = lax.axis_size("seq")
    groups, nbrs, nlen = neighbour_ids.shape
    per_group = nbrs * nlen
    rows = groups * per_group
    voc, width = vocab_rows.shape
    tok, head_cols = queries.shape
    cap = max(2, 2 * rows // seq_size)
    slots = seq_size * cap
    sds = jax.ShapeDtypeStruct

    wanted, slot = call(
        functools.partial(route_body, voc, cap),
        (sds((seq_size, cap), jnp.int32), sds((rows, LANES), jnp.int32)),
        "route",
        (neighbour_ids.reshape(1, rows),),
        flops=8 * 10**9,
    )
    request = lax.all_to_all(wanted, "seq", split_axis=0, concat_axis=0, tiled=True)
    found = call(
        fetch_body,
        sds((slots, width), BF16),
        "fetch",
        (request.reshape(1, slots), vocab_rows),
    )
    answered = lax.all_to_all(
        found.reshape(seq_size, cap, width), "seq", split_axis=0, concat_axis=0, tiled=True
    ).reshape(slots, width)
    order = [groups - 1] + list(range(groups - 1))
    plan = [order[:2], order[2:]]
    first, window = {}, {}
    token = slot
    pieces = []
    for part in plan:
        e0 = token = call(
            functools.partial(order_body, part),
            sds((len(part) * per_group, width), BF16),
            "order",
            (slot, answered),
            (token,),
        )
        pieces.append([e0, exchange(e0, 2), None])
        for at, g in enumerate(part):
            first[g] = at * per_group

    def across(piece, after=()):
        count = piece[0].shape[0]
        both = call(pair_body, sds((count, 2 * width), BF16), "pair", piece[:2], after)
        piece[2] = exchange(both, 1)
        return both

    across(pieces[0], (token,))
    head = call(head_body, sds((GROUP, head_cols), BF16), "head", (queries,), (token,))
    next_q = shifted(head, -1)
    half = sds((per_group, 2 * width), BF16)
    whole = sds((per_group, 2 * width), F32)
    fed, summed, far, encoded = {}, {}, {}, {}
    behind = out = None

    def emb(g):
        return pieces[0 if g in plan[0] else 1]

    def rest(_):
        nonlocal token
        token = across(pieces[1], (token,))

    def pause(_):
        nonlocal token
        token = call(mark_body, sds((8, LANES), F32), "mark", (), (token, pieces[1][1], next_q))

    def feed(g):
        nonlocal token
        keep, token = call(
            functools.partial(feed_body, first[g]),
            (whole, half),
            "feed",
            (*emb(g), w_in, w_out),
            (token,),
        )
        fed[g] = keep, exchange(token, 1)

    def add(g):
        nonlocal token
        summed[g], token = call(add_body, (whole, half), "add", fed[g], (token,))
        far[g] = exchange(token, 2)

    def finish(g):
        nonlocal token
        token = call(
            functools.partial(finish_body, first[g]),
            half,
            "finish",
            (*emb(g)[:2], summed[g], far[g]),
            (token, behind) if g == order[-1] else (token,),
        )
        encoded[g] = token, exchange(token, 1)

    def attend(g):
        nonlocal token, behind, out
        start = (g + 1) * GROUP - 1
        args = (*encoded[g], w_key, w_value)
        if g == order[0]:
            window[g] = token = call(
                attend_first_body,
                sds((GROUP, head_cols), BF16),
                "attend_first",
                (*args, queries, next_q),
                (token,),
                scratch_shapes=[pltpu.VMEM((GROUP, head_cols), BF16)],
            )
            behind = shifted(token, 1)
            return
        args += (queries[start : start + GROUP],)
        if g == order[-1]:
            before = [window[at] for at in order[1:-1]]
            out = call(
                attend_last_body,
                sds((tok, head_cols), BF16),
                "attend_last",
                (*args, behind, *before, window[order[0]]),
            )
            return
        window[g] = token = call(
            attend_body,
            sds((GROUP, head_cols), BF16),
            "attend",
            args,
            (token,),
        )

    a, b, c, d = order
    for step, g in (
        (feed, a), (feed, b), (pause, c), (add, a), (rest, c), (feed, c), (add, b),
        (finish, a), (feed, d), (add, c),
        (finish, b), (attend, a), (add, d),
        (finish, c), (attend, b),
        (finish, d), (attend, c), (attend, d),
    ):
        step(g)
    return out


def solution(mesh):
    return jax.shard_map(
        per_device,
        mesh=mesh,
        in_specs=(
            P("seq", "tp"),
            P("seq", "tp"),
            P("seq", None, None),
            P(None, "tp"),
            P("tp", None),
            P(None, "tp"),
            P(None, "tp"),
        ),
        out_specs=P("seq", "tp"),
        check_vma=False,
    )
```

```python
import functools

import jax
import jax.numpy as jnp
from jax import lax
from jax.experimental import pallas as pl
from jax.experimental.pallas import tpu as pltpu
from jax.sharding import PartitionSpec as P

HEAD_WIDTH = 128
GROUP = 64
LANES = 128
VMEM_LIMIT = 24 * 1024 * 1024
F32 = jnp.float32
BF16 = jnp.bfloat16


def call(body, outs, name, used, after=(), flops=1024, **extra):
    vmem = pl.BlockSpec(memory_space=pltpu.VMEM)
    unread = pl.BlockSpec(memory_space=pl.ANY)
    in_specs = extra.pop("in_specs", [vmem] * len(used))

    def without_after(*refs):
        body(*refs[: len(used)], *refs[len(used) + len(after) :])

    return pl.pallas_call(
        without_after,
        out_shape=outs,
        in_specs=in_specs + [unread] * len(after),
        compiler_params=pltpu.CompilerParams(vmem_limit_bytes=VMEM_LIMIT),
        cost_estimate=pl.CostEstimate(flops=flops, bytes_accessed=1024, transcendentals=0),
        name=name,
        **extra,
    )(*used, *after)


def exchange(x, bit):
    size = lax.axis_size("tp")
    return lax.ppermute(x, "tp", [(i, i ^ bit) for i in range(size)])


def shifted(x, by):
    length = lax.axis_size("seq")
    pairs = [(i, i + by) for i in range(length) if 0 <= i + by < length]
    return lax.ppermute(x, "seq", pairs)


def columns_of(row):
    return jnp.broadcast_to(row, (LANES, row.shape[1])).T


def one_hot(column, width):
    lane = lax.broadcasted_iota(jnp.int32, column.shape, 1)
    return jnp.concatenate(
        [jnp.where(column == lane + at, 1.0, 0.0).astype(BF16) for at in range(0, width, LANES)],
        axis=1,
    )


def route_body(voc, cap, ids_ref, wanted_ref, slot_ref):
    ids = ids_ref[...]
    count = ids.shape[1]
    owners = wanted_ref.shape[0]
    owner = lax.div(ids, jnp.int32(voc))
    local = ids - owner * voc
    hit = owner == lax.broadcasted_iota(jnp.int32, (owners, count), 0)
    hot = jnp.where(hit, 1.0, 0.0)
    upper = jnp.where(
        lax.broadcasted_iota(jnp.int32, (LANES, LANES), 0)
        <= lax.broadcasted_iota(jnp.int32, (LANES, LANES), 1),
        1.0,
        0.0,
    ).astype(BF16)
    carry = jnp.zeros((owners, 1), F32)
    ranks = []
    for at in range(0, count, LANES):
        part = hot[:, at : at + LANES]
        running = jnp.dot(part.astype(BF16), upper, preferred_element_type=F32) + carry
        ranks.append(jnp.sum(part * running, axis=0, keepdims=True))
        carry = running[:, LANES - 1 :]
    rank = jnp.concatenate(ranks, axis=1).astype(jnp.int32) - 1
    high = jnp.where(hit, lax.div(local, jnp.int32(256)), 0)
    low = jnp.where(hit, lax.rem(local, jnp.int32(256)), 0)
    digits = jnp.concatenate([high, low], axis=0).astype(F32).astype(BF16)
    place = jnp.where(
        rank == lax.broadcasted_iota(jnp.int32, (cap, count), 0), 1.0, 0.0
    ).astype(BF16)
    found = lax.dot_general(
        digits, place, (((1,), (1,)), ((), ())), preferred_element_type=F32
    ).astype(jnp.int32)
    wanted_ref[...] = found[:owners] * 256 + found[owners:]
    slot_ref[...] = columns_of(owner * cap + rank)


def fetch_body(req_ref, vocab_ref, out_ref):
    step = 256
    table = vocab_ref[...]
    for at in range(0, req_ref.shape[1], step):
        picked = one_hot(columns_of(req_ref[:, at : at + step]), table.shape[0])
        out_ref[at : at + step, :] = jnp.dot(
            picked, table, preferred_element_type=F32
        ).astype(BF16)


def mark_body(out_ref):
    out_ref[...] = jnp.zeros_like(out_ref)


def pair_body(left_ref, right_ref, out_ref):
    width = left_ref.shape[1]
    out_ref[:, :width] = left_ref[...]
    out_ref[:, width:] = right_ref[...]


def head_body(queries_ref, out_ref):
    out_ref[...] = queries_ref[: out_ref.shape[0], :]


def order_body(groups, slot_ref, rows_ref, out_ref):
    rows = rows_ref[...]
    count = out_ref.shape[0] // len(groups)
    for at, g in enumerate(groups):
        picked = one_hot(slot_ref[g * count : (g + 1) * count, :], rows.shape[0])
        out_ref[at * count : (at + 1) * count, :] = jnp.dot(
            picked, rows, preferred_element_type=F32
        ).astype(BF16)


def block_rows(ref, index, width):
    return ref[pl.ds(pl.multiple_of(index * width, width), width), :]


def block_cols(ref, index, width):
    return ref[:, pl.ds(pl.multiple_of(index * width, width), width)]


def feed_body(first, e0_ref, e2_ref, other_ref, w_in_ref, w_out_ref, keep_ref, send_ref):
    me = lax.axis_index("tp")
    width = e0_ref.shape[1]
    index = [me, me ^ 2, me ^ 1, me ^ 3]
    here = slice(first, first + keep_ref.shape[0])
    parts = [e0_ref[here, :], e2_ref[here, :], other_ref[here, :width], other_ref[here, width:]]
    parts = [part.astype(F32) for part in parts]
    square = sum(jnp.sum(part * part, axis=1, keepdims=True) for part in parts)
    scale = lax.rsqrt(square / (4 * width) + 1e-06)
    hidden = sum(
        jnp.dot(
            (part * scale).astype(BF16), block_rows(w_in_ref, at, width), preferred_element_type=F32
        )
        for part, at in zip(parts, index)
    )
    inner = jax.nn.gelu(hidden, approximate=True).astype(BF16)
    for slot in range(2):
        cols = slice(slot * width, (slot + 1) * width)
        keep_ref[:, cols] = jnp.dot(
            inner, block_cols(w_out_ref, index[slot], width), preferred_element_type=F32
        )
        send_ref[:, cols] = jnp.dot(
            inner, block_cols(w_out_ref, index[2 + slot], width), preferred_element_type=F32
        ).astype(BF16)


def add_body(keep_ref, recv_ref, chip_ref, send_ref):
    chip = keep_ref[...] + recv_ref[...].astype(F32)
    chip_ref[...] = chip
    send_ref[...] = chip.astype(BF16)


def finish_body(first, e0_ref, e2_ref, chip_ref, far_ref, mine_ref):
    width = e0_ref.shape[1]
    near, past = slice(0, width), slice(width, 2 * width)
    here = slice(first, first + mine_ref.shape[0])
    mine_ref[:, near] = (
        e0_ref[here, :].astype(F32) + (chip_ref[:, near] + far_ref[:, past].astype(F32))
    ).astype(BF16)
    mine_ref[:, past] = (
        e2_ref[here, :].astype(F32) + (chip_ref[:, past] + far_ref[:, near].astype(F32))
    ).astype(BF16)


def attended(mine_ref, other_ref, w_key_ref, w_value_ref, q_ref):
    me = lax.axis_index("tp")
    width = mine_ref.shape[1] // 2
    parts = [
        (mine_ref[:, :width], me),
        (mine_ref[:, width:], me ^ 2),
        (other_ref[:, :width], me ^ 1),
        (other_ref[:, width:], me ^ 3),
    ]

    def project(w_ref):
        return sum(
            jnp.dot(part, block_rows(w_ref, at, width), preferred_element_type=F32)
            for part, at in parts
        ).astype(BF16)

    heads = [slice(at, at + HEAD_WIDTH) for at in range(0, q_ref.shape[1], HEAD_WIDTH)]
    keys = project(w_key_ref)
    weights = []
    for cols in heads:
        logits = lax.dot_general(
            q_ref[:, cols], keys[:, cols], (((1,), (1,)), ((), ())), preferred_element_type=F32
        ) * HEAD_WIDTH ** (-0.5)
        expo = jnp.exp(logits)
        weights.append((expo * (1.0 / jnp.sum(expo, axis=1, keepdims=True))).astype(BF16))
    values = project(w_value_ref)
    return [
        jnp.dot(weight, values[:, cols], preferred_element_type=F32)
        for weight, cols in zip(weights, heads)
    ]


def attend_body(mine_ref, other_ref, w_key_ref, w_value_ref, q_ref, out_ref):
    for at, part in enumerate(attended(mine_ref, other_ref, w_key_ref, w_value_ref, q_ref)):
        out_ref[:, at * HEAD_WIDTH : (at + 1) * HEAD_WIDTH] = part.astype(BF16)


def attend_first_body(
    mine_ref, other_ref, w_key_ref, w_value_ref, queries_ref, next_ref, out_ref, q_ref
):
    edge = 16
    for at in range(0, q_ref.shape[1], HEAD_WIDTH):
        cols = slice(at, at + HEAD_WIDTH)
        tall = jnp.concatenate(
            [queries_ref[-edge:, cols].astype(F32), next_ref[:, cols].astype(F32)], axis=0
        )
        moved = pltpu.roll(tall, tall.shape[0] - edge + 1, 0)
        q_ref[:, cols] = moved[: q_ref.shape[0]].astype(BF16)
    attend_body(mine_ref, other_ref, w_key_ref, w_value_ref, q_ref, out_ref)


def attend_last_body(
    mine_ref, other_ref, w_key_ref, w_value_ref, q_ref, behind_ref, *refs
):
    before, last_ref, out_ref = refs[:-2], refs[-2], refs[-1]
    parts = attended(mine_ref, other_ref, w_key_ref, w_value_ref, q_ref)
    for at, part in enumerate(parts):
        cols = slice(at * HEAD_WIDTH, (at + 1) * HEAD_WIDTH)
        part = part.astype(BF16).astype(F32)
        stack = [behind_ref[:, cols].astype(F32)]
        stack += [ref[:, cols].astype(F32) for ref in before]
        stack += [part, last_ref[:, cols].astype(F32)]
        tall = jnp.concatenate(stack, axis=0)
        moved = pltpu.roll(tall, tall.shape[0] - 1, 0)
        out_ref[:, cols] = moved[: out_ref.shape[0]].astype(BF16)


def per_device(queries, vocab_rows, neighbour_ids, w_in, w_out, w_key, w_value):
    seq_size = lax.axis_size("seq")
    groups, nbrs, nlen = neighbour_ids.shape
    per_group = nbrs * nlen
    rows = groups * per_group
    voc, width = vocab_rows.shape
    tok, head_cols = queries.shape
    cap = max(2, 2 * rows // seq_size)
    slots = seq_size * cap
    sds = jax.ShapeDtypeStruct

    wanted, slot = call(
        functools.partial(route_body, voc, cap),
        (sds((seq_size, cap), jnp.int32), sds((rows, LANES), jnp.int32)),
        "route",
        (neighbour_ids.reshape(1, rows),),
        flops=8 * 10**9,
    )
    request = lax.all_to_all(wanted, "seq", split_axis=0, concat_axis=0, tiled=True)
    found = call(
        fetch_body,
        sds((slots, width), BF16),
        "fetch",
        (request.reshape(1, slots), vocab_rows),
    )
    answered = lax.all_to_all(
        found.reshape(seq_size, cap, width), "seq", split_axis=0, concat_axis=0, tiled=True
    ).reshape(slots, width)
    order = [groups - 1] + list(range(groups - 1))
    plan = [order[:2], order[2:]]
    first, window = {}, {}
    token = slot
    pieces = []
    for part in plan:
        e0 = token = call(
            functools.partial(order_body, part),
            sds((len(part) * per_group, width), BF16),
            "order",
            (slot, answered),
            (token,),
        )
        pieces.append([e0, exchange(e0, 2), None])
        for at, g in enumerate(part):
            first[g] = at * per_group

    def across(piece, after=()):
        count = piece[0].shape[0]
        both = call(pair_body, sds((count, 2 * width), BF16), "pair", piece[:2], after)
        piece[2] = exchange(both, 1)
        return both

    across(pieces[0], (token,))
    half = sds((per_group, 2 * width), BF16)
    whole = sds((per_group, 2 * width), F32)
    fed, summed, far, encoded = {}, {}, {}, {}
    behind = out = next_q = None

    def emb(g):
        return pieces[0 if g in plan[0] else 1]

    def rest(_):
        nonlocal token
        token = across(pieces[1], (token, fed[order[1]][1]))

    def pause(_):
        nonlocal token
        token = call(mark_body, sds((8, LANES), F32), "mark", (), (token, pieces[1][1]))

    def ask(_):
        nonlocal next_q
        head = call(head_body, sds((GROUP, head_cols), BF16), "head", (queries,), (token,))
        next_q = shifted(head, -1)

    def feed(g):
        nonlocal token
        keep, token = call(
            functools.partial(feed_body, first[g]),
            (whole, half),
            "feed",
            (*emb(g), w_in, w_out),
            (token,),
        )
        fed[g] = keep, exchange(token, 1)

    def add(g):
        nonlocal token
        summed[g], token = call(add_body, (whole, half), "add", fed[g], (token,))
        far[g] = exchange(token, 2)

    def finish(g):
        nonlocal token
        token = call(
            functools.partial(finish_body, first[g]),
            half,
            "finish",
            (*emb(g)[:2], summed[g], far[g]),
            (token, *{order[0]: (next_q,), order[-1]: (behind,)}.get(g, ())),
        )
        encoded[g] = token, exchange(token, 1)

    def attend(g):
        nonlocal token, behind, out
        start = (g + 1) * GROUP - 1
        args = (*encoded[g], w_key, w_value)
        if g == order[0]:
            window[g] = token = call(
                attend_first_body,
                sds((GROUP, head_cols), BF16),
                "attend_first",
                (*args, queries, next_q),
                (token,),
                scratch_shapes=[pltpu.VMEM((GROUP, head_cols), BF16)],
            )
            behind = shifted(token, 1)
            return
        args += (queries[start : start + GROUP],)
        if g == order[-1]:
            before = [window[at] for at in order[1:-1]]
            out = call(
                attend_last_body,
                sds((tok, head_cols), BF16),
                "attend_last",
                (*args, behind, *before, window[order[0]]),
            )
            return
        window[g] = token = call(
            attend_body,
            sds((GROUP, head_cols), BF16),
            "attend",
            args,
            (token,),
        )

    a, b, c, d = order
    for step, g in (
        (feed, a), (feed, b), (pause, c), (add, a), (ask, a), (rest, c), (feed, c), (add, b),
        (finish, a), (feed, d), (add, c),
        (finish, b), (attend, a), (add, d),
        (finish, c), (attend, b),
        (finish, d), (attend, c), (attend, d),
    ):
        step(g)
    return out


def solution(mesh):
    return jax.shard_map(
        per_device,
        mesh=mesh,
        in_specs=(
            P("seq", "tp"),
            P("seq", "tp"),
            P("seq", None, None),
            P(None, "tp"),
            P("tp", None),
            P(None, "tp"),
            P(None, "tp"),
        ),
        out_specs=P("seq", "tp"),
        check_vma=False,
    )
```

```python
import functools

import jax
import jax.numpy as jnp
from jax import lax
from jax.experimental import pallas as pl
from jax.experimental.pallas import tpu as pltpu
from jax.sharding import PartitionSpec as P

HEAD_WIDTH = 128
GROUP = 64
LANES = 128
VMEM_LIMIT = 24 * 1024 * 1024
F32 = jnp.float32
BF16 = jnp.bfloat16


def call(body, outs, name, used, after=(), flops=1024, **extra):
    vmem = pl.BlockSpec(memory_space=pltpu.VMEM)
    unread = pl.BlockSpec(memory_space=pl.ANY)
    in_specs = extra.pop("in_specs", [vmem] * len(used))

    def without_after(*refs):
        body(*refs[: len(used)], *refs[len(used) + len(after) :])

    return pl.pallas_call(
        without_after,
        out_shape=outs,
        in_specs=in_specs + [unread] * len(after),
        compiler_params=pltpu.CompilerParams(vmem_limit_bytes=VMEM_LIMIT),
        cost_estimate=pl.CostEstimate(flops=flops, bytes_accessed=1024, transcendentals=0),
        name=name,
        **extra,
    )(*used, *after)


def exchange(x, bit):
    size = lax.axis_size("tp")
    return lax.ppermute(x, "tp", [(i, i ^ bit) for i in range(size)])


def shifted(x, by):
    length = lax.axis_size("seq")
    pairs = [(i, i + by) for i in range(length) if 0 <= i + by < length]
    return lax.ppermute(x, "seq", pairs)


def columns_of(row):
    return jnp.broadcast_to(row, (LANES, row.shape[1])).T


def one_hot(column, width):
    lane = lax.broadcasted_iota(jnp.int32, column.shape, 1)
    inside = jnp.where(lax.rem(column, jnp.int32(LANES)) == lane, 1.0, 0.0).astype(BF16)
    block = lax.div(column, jnp.int32(LANES)).astype(F32).astype(BF16)
    nothing = jnp.zeros_like(inside)
    return jnp.concatenate(
        [jnp.where(block == BF16(at), inside, nothing) for at in range(width // LANES)], axis=1
    )


def route_body(voc, cap, ids_ref, wanted_ref, slot_ref):
    ids = ids_ref[...]
    count = ids.shape[1]
    owners = wanted_ref.shape[0]
    owner = lax.div(ids, jnp.int32(voc))
    local = ids - owner * voc
    hit = owner == lax.broadcasted_iota(jnp.int32, (owners, count), 0)
    hot = jnp.where(hit, 1.0, 0.0)
    upper = jnp.where(
        lax.broadcasted_iota(jnp.int32, (LANES, LANES), 0)
        <= lax.broadcasted_iota(jnp.int32, (LANES, LANES), 1),
        1.0,
        0.0,
    ).astype(BF16)
    carry = jnp.zeros((owners, 1), F32)
    ranks = []
    for at in range(0, count, LANES):
        part = hot[:, at : at + LANES]
        running = jnp.dot(part.astype(BF16), upper, preferred_element_type=F32) + carry
        ranks.append(jnp.sum(part * running, axis=0, keepdims=True))
        carry = running[:, LANES - 1 :]
    rank = jnp.concatenate(ranks, axis=1).astype(jnp.int32) - 1
    high = jnp.where(hit, lax.div(local, jnp.int32(256)), 0)
    low = jnp.where(hit, lax.rem(local, jnp.int32(256)), 0)
    digits = jnp.concatenate([high, low], axis=0).astype(F32).astype(BF16)
    place = jnp.where(
        rank == lax.broadcasted_iota(jnp.int32, (cap, count), 0), 1.0, 0.0
    ).astype(BF16)
    found = lax.dot_general(
        digits, place, (((1,), (1,)), ((), ())), preferred_element_type=F32
    ).astype(jnp.int32)
    wanted_ref[...] = found[:owners] * 256 + found[owners:]
    slot_ref[...] = columns_of(owner * cap + rank)


def fetch_body(req_ref, vocab_ref, out_ref):
    step = 256
    table = vocab_ref[...]
    for at in range(0, req_ref.shape[1], step):
        picked = one_hot(columns_of(req_ref[:, at : at + step]), table.shape[0])
        out_ref[at : at + step, :] = jnp.dot(
            picked, table, preferred_element_type=F32
        ).astype(BF16)


def mark_body(out_ref):
    out_ref[...] = jnp.zeros_like(out_ref)


def pair_body(left_ref, right_ref, out_ref):
    width = left_ref.shape[1]
    out_ref[:, :width] = left_ref[...]
    out_ref[:, width:] = right_ref[...]


def split_body(joint_ref, *out_refs):
    count = out_refs[0].shape[0]
    for at, out_ref in enumerate(out_refs):
        out_ref[...] = joint_ref[at * count : (at + 1) * count, :]


def head_body(queries_ref, out_ref):
    out_ref[...] = queries_ref[: out_ref.shape[0], :]


def order_body(groups, slot_ref, rows_ref, joint_ref, *out_refs):
    rows = rows_ref[...]
    for at, (g, out_ref) in enumerate(zip(groups, out_refs)):
        count = out_ref.shape[0]
        picked = one_hot(slot_ref[g * count : (g + 1) * count, :], rows.shape[0])
        own = jnp.dot(picked, rows, preferred_element_type=F32).astype(BF16)
        out_ref[...] = own
        joint_ref[at * count : (at + 1) * count, :] = own


def block_rows(ref, index, width):
    return ref[pl.ds(pl.multiple_of(index * width, width), width), :]


def block_cols(ref, index, width):
    return ref[:, pl.ds(pl.multiple_of(index * width, width), width)]


def feed_body(first, e0_ref, e2_ref, *refs):
    other_refs, (w_in_ref, w_out_ref, keep_ref, send_ref) = refs[:-4], refs[-4:]
    me = lax.axis_index("tp")
    width = e0_ref.shape[1]
    index = [me, me ^ 2, me ^ 1, me ^ 3]
    here = slice(first, first + keep_ref.shape[0])
    parts = [e0_ref[here, :], e2_ref[here, :]]
    if len(other_refs) == 1:
        parts += [other_refs[0][here, :width], other_refs[0][here, width:]]
    else:
        parts += [ref[...] for ref in other_refs]
    parts = [part.astype(F32) for part in parts]
    square = sum(jnp.sum(part * part, axis=1, keepdims=True) for part in parts)
    scale = lax.rsqrt(square / (4 * width) + 1e-06)
    hidden = sum(
        jnp.dot(
            (part * scale).astype(BF16), block_rows(w_in_ref, at, width), preferred_element_type=F32
        )
        for part, at in zip(parts, index)
    )
    inner = jax.nn.gelu(hidden, approximate=True).astype(BF16)
    for slot in range(2):
        cols = slice(slot * width, (slot + 1) * width)
        keep_ref[:, cols] = jnp.dot(
            inner, block_cols(w_out_ref, index[slot], width), preferred_element_type=F32
        )
        send_ref[:, cols] = jnp.dot(
            inner, block_cols(w_out_ref, index[2 + slot], width), preferred_element_type=F32
        ).astype(BF16)


def add_body(keep_ref, recv_ref, chip_ref, send_ref):
    chip = keep_ref[...] + recv_ref[...].astype(F32)
    chip_ref[...] = chip
    send_ref[...] = chip.astype(BF16)


def finish_body(first, e0_ref, e2_ref, chip_ref, far_ref, mine_ref):
    width = e0_ref.shape[1]
    near, past = slice(0, width), slice(width, 2 * width)
    here = slice(first, first + mine_ref.shape[0])
    mine_ref[:, near] = (
        e0_ref[here, :].astype(F32) + (chip_ref[:, near] + far_ref[:, past].astype(F32))
    ).astype(BF16)
    mine_ref[:, past] = (
        e2_ref[here, :].astype(F32) + (chip_ref[:, past] + far_ref[:, near].astype(F32))
    ).astype(BF16)


def attended(mine_ref, other_ref, w_key_ref, w_value_ref, q_ref):
    me = lax.axis_index("tp")
    width = mine_ref.shape[1] // 2
    parts = [
        (mine_ref[:, :width], me),
        (mine_ref[:, width:], me ^ 2),
        (other_ref[:, :width], me ^ 1),
        (other_ref[:, width:], me ^ 3),
    ]

    def project(w_ref):
        return sum(
            jnp.dot(part, block_rows(w_ref, at, width), preferred_element_type=F32)
            for part, at in parts
        ).astype(BF16)

    heads = [slice(at, at + HEAD_WIDTH) for at in range(0, q_ref.shape[1], HEAD_WIDTH)]
    keys = project(w_key_ref)
    weights = []
    for cols in heads:
        logits = lax.dot_general(
            q_ref[:, cols], keys[:, cols], (((1,), (1,)), ((), ())), preferred_element_type=F32
        ) * HEAD_WIDTH ** (-0.5)
        expo = jnp.exp(logits)
        weights.append((expo * (1.0 / jnp.sum(expo, axis=1, keepdims=True))).astype(BF16))
    values = project(w_value_ref)
    return [
        jnp.dot(weight, values[:, cols], preferred_element_type=F32)
        for weight, cols in zip(weights, heads)
    ]


def attend_body(mine_ref, other_ref, w_key_ref, w_value_ref, q_ref, out_ref):
    for at, part in enumerate(attended(mine_ref, other_ref, w_key_ref, w_value_ref, q_ref)):
        out_ref[:, at * HEAD_WIDTH : (at + 1) * HEAD_WIDTH] = part.astype(BF16)


def attend_first_body(
    mine_ref, other_ref, w_key_ref, w_value_ref, queries_ref, next_ref, out_ref, q_ref
):
    edge = 16
    for at in range(0, q_ref.shape[1], HEAD_WIDTH):
        cols = slice(at, at + HEAD_WIDTH)
        tall = jnp.concatenate(
            [queries_ref[-edge:, cols].astype(F32), next_ref[:, cols].astype(F32)], axis=0
        )
        moved = pltpu.roll(tall, tall.shape[0] - edge + 1, 0)
        q_ref[:, cols] = moved[: q_ref.shape[0]].astype(BF16)
    attend_body(mine_ref, other_ref, w_key_ref, w_value_ref, q_ref, out_ref)


def attend_last_body(
    mine_ref, other_ref, w_key_ref, w_value_ref, q_ref, behind_ref, *refs
):
    before, last_ref, out_ref = refs[:-2], refs[-2], refs[-1]
    parts = attended(mine_ref, other_ref, w_key_ref, w_value_ref, q_ref)
    for at, part in enumerate(parts):
        cols = slice(at * HEAD_WIDTH, (at + 1) * HEAD_WIDTH)
        part = part.astype(BF16).astype(F32)
        stack = [behind_ref[:, cols].astype(F32)]
        stack += [ref[:, cols].astype(F32) for ref in before]
        stack += [part, last_ref[:, cols].astype(F32)]
        tall = jnp.concatenate(stack, axis=0)
        moved = pltpu.roll(tall, tall.shape[0] - 1, 0)
        out_ref[:, cols] = moved[: out_ref.shape[0]].astype(BF16)


def per_device(queries, vocab_rows, neighbour_ids, w_in, w_out, w_key, w_value):
    seq_size = lax.axis_size("seq")
    groups, nbrs, nlen = neighbour_ids.shape
    per_group = nbrs * nlen
    rows = groups * per_group
    voc, width = vocab_rows.shape
    tok, head_cols = queries.shape
    cap = max(2, 2 * rows // seq_size)
    slots = seq_size * cap
    sds = jax.ShapeDtypeStruct

    wanted, slot = call(
        functools.partial(route_body, voc, cap),
        (sds((seq_size, cap), jnp.int32), sds((rows, LANES), jnp.int32)),
        "route",
        (neighbour_ids.reshape(1, rows),),
        flops=8 * 10**9,
    )
    request = lax.all_to_all(wanted, "seq", split_axis=0, concat_axis=0, tiled=True)
    found = call(
        fetch_body,
        sds((slots, width), BF16),
        "fetch",
        (request.reshape(1, slots), vocab_rows),
    )
    answered = lax.all_to_all(
        found.reshape(seq_size, cap, width), "seq", split_axis=0, concat_axis=0, tiled=True
    ).reshape(slots, width)
    order = [groups - 1] + list(range(groups - 1))
    plan = [order[:2], order[2:]]
    first, window, other = {}, {}, {}
    token = slot
    pieces = []
    single = sds((per_group, width), BF16)
    for part in plan:
        e0, *own = call(
            functools.partial(order_body, part),
            (sds((len(part) * per_group, width), BF16), *[single] * len(part)),
            "order",
            (slot, answered),
            (token,),
        )
        token = e0
        pieces.append((e0, exchange(e0, 2)))
        for at, g in enumerate(part):
            first[g] = at * per_group
            other[g] = [exchange(own[at], 1)] if part == plan[1] else []

    both = call(
        pair_body, sds((len(plan[0]) * per_group, 2 * width), BF16), "pair", pieces[0], (token,)
    )
    both = exchange(both, 1)
    for g in plan[0]:
        other[g] = [both]
    half = sds((per_group, 2 * width), BF16)
    whole = sds((per_group, 2 * width), F32)
    fed, summed, far, encoded = {}, {}, {}, {}
    behind = out = next_q = None

    def emb(g):
        return *pieces[0 if g in plan[0] else 1], *other[g]

    def rest(_):
        nonlocal token
        after = token, fed[order[1]][1]
        far_own = call(split_body, (single,) * len(plan[1]), "split", pieces[1][1:], after)
        for g, own in zip(plan[1], far_own):
            other[g].append(exchange(own, 1))
        token = far_own[0]

    def pause(_):
        nonlocal token
        token = call(mark_body, sds((8, LANES), F32), "mark", (), (token, pieces[1][1]))

    def ask(_):
        nonlocal next_q
        head = call(head_body, sds((GROUP, head_cols), BF16), "head", (queries,), (token,))
        next_q = shifted(head, -1)

    def feed(g):
        nonlocal token
        keep, token = call(
            functools.partial(feed_body, first[g]),
            (whole, half),
            "feed",
            (*emb(g), w_in, w_out),
            (token,),
        )
        fed[g] = keep, exchange(token, 1)

    def add(g):
        nonlocal token
        summed[g], token = call(add_body, (whole, half), "add", fed[g], (token,))
        far[g] = exchange(token, 2)

    def finish(g):
        nonlocal token
        token = call(
            functools.partial(finish_body, first[g]),
            half,
            "finish",
            (*emb(g)[:2], summed[g], far[g]),
            (token, *{order[0]: (next_q,), order[-1]: (behind,)}.get(g, ())),
        )
        encoded[g] = token, exchange(token, 1)

    def attend(g):
        nonlocal token, behind, out
        start = (g + 1) * GROUP - 1
        args = (*encoded[g], w_key, w_value)
        if g == order[0]:
            window[g] = token = call(
                attend_first_body,
                sds((GROUP, head_cols), BF16),
                "attend_first",
                (*args, queries, next_q),
                (token,),
                scratch_shapes=[pltpu.VMEM((GROUP, head_cols), BF16)],
            )
            behind = shifted(token, 1)
            return
        args += (queries[start : start + GROUP],)
        if g == order[-1]:
            before = [window[at] for at in order[1:-1]]
            out = call(
                attend_last_body,
                sds((tok, head_cols), BF16),
                "attend_last",
                (*args, behind, *before, window[order[0]]),
            )
            return
        window[g] = token = call(
            attend_body,
            sds((GROUP, head_cols), BF16),
            "attend",
            args,
            (token,),
        )

    a, b, c, d = order
    for step, g in (
        (feed, a), (feed, b), (pause, c), (add, a), (ask, a), (rest, c), (feed, c), (add, b),
        (finish, a), (feed, d), (add, c),
        (finish, b), (attend, a), (add, d),
        (finish, c), (attend, b),
        (finish, d), (attend, c), (attend, d),
    ):
        step(g)
    return out


def solution(mesh):
    return jax.shard_map(
        per_device,
        mesh=mesh,
        in_specs=(
            P("seq", "tp"),
            P("seq", "tp"),
            P("seq", None, None),
            P(None, "tp"),
            P("tp", None),
            P(None, "tp"),
            P(None, "tp"),
        ),
        out_specs=P("seq", "tp"),
        check_vma=False,
    )
```

```python
import functools

import jax
import jax.numpy as jnp
from jax import lax
from jax.experimental import pallas as pl
from jax.experimental.pallas import tpu as pltpu
from jax.sharding import PartitionSpec as P

HEAD_WIDTH = 128
GROUP = 64
LANES = 128
VMEM_LIMIT = 24 * 1024 * 1024
F32 = jnp.float32
BF16 = jnp.bfloat16


def call(body, outs, name, used, after=(), flops=1024, **extra):
    vmem = pl.BlockSpec(memory_space=pltpu.VMEM)
    unread = pl.BlockSpec(memory_space=pl.ANY)
    in_specs = extra.pop("in_specs", [vmem] * len(used))

    def without_after(*refs):
        body(*refs[: len(used)], *refs[len(used) + len(after) :])

    return pl.pallas_call(
        without_after,
        out_shape=outs,
        in_specs=in_specs + [unread] * len(after),
        compiler_params=pltpu.CompilerParams(vmem_limit_bytes=VMEM_LIMIT),
        cost_estimate=pl.CostEstimate(flops=flops, bytes_accessed=1024, transcendentals=0),
        name=name,
        **extra,
    )(*used, *after)


def exchange(x, bit):
    size = lax.axis_size("tp")
    return lax.ppermute(x, "tp", [(i, i ^ bit) for i in range(size)])


def shifted(x, by):
    length = lax.axis_size("seq")
    pairs = [(i, i + by) for i in range(length) if 0 <= i + by < length]
    return lax.ppermute(x, "seq", pairs)


def columns_of(row):
    return jnp.broadcast_to(row, (LANES, row.shape[1])).T


def one_hot(column, width):
    lane = lax.broadcasted_iota(jnp.int32, column.shape, 1)
    return jnp.concatenate(
        [jnp.where(column == lane + at, 1.0, 0.0).astype(BF16) for at in range(0, width, LANES)],
        axis=1,
    )


def route_body(voc, cap, ids_ref, wanted_ref, slot_ref):
    ids = ids_ref[...]
    count = ids.shape[1]
    owners = wanted_ref.shape[0]
    owner = lax.div(ids, jnp.int32(voc))
    local = ids - owner * voc
    hit = owner == lax.broadcasted_iota(jnp.int32, (owners, count), 0)
    hot = jnp.where(hit, 1.0, 0.0)
    upper = jnp.where(
        lax.broadcasted_iota(jnp.int32, (LANES, LANES), 0)
        <= lax.broadcasted_iota(jnp.int32, (LANES, LANES), 1),
        1.0,
        0.0,
    ).astype(BF16)
    carry = jnp.zeros((owners, 1), F32)
    ranks = []
    for at in range(0, count, LANES):
        part = hot[:, at : at + LANES]
        running = jnp.dot(part.astype(BF16), upper, preferred_element_type=F32) + carry
        ranks.append(jnp.sum(part * running, axis=0, keepdims=True))
        carry = running[:, LANES - 1 :]
    rank = jnp.concatenate(ranks, axis=1).astype(jnp.int32) - 1
    high = jnp.where(hit, lax.div(local, jnp.int32(256)), 0)
    low = jnp.where(hit, lax.rem(local, jnp.int32(256)), 0)
    digits = jnp.concatenate([high, low], axis=0).astype(F32).astype(BF16)
    place = jnp.where(
        rank == lax.broadcasted_iota(jnp.int32, (cap, count), 0), 1.0, 0.0
    ).astype(BF16)
    found = lax.dot_general(
        digits, place, (((1,), (1,)), ((), ())), preferred_element_type=F32
    ).astype(jnp.int32)
    wanted_ref[...] = found[:owners] * 256 + found[owners:]
    slot_ref[...] = columns_of(owner * cap + rank)


def fetch_body(req_ref, vocab_ref, out_ref):
    step = 256
    table = vocab_ref[...]
    for at in range(0, req_ref.shape[1], step):
        picked = one_hot(columns_of(req_ref[:, at : at + step]), table.shape[0])
        out_ref[at : at + step, :] = jnp.dot(
            picked, table, preferred_element_type=F32
        ).astype(BF16)


def deal_body(left_ref, right_ref, left_out, right_out, both_out):
    count, width = left_out.shape
    left_out[...] = left_ref[:count, :]
    right_out[...] = right_ref[:count, :]
    both_out[:, :width] = left_ref[count:, :]
    both_out[:, width:] = right_ref[count:, :]


def mark_body(out_ref):
    out_ref[...] = jnp.zeros_like(out_ref)


def pair_body(left_ref, right_ref, out_ref):
    width = left_ref.shape[1]
    out_ref[:, :width] = left_ref[...]
    out_ref[:, width:] = right_ref[...]


def head_body(queries_ref, out_ref):
    out_ref[...] = queries_ref[: out_ref.shape[0], :]


def order_body(groups, slot_ref, rows_ref, out_ref):
    rows = rows_ref[...]
    count = out_ref.shape[0] // len(groups)
    for at, g in enumerate(groups):
        picked = one_hot(slot_ref[g * count : (g + 1) * count, :], rows.shape[0])
        out_ref[at * count : (at + 1) * count, :] = jnp.dot(
            picked, rows, preferred_element_type=F32
        ).astype(BF16)


def block_rows(ref, index, width):
    return ref[pl.ds(pl.multiple_of(index * width, width), width), :]


def block_cols(ref, index, width):
    return ref[:, pl.ds(pl.multiple_of(index * width, width), width)]


def feed_body(first, e0_ref, e2_ref, *refs):
    other_refs, (w_in_ref, w_out_ref, keep_ref, send_ref) = refs[:-4], refs[-4:]
    me = lax.axis_index("tp")
    width = e0_ref.shape[1]
    index = [me, me ^ 2, me ^ 1, me ^ 3]
    here = slice(first, first + keep_ref.shape[0])
    parts = [e0_ref[here, :], e2_ref[here, :]]
    if len(other_refs) == 1:
        there = here if other_refs[0].shape[0] == e0_ref.shape[0] else slice(None)
        parts += [other_refs[0][there, :width], other_refs[0][there, width:]]
    else:
        parts += [ref[...] for ref in other_refs]
    parts = [part.astype(F32) for part in parts]
    square = sum(jnp.sum(part * part, axis=1, keepdims=True) for part in parts)
    scale = lax.rsqrt(square / (4 * width) + 1e-06)
    hidden = sum(
        jnp.dot(
            (part * scale).astype(BF16), block_rows(w_in_ref, at, width), preferred_element_type=F32
        )
        for part, at in zip(parts, index)
    )
    inner = jax.nn.gelu(hidden, approximate=True).astype(BF16)
    for slot in range(2):
        cols = slice(slot * width, (slot + 1) * width)
        keep_ref[:, cols] = jnp.dot(
            inner, block_cols(w_out_ref, index[slot], width), preferred_element_type=F32
        )
        send_ref[:, cols] = jnp.dot(
            inner, block_cols(w_out_ref, index[2 + slot], width), preferred_element_type=F32
        ).astype(BF16)


def add_body(keep_ref, recv_ref, chip_ref, send_ref):
    chip = keep_ref[...] + recv_ref[...].astype(F32)
    chip_ref[...] = chip
    send_ref[...] = chip.astype(BF16)


def finish_body(first, e0_ref, e2_ref, chip_ref, far_ref, mine_ref):
    width = e0_ref.shape[1]
    near, past = slice(0, width), slice(width, 2 * width)
    here = slice(first, first + mine_ref.shape[0])
    mine_ref[:, near] = (
        e0_ref[here, :].astype(F32) + (chip_ref[:, near] + far_ref[:, past].astype(F32))
    ).astype(BF16)
    mine_ref[:, past] = (
        e2_ref[here, :].astype(F32) + (chip_ref[:, past] + far_ref[:, near].astype(F32))
    ).astype(BF16)


def attended(mine_ref, other_ref, w_key_ref, w_value_ref, q_ref):
    me = lax.axis_index("tp")
    width = mine_ref.shape[1] // 2
    parts = [
        (mine_ref[:, :width], me),
        (mine_ref[:, width:], me ^ 2),
        (other_ref[:, :width], me ^ 1),
        (other_ref[:, width:], me ^ 3),
    ]

    def project(w_ref):
        return sum(
            jnp.dot(part, block_rows(w_ref, at, width), preferred_element_type=F32)
            for part, at in parts
        ).astype(BF16)

    heads = [slice(at, at + HEAD_WIDTH) for at in range(0, q_ref.shape[1], HEAD_WIDTH)]
    keys = project(w_key_ref)
    weights = []
    for cols in heads:
        logits = lax.dot_general(
            q_ref[:, cols], keys[:, cols], (((1,), (1,)), ((), ())), preferred_element_type=F32
        ) * HEAD_WIDTH ** (-0.5)
        expo = jnp.exp(logits)
        weights.append((expo * (1.0 / jnp.sum(expo, axis=1, keepdims=True))).astype(BF16))
    values = project(w_value_ref)
    return [
        jnp.dot(weight, values[:, cols], preferred_element_type=F32)
        for weight, cols in zip(weights, heads)
    ]


def attend_body(mine_ref, other_ref, w_key_ref, w_value_ref, q_ref, out_ref):
    for at, part in enumerate(attended(mine_ref, other_ref, w_key_ref, w_value_ref, q_ref)):
        out_ref[:, at * HEAD_WIDTH : (at + 1) * HEAD_WIDTH] = part.astype(BF16)


def attend_first_body(
    mine_ref, other_ref, w_key_ref, w_value_ref, queries_ref, next_ref, out_ref, q_ref
):
    edge = 16
    for at in range(0, q_ref.shape[1], HEAD_WIDTH):
        cols = slice(at, at + HEAD_WIDTH)
        tall = jnp.concatenate(
            [queries_ref[-edge:, cols].astype(F32), next_ref[:, cols].astype(F32)], axis=0
        )
        moved = pltpu.roll(tall, tall.shape[0] - edge + 1, 0)
        q_ref[:, cols] = moved[: q_ref.shape[0]].astype(BF16)
    attend_body(mine_ref, other_ref, w_key_ref, w_value_ref, q_ref, out_ref)


def attend_last_body(
    mine_ref, other_ref, w_key_ref, w_value_ref, q_ref, behind_ref, *refs
):
    before, last_ref, out_ref = refs[:-2], refs[-2], refs[-1]
    parts = attended(mine_ref, other_ref, w_key_ref, w_value_ref, q_ref)
    for at, part in enumerate(parts):
        cols = slice(at * HEAD_WIDTH, (at + 1) * HEAD_WIDTH)
        part = part.astype(BF16).astype(F32)
        stack = [behind_ref[:, cols].astype(F32)]
        stack += [ref[:, cols].astype(F32) for ref in before]
        stack += [part, last_ref[:, cols].astype(F32)]
        tall = jnp.concatenate(stack, axis=0)
        moved = pltpu.roll(tall, tall.shape[0] - 1, 0)
        out_ref[:, cols] = moved[: out_ref.shape[0]].astype(BF16)


def per_device(queries, vocab_rows, neighbour_ids, w_in, w_out, w_key, w_value):
    seq_size = lax.axis_size("seq")
    groups, nbrs, nlen = neighbour_ids.shape
    per_group = nbrs * nlen
    rows = groups * per_group
    voc, width = vocab_rows.shape
    tok, head_cols = queries.shape
    cap = max(2, 2 * rows // seq_size)
    slots = seq_size * cap
    sds = jax.ShapeDtypeStruct

    wanted, slot = call(
        functools.partial(route_body, voc, cap),
        (sds((seq_size, cap), jnp.int32), sds((rows, LANES), jnp.int32)),
        "route",
        (neighbour_ids.reshape(1, rows),),
        flops=8 * 10**9,
    )
    request = lax.all_to_all(wanted, "seq", split_axis=0, concat_axis=0, tiled=True)
    found = call(
        fetch_body,
        sds((slots, width), BF16),
        "fetch",
        (request.reshape(1, slots), vocab_rows),
    )
    answered = lax.all_to_all(
        found.reshape(seq_size, cap, width), "seq", split_axis=0, concat_axis=0, tiled=True
    ).reshape(slots, width)
    order = [groups - 1] + list(range(groups - 1))
    plan = [order[:2], order[2:]]
    first, window = {}, {}
    token = slot
    pieces = []
    for part in plan:
        e0 = token = call(
            functools.partial(order_body, part),
            sds((len(part) * per_group, width), BF16),
            "order",
            (slot, answered),
            (token,),
        )
        pieces.append([e0, exchange(e0, 2), None])
        for at, g in enumerate(part):
            first[g] = at * per_group

    def across(piece, after=()):
        count = piece[0].shape[0]
        both = call(pair_body, sds((count, 2 * width), BF16), "pair", piece[:2], after)
        piece[2] = exchange(both, 1)
        return both

    across(pieces[0], (token,))
    half = sds((per_group, 2 * width), BF16)
    whole = sds((per_group, 2 * width), F32)
    fed, summed, far, encoded = {}, {}, {}, {}
    behind = out = next_q = None

    other = {g: (pieces[0][2],) for g in plan[0]}

    def emb(g):
        return *pieces[0 if g in plan[0] else 1][:2], *other[g]

    def rest(_):
        nonlocal token
        single, double = sds((per_group, width), BF16), sds((per_group, 2 * width), BF16)
        token, far_own, both = call(
            deal_body,
            (single, single, double),
            "deal",
            pieces[1][:2],
            (token, fed[order[1]][1]),
        )
        other[order[2]] = exchange(token, 1), exchange(far_own, 1)
        other[order[3]] = (exchange(both, 1),)

    def pause(_):
        nonlocal token
        token = call(mark_body, sds((8, LANES), F32), "mark", (), (token, pieces[1][1]))

    def ask(_):
        nonlocal next_q
        head = call(head_body, sds((GROUP, head_cols), BF16), "head", (queries,), (token,))
        next_q = shifted(head, -1)

    def feed(g):
        nonlocal token
        keep, token = call(
            functools.partial(feed_body, first[g]),
            (whole, half),
            "feed",
            (*emb(g), w_in, w_out),
            (token,),
        )
        fed[g] = keep, exchange(token, 1)

    def add(g):
        nonlocal token
        summed[g], token = call(add_body, (whole, half), "add", fed[g], (token,))
        far[g] = exchange(token, 2)

    def finish(g):
        nonlocal token
        token = call(
            functools.partial(finish_body, first[g]),
            half,
            "finish",
            (*pieces[0 if g in plan[0] else 1][:2], summed[g], far[g]),
            (token, *{order[0]: (next_q,), order[-1]: (behind,)}.get(g, ())),
        )
        encoded[g] = token, exchange(token, 1)

    def attend(g):
        nonlocal token, behind, out
        start = (g + 1) * GROUP - 1
        args = (*encoded[g], w_key, w_value)
        if g == order[0]:
            window[g] = token = call(
                attend_first_body,
                sds((GROUP, head_cols), BF16),
                "attend_first",
                (*args, queries, next_q),
                (token,),
                scratch_shapes=[pltpu.VMEM((GROUP, head_cols), BF16)],
            )
            behind = shifted(token, 1)
            return
        args += (queries[start : start + GROUP],)
        if g == order[-1]:
            before = [window[at] for at in order[1:-1]]
            out = call(
                attend_last_body,
                sds((tok, head_cols), BF16),
                "attend_last",
                (*args, behind, *before, window[order[0]]),
            )
            return
        window[g] = token = call(
            attend_body,
            sds((GROUP, head_cols), BF16),
            "attend",
            args,
            (token,),
        )

    a, b, c, d = order
    for step, g in (
        (feed, a), (feed, b), (add, a), (pause, c), (ask, a), (rest, c), (feed, c), (add, b),
        (finish, a), (feed, d), (add, c),
        (finish, b), (attend, a), (add, d),
        (finish, c), (attend, b),
        (finish, d), (attend, c), (attend, d),
    ):
        step(g)
    return out


def solution(mesh):
    return jax.shard_map(
        per_device,
        mesh=mesh,
        in_specs=(
            P("seq", "tp"),
            P("seq", "tp"),
            P("seq", None, None),
            P(None, "tp"),
            P("tp", None),
            P(None, "tp"),
            P(None, "tp"),
        ),
        out_specs=P("seq", "tp"),
        check_vma=False,
    )
```

```python
import functools

import jax
import jax.numpy as jnp
from jax import lax
from jax.experimental import pallas as pl
from jax.experimental.pallas import tpu as pltpu
from jax.sharding import PartitionSpec as P

HEAD_WIDTH = 128
GROUP = 64
LANES = 128
VMEM_LIMIT = 24 * 1024 * 1024
F32 = jnp.float32
BF16 = jnp.bfloat16


def call(body, outs, name, used, after=(), flops=1024, **extra):
    vmem = pl.BlockSpec(memory_space=pltpu.VMEM)
    unread = pl.BlockSpec(memory_space=pl.ANY)
    in_specs = extra.pop("in_specs", [vmem] * len(used))

    def without_after(*refs):
        body(*refs[: len(used)], *refs[len(used) + len(after) :])

    return pl.pallas_call(
        without_after,
        out_shape=outs,
        in_specs=in_specs + [unread] * len(after),
        compiler_params=pltpu.CompilerParams(vmem_limit_bytes=VMEM_LIMIT),
        cost_estimate=pl.CostEstimate(flops=flops, bytes_accessed=1024, transcendentals=0),
        name=name,
        **extra,
    )(*used, *after)


def exchange(x, bit):
    size = lax.axis_size("tp")
    return lax.ppermute(x, "tp", [(i, i ^ bit) for i in range(size)])


def shifted(x, by):
    length = lax.axis_size("seq")
    pairs = [(i, i + by) for i in range(length) if 0 <= i + by < length]
    return lax.ppermute(x, "seq", pairs)


def columns_of(row):
    return jnp.broadcast_to(row, (LANES, row.shape[1])).T


def one_hot(column, width):
    lane = lax.broadcasted_iota(jnp.int32, column.shape, 1)
    return jnp.concatenate(
        [jnp.where(column == lane + at, 1.0, 0.0).astype(BF16) for at in range(0, width, LANES)],
        axis=1,
    )


def route_body(voc, cap, ids_ref, wanted_ref, slot_ref):
    ids = ids_ref[...]
    count = ids.shape[1]
    owners = wanted_ref.shape[0]
    owner = lax.div(ids, jnp.int32(voc))
    local = ids - owner * voc
    hit = owner == lax.broadcasted_iota(jnp.int32, (owners, count), 0)
    hot = jnp.where(hit, 1.0, 0.0)
    upper = jnp.where(
        lax.broadcasted_iota(jnp.int32, (LANES, LANES), 0)
        <= lax.broadcasted_iota(jnp.int32, (LANES, LANES), 1),
        1.0,
        0.0,
    ).astype(BF16)
    carry = jnp.zeros((owners, 1), F32)
    ranks = []
    for at in range(0, count, LANES):
        part = hot[:, at : at + LANES]
        running = jnp.dot(part.astype(BF16), upper, preferred_element_type=F32) + carry
        ranks.append(jnp.sum(part * running, axis=0, keepdims=True))
        carry = running[:, LANES - 1 :]
    rank = jnp.concatenate(ranks, axis=1).astype(jnp.int32) - 1
    high = jnp.where(hit, lax.div(local, jnp.int32(256)), 0)
    low = jnp.where(hit, lax.rem(local, jnp.int32(256)), 0)
    digits = jnp.concatenate([high, low], axis=0).astype(F32).astype(BF16)
    place = jnp.where(
        rank == lax.broadcasted_iota(jnp.int32, (cap, count), 0), 1.0, 0.0
    ).astype(BF16)
    found = lax.dot_general(
        digits, place, (((1,), (1,)), ((), ())), preferred_element_type=F32
    ).astype(jnp.int32)
    wanted_ref[...] = found[:owners] * 256 + found[owners:]
    slot_ref[...] = columns_of(owner * cap + rank)


def fetch_body(req_ref, vocab_ref, out_ref):
    step = 256
    table = vocab_ref[...]
    for at in range(0, req_ref.shape[1], step):
        picked = one_hot(columns_of(req_ref[:, at : at + step]), table.shape[0])
        out_ref[at : at + step, :] = jnp.dot(
            picked, table, preferred_element_type=F32
        ).astype(BF16)


def mark_body(out_ref):
    out_ref[...] = jnp.zeros_like(out_ref)


def pair_body(left_ref, right_ref, out_ref):
    width = left_ref.shape[1]
    out_ref[:, :width] = left_ref[...]
    out_ref[:, width:] = right_ref[...]


def head_body(queries_ref, out_ref):
    out_ref[...] = queries_ref[: out_ref.shape[0], :]


def order_body(groups, slot_ref, rows_ref, out_ref):
    rows = rows_ref[...]
    count = out_ref.shape[0] // len(groups)
    for at, g in enumerate(groups):
        picked = one_hot(slot_ref[g * count : (g + 1) * count, :], rows.shape[0])
        out_ref[at * count : (at + 1) * count, :] = jnp.dot(
            picked, rows, preferred_element_type=F32
        ).astype(BF16)


def block_rows(ref, index, width):
    return ref[pl.ds(pl.multiple_of(index * width, width), width), :]


def block_cols(ref, index, width):
    return ref[:, pl.ds(pl.multiple_of(index * width, width), width)]


def feed_body(first, e0_ref, e2_ref, other_ref, w_in_ref, w_out_ref, keep_ref, send_ref):
    me = lax.axis_index("tp")
    width = e0_ref.shape[1]
    index = [me, me ^ 2, me ^ 1, me ^ 3]
    here = slice(first, first + keep_ref.shape[0])
    parts = [e0_ref[here, :], e2_ref[here, :], other_ref[here, :width], other_ref[here, width:]]
    parts = [part.astype(F32) for part in parts]
    square = sum(jnp.sum(part * part, axis=1, keepdims=True) for part in parts)
    scale = lax.rsqrt(square / (4 * width) + 1e-06)
    hidden = sum(
        jnp.dot(
            (part * scale).astype(BF16), block_rows(w_in_ref, at, width), preferred_element_type=F32
        )
        for part, at in zip(parts, index)
    )
    inner = jax.nn.gelu(hidden, approximate=True).astype(BF16)
    for slot in range(2):
        cols = slice(slot * width, (slot + 1) * width)
        keep_ref[:, cols] = jnp.dot(
            inner, block_cols(w_out_ref, index[slot], width), preferred_element_type=F32
        )
        send_ref[:, cols] = jnp.dot(
            inner, block_cols(w_out_ref, index[2 + slot], width), preferred_element_type=F32
        ).astype(BF16)


def add_body(keep_ref, recv_ref, chip_ref, send_ref):
    chip = keep_ref[...] + recv_ref[...].astype(F32)
    chip_ref[...] = chip
    send_ref[...] = chip.astype(BF16)


def finish_body(first, e0_ref, e2_ref, chip_ref, far_ref, mine_ref):
    width = e0_ref.shape[1]
    near, past = slice(0, width), slice(width, 2 * width)
    here = slice(first, first + mine_ref.shape[0])
    mine_ref[:, near] = (
        e0_ref[here, :].astype(F32) + (chip_ref[:, near] + far_ref[:, past].astype(F32))
    ).astype(BF16)
    mine_ref[:, past] = (
        e2_ref[here, :].astype(F32) + (chip_ref[:, past] + far_ref[:, near].astype(F32))
    ).astype(BF16)


def attended(mine_ref, other_ref, w_key_ref, w_value_ref, q_ref):
    me = lax.axis_index("tp")
    width = mine_ref.shape[1] // 2
    parts = [
        (mine_ref[:, :width], me),
        (mine_ref[:, width:], me ^ 2),
        (other_ref[:, :width], me ^ 1),
        (other_ref[:, width:], me ^ 3),
    ]

    def project(w_ref):
        return sum(
            jnp.dot(part, block_rows(w_ref, at, width), preferred_element_type=F32)
            for part, at in parts
        ).astype(BF16)

    heads = [slice(at, at + HEAD_WIDTH) for at in range(0, q_ref.shape[1], HEAD_WIDTH)]
    keys = project(w_key_ref)
    weights = []
    for cols in heads:
        logits = lax.dot_general(
            q_ref[:, cols], keys[:, cols], (((1,), (1,)), ((), ())), preferred_element_type=F32
        ) * HEAD_WIDTH ** (-0.5)
        expo = jnp.exp(logits)
        weights.append((expo * (1.0 / jnp.sum(expo, axis=1, keepdims=True))).astype(BF16))
    values = project(w_value_ref)
    return [
        jnp.dot(weight, values[:, cols], preferred_element_type=F32)
        for weight, cols in zip(weights, heads)
    ]


def attend_body(mine_ref, other_ref, w_key_ref, w_value_ref, q_ref, out_ref):
    for at, part in enumerate(attended(mine_ref, other_ref, w_key_ref, w_value_ref, q_ref)):
        out_ref[:, at * HEAD_WIDTH : (at + 1) * HEAD_WIDTH] = part.astype(BF16)


def attend_first_body(
    mine_ref, other_ref, w_key_ref, w_value_ref, queries_ref, next_ref, out_ref, q_ref
):
    edge = 16
    for at in range(0, q_ref.shape[1], HEAD_WIDTH):
        cols = slice(at, at + HEAD_WIDTH)
        tall = jnp.concatenate(
            [queries_ref[-edge:, cols].astype(F32), next_ref[:, cols].astype(F32)], axis=0
        )
        moved = pltpu.roll(tall, tall.shape[0] - edge + 1, 0)
        q_ref[:, cols] = moved[: q_ref.shape[0]].astype(BF16)
    attend_body(mine_ref, other_ref, w_key_ref, w_value_ref, q_ref, out_ref)


def attend_last_body(
    mine_ref, other_ref, w_key_ref, w_value_ref, q_ref, behind_ref, *refs
):
    before, (last_ref, out_hbm, out_ref, sems) = refs[:-4], refs[-4:]
    copies = []
    parts = attended(mine_ref, other_ref, w_key_ref, w_value_ref, q_ref)
    for at, part in enumerate(parts):
        cols = slice(at * HEAD_WIDTH, (at + 1) * HEAD_WIDTH)
        part = part.astype(BF16).astype(F32)
        stack = [behind_ref[:, cols].astype(F32)]
        stack += [ref[:, cols].astype(F32) for ref in before]
        stack += [part, last_ref[:, cols].astype(F32)]
        tall = jnp.concatenate(stack, axis=0)
        moved = pltpu.roll(tall, tall.shape[0] - 1, 0)
        out_ref[:, cols] = moved[: out_ref.shape[0]].astype(BF16)
        copy = pltpu.make_async_copy(out_ref.at[:, cols], out_hbm.at[:, cols], sems.at[at])
        copy.start()
        copies.append(copy)
    for copy in copies:
        copy.wait()


def per_device(queries, vocab_rows, neighbour_ids, w_in, w_out, w_key, w_value):
    seq_size = lax.axis_size("seq")
    groups, nbrs, nlen = neighbour_ids.shape
    per_group = nbrs * nlen
    rows = groups * per_group
    voc, width = vocab_rows.shape
    tok, head_cols = queries.shape
    cap = max(2, 2 * rows // seq_size)
    slots = seq_size * cap
    sds = jax.ShapeDtypeStruct

    wanted, slot = call(
        functools.partial(route_body, voc, cap),
        (sds((seq_size, cap), jnp.int32), sds((rows, LANES), jnp.int32)),
        "route",
        (neighbour_ids.reshape(1, rows),),
        flops=8 * 10**9,
    )
    request = lax.all_to_all(wanted, "seq", split_axis=0, concat_axis=0, tiled=True)
    found = call(
        fetch_body,
        sds((slots, width), BF16),
        "fetch",
        (request.reshape(1, slots), vocab_rows),
    )
    answered = lax.all_to_all(
        found.reshape(seq_size, cap, width), "seq", split_axis=0, concat_axis=0, tiled=True
    ).reshape(slots, width)
    order = [groups - 1] + list(range(groups - 1))
    plan = [order[:2], order[2:]]
    first, window = {}, {}
    token = slot
    pieces = []
    for part in plan:
        e0 = token = call(
            functools.partial(order_body, part),
            sds((len(part) * per_group, width), BF16),
            "order",
            (slot, answered),
            (token,),
        )
        pieces.append([e0, exchange(e0, 2), None])
        for at, g in enumerate(part):
            first[g] = at * per_group

    def across(piece, after=()):
        count = piece[0].shape[0]
        both = call(pair_body, sds((count, 2 * width), BF16), "pair", piece[:2], after)
        piece[2] = exchange(both, 1)
        return both

    across(pieces[0], (token,))
    half = sds((per_group, 2 * width), BF16)
    whole = sds((per_group, 2 * width), F32)
    fed, summed, far, encoded = {}, {}, {}, {}
    behind = out = next_q = None

    def emb(g):
        return pieces[0 if g in plan[0] else 1]

    def rest(_):
        nonlocal token
        token = across(pieces[1], (token, fed[order[1]][1]))

    def pause(_):
        nonlocal token
        token = call(mark_body, sds((8, LANES), F32), "mark", (), (token, pieces[1][1]))

    def ask(_):
        nonlocal next_q
        head = call(head_body, sds((GROUP, head_cols), BF16), "head", (queries,), (token,))
        next_q = shifted(head, -1)

    def feed(g):
        nonlocal token
        keep, token = call(
            functools.partial(feed_body, first[g]),
            (whole, half),
            "feed",
            (*emb(g), w_in, w_out),
            (token,),
        )
        fed[g] = keep, exchange(token, 1)

    def add(g):
        nonlocal token
        summed[g], token = call(add_body, (whole, half), "add", fed[g], (token,))
        far[g] = exchange(token, 2)

    def finish(g):
        nonlocal token
        token = call(
            functools.partial(finish_body, first[g]),
            half,
            "finish",
            (*emb(g)[:2], summed[g], far[g]),
            (token, *{order[0]: (next_q,), order[-1]: (behind,)}.get(g, ())),
        )
        encoded[g] = token, exchange(token, 1)

    def attend(g):
        nonlocal token, behind, out
        start = (g + 1) * GROUP - 1
        args = (*encoded[g], w_key, w_value)
        if g == order[0]:
            window[g] = token = call(
                attend_first_body,
                sds((GROUP, head_cols), BF16),
                "attend_first",
                (*args, queries, next_q),
                (token,),
                scratch_shapes=[pltpu.VMEM((GROUP, head_cols), BF16)],
            )
            behind = shifted(token, 1)
            return
        args += (queries[start : start + GROUP],)
        if g == order[-1]:
            before = [window[at] for at in order[1:-1]]
            out = call(
                attend_last_body,
                sds((tok, head_cols), BF16),
                "attend_last",
                (*args, behind, *before, window[order[0]]),
                out_specs=pl.BlockSpec(memory_space=pl.ANY),
                scratch_shapes=[
                    pltpu.VMEM((tok, head_cols), BF16),
                    pltpu.SemaphoreType.DMA((head_cols // HEAD_WIDTH,)),
                ],
            )
            return
        window[g] = token = call(
            attend_body,
            sds((GROUP, head_cols), BF16),
            "attend",
            args,
            (token,),
        )

    a, b, c, d = order
    for step, g in (
        (feed, a), (feed, b), (pause, c), (add, a), (ask, a), (rest, c), (feed, c), (add, b),
        (finish, a), (feed, d), (add, c),
        (finish, b), (attend, a), (add, d),
        (finish, c), (attend, b),
        (finish, d), (attend, c), (attend, d),
    ):
        step(g)
    return out


def solution(mesh):
    return jax.shard_map(
        per_device,
        mesh=mesh,
        in_specs=(
            P("seq", "tp"),
            P("seq", "tp"),
            P("seq", None, None),
            P(None, "tp"),
            P("tp", None),
            P(None, "tp"),
            P(None, "tp"),
        ),
        out_specs=P("seq", "tp"),
        check_vma=False,
    )
```
